128 devices in a mesh: dp: 32 (over x, y, core), tensor: 4 (over z).
Axes of the slice: x: 4, y: 4, z: 4, core: 2. Of those that a mesh axis runs over, the one named last changes fastest.
Arguments:
- inputs: bfloat16 [16384, 2048], P(('dp', 'tensor')), may hold values from -6 to 6
- cotangent: bfloat16 [16384, 2048], P(('dp', 'tensor')), may hold values from -6 to 6
- positions: int32 [16384], P('dp'), may hold values from 0 to 511, as said below
- qkv_weight: float32 [2048, 3, 2048], P('dp', None, 'tensor'), may hold values from -0.1875 to 0.1875
- out_weight: float32 [2048, 2048], P('tensor', 'dp'), may hold values from -0.75 to 0.75
- up_weight: float32 [2048, 8192], P('dp', 'tensor'), may hold values from -0.125 to 0.125
- down_weight: float32 [8192, 2048], P('tensor', 'dp'), may hold values from -0.0625 to 0.0625
- qkv_moment: float32 [2048, 3, 2048], P('dp', None, 'tensor'), may hold values from -160 to 160
- out_moment: float32 [2048, 2048], P('tensor', 'dp'), may hold values from -160 to 160
- up_moment: float32 [2048, 8192], P('dp', 'tensor'), may hold values from -192 to 192
- down_moment: float32 [8192, 2048], P('tensor', 'dp'), may hold values from -448 to 448
- vectors: float32 [11, 2048], P(None, ('dp', 'tensor')), may hold values from -0.6 to 1.6, as said below
- vector_first: float32 [11, 2048], P(None, ('dp', 'tensor')), may hold values from -57.6 to 57.6
- vector_second: float32 [11, 2048], P(None, ('dp', 'tensor')), may hold values from 8.192 to 3604.48
Outputs:
- layer_out: bfloat16 [16384, 2048], P(('dp', 'tensor'))
- input_grad: float32 [16384, 2048], P(('dp', 'tensor'))
- qkv_new: float32 [2048, 3, 2048], P('dp', None, 'tensor')
- out_new: float32 [2048, 2048], P('tensor', 'dp')
- up_new: float32 [2048, 8192], P('dp', 'tensor')
- down_new: float32 [8192, 2048], P('tensor', 'dp')
- qkv_moment_new: float32 [2048, 3, 2048], P('dp', None, 'tensor')
- out_moment_new: float32 [2048, 2048], P('tensor', 'dp')
- up_moment_new: float32 [2048, 8192], P('dp', 'tensor')
- down_moment_new: float32 [8192, 2048], P('tensor', 'dp')
- vector_first_new: float32 [11, 2048], P(None, ('dp', 'tensor'))
- vector_second_new: float32 [11, 2048], P(None, ('dp', 'tensor'))
- vectors_new: float32 [11, 2048], P(None, ('dp', 'tensor'))
The draws below stay inside these ranges and needn't reach their ends.
Inputs may be any that keep to these rules, and one draw needn't show every extreme that they name: `positions`: within each aligned block of 512 tokens, the first has position 0 and every other has the position of the token before it plus one, or 0 where a new sequence starts; in some block all 512 tokens form one sequence. `vectors`: row 0 lies near 1, the other rows near 0.
All inputs are finite; a program needn't handle non-finite values.
Results may differ from the reference program's by a relative error of at most 0.015.
The reference program's roundings to bfloat16 on the way count: a program that leaves them out, or rounds other values in their place, can miss the bound.
Values may be sent and summed in bfloat16 or wider, within the bound.
A program may use at most 192 MiB of HBM per device.

```python
import jax
import jax.numpy as jnp
from jax import lax

D = 2048
HEADS = 32
HEAD = 64
ROT = 32
FF = 8192
BR = 256
SWEEPS = 5
STEP = 10
ROWS = 512
TOKENS = 16384
NVEC = 11


def row_scales(count):
    row_ids = jnp.arange(count)
    scale_table = jnp.array([0.6, 0.6, 0.1, 0.1, 0.3, 1.0, 1.0], jnp.float32)
    return jnp.where(row_ids < 7, scale_table[jnp.minimum(row_ids, 6)], 0.25)


def draw_positions(key, part):
    key = jax.random.fold_in(key, 4)
    slot_total = TOKENS // ROWS
    cut_key, count_key, pick_key = jax.random.split(key, 3)
    cuts = jax.random.randint(cut_key, (slot_total, 3), 1, ROWS)
    active_count = jax.random.randint(count_key, (slot_total, 1), 0, 4)
    chosen = jax.random.randint(pick_key, (), 0, slot_total)
    active_count = jnp.where(jnp.arange(slot_total)[:, None] == chosen, 0, active_count)
    active = jnp.arange(3)[None, :] < active_count
    row_ids = jnp.arange(ROWS)
    starts = jnp.where(active[:, None, :] & (cuts[:, None, :] <= row_ids[None, :, None]), cuts[:, None, :], 0)
    begins = jnp.max(starts, -1)
    return (row_ids[None, :] - begins).reshape(TOKENS).astype(jnp.int32)


def draw_vectors(key, part):
    key = jax.random.fold_in(key, 1)
    noise = jnp.clip(jax.random.normal(key, (NVEC, D), jnp.float32), -3.0, 3.0)
    row_ids = jnp.arange(NVEC)[:, None]
    return jnp.where(row_ids == 0, 1.0 + 0.2 * noise, 0.2 * noise).astype(jnp.float32)


def draw_vector_first(key, part):
    key = jax.random.fold_in(key, 2)
    noise = jnp.clip(jax.random.normal(key, (NVEC, D), jnp.float32), -4.0, 4.0)
    scales = row_scales(NVEC)[:, None] * TOKENS ** 0.5
    return (noise * scales * (0.1 / 0.9)).astype(jnp.float32)


def draw_vector_second(key, part):
    key = jax.random.fold_in(key, 3)
    factor = jnp.exp(jax.random.uniform(key, (NVEC, D), jnp.float32, 0.0, 1.3862944))
    scales = row_scales(NVEC)[:, None]
    return (factor * scales * scales * TOKENS * (0.05 / 0.95)).astype(jnp.float32)


def block_levels(own_key, dims, cuts, smallest, largest):
    factor_of = 1.0
    for dim, parts in cuts:
        heights = jax.random.uniform(jax.random.fold_in(jax.random.fold_in(own_key, 6), dim), (parts,), jnp.float32, smallest / len(cuts), largest / len(cuts))
        factor_of = factor_of * jnp.repeat(jnp.exp(heights), dims[dim] // parts).reshape((-1,) + (1,) * (len(dims) - 1 - dim))
    return factor_of


def gaussian(own_key, dims, scale, most, pieces=(), dtype=jnp.bfloat16):
    values = scale * jax.random.normal(own_key, dims, jnp.float32)
    if pieces:
        values = values * block_levels(own_key, dims, pieces, -0.22, 0.18)
    return jnp.clip(values, -most, most).astype(dtype)


def setup_inputs(seed: int = 0) -> dict:
    keys = jax.random.split(jax.random.key(seed), 15)
    inputs = gaussian(keys[0], (TOKENS, D), 1.0, 6.0, ((0, 128),))
    cotangent = gaussian(keys[1], (TOKENS, D), 1.0, 6.0, ((0, 128),))
    positions = draw_positions(jax.random.fold_in(keys[14], 71), 0)
    qkv_weight = gaussian(keys[3], (D, 3, HEADS * HEAD), (D // 2) ** -0.5, 0.1875, ((0, 32), (2, 4)), jnp.float32)
    out_weight = gaussian(keys[4], (HEADS * HEAD, D), (D // 32) ** -0.5, 0.75, ((0, 4), (1, 32)), jnp.float32)
    up_weight = gaussian(keys[5], (D, FF), D ** -0.5, 0.125, ((0, 32), (1, 4)), jnp.float32)
    down_weight = gaussian(keys[6], (FF, D), FF ** -0.5, 0.0625, ((0, 4), (1, 32)), jnp.float32)
    qkv_moment = gaussian(keys[7], (D, 3, HEADS * HEAD), (0.2 * TOKENS ** 0.5), 160.0, ((0, 32), (2, 4)), jnp.float32)
    out_moment = gaussian(keys[8], (HEADS * HEAD, D), (0.2 * TOKENS ** 0.5), 160.0, ((0, 4), (1, 32)), jnp.float32)
    up_moment = gaussian(keys[9], (D, FF), (0.25 * TOKENS ** 0.5), 192.0, ((0, 32), (1, 4)), jnp.float32)
    down_moment = gaussian(keys[10], (FF, D), (0.6 * TOKENS ** 0.5), 448.0, ((0, 4), (1, 32)), jnp.float32)
    vectors = draw_vectors(jax.random.fold_in(keys[14], 71), 0)
    vector_first = draw_vector_first(jax.random.fold_in(keys[14], 71), 0)
    vector_second = draw_vector_second(jax.random.fold_in(keys[14], 71), 0)
    return dict(inputs=inputs, cotangent=cotangent, positions=positions, qkv_weight=qkv_weight, out_weight=out_weight, up_weight=up_weight, down_weight=down_weight, qkv_moment=qkv_moment, out_moment=out_moment, up_moment=up_moment, down_moment=down_moment, vectors=vectors, vector_first=vector_first, vector_second=vector_second)


@jax.custom_vjp
def low(v):
    return lax.optimization_barrier(v.astype(jnp.bfloat16)).astype(jnp.float32)

@jax.custom_vjp
def low_back(v):
    return v

def low_keep(v):
    return (low(v), None)

def low_pass(kept, grad):
    return (grad,)

def back_keep(v):
    return (v, None)

def back_low(kept, grad):
    return (low(grad),)
low.defvjp(low_keep, low_pass)
low_back.defvjp(back_keep, back_low)
highest = lax.Precision.HIGHEST
norm_epsilon = 1e-05
ortho_epsilon = 1e-07
masked_score = -1e+30
rotary_base = 10000.0
muon_decay = 0.95
coef_linear = 3.4445
coef_square = -4.775
coef_cubic = 2.0315
decay_factor = 0.01
rate_qkv = 1.0
rate_out = 4.0
rate_up = 0.8
rate_down = 0.4
adam_rate = 0.2
first_decay = 0.9
second_decay = 0.95
adam_epsilon = 1e-08

def rotary_tables(positions, half_rot):
    freq_index = jnp.arange(half_rot).astype(jnp.float32)
    inverse_freq = rotary_base ** (-2.0 * freq_index / (2 * half_rot))
    angles = positions.astype(jnp.float32)[:, None] * inverse_freq[None, :]
    return (jnp.cos(angles)[:, None, :], jnp.sin(angles)[:, None, :])

def rotate(vectors_in, cosine_table, sine_table, half_rot):
    first_half = vectors_in[..., :half_rot]
    second = vectors_in[..., half_rot:2 * half_rot]
    remainder = vectors_in[..., 2 * half_rot:]
    return jnp.concatenate([first_half * cosine_table - second * sine_table, second * cosine_table + first_half * sine_table, remainder], -1)

def gelu_tanh(values):
    return jax.nn.gelu(values, approximate=True)

def slot_forward(residual, params, slot_positions):
    qkv_weight, out_weight, up_weight, down_weight, vector_table = params
    row_count = residual.shape[0]
    center = residual - lax.optimization_barrier(jnp.mean(residual, -1, keepdims=True))
    variance = lax.optimization_barrier(jnp.mean(center * center, -1, keepdims=True))
    normed = center * lax.rsqrt(variance + norm_epsilon)
    hidden_low = low(normed * vector_table[0] + vector_table[1])
    qkv_lin = jnp.einsum('rd,dcn->rcn', hidden_low, low(qkv_weight), precision=highest) + vector_table[2:5][None]
    qkv_lin = low_back(qkv_lin)
    cosine_table, sine_table = rotary_tables(slot_positions, ROT // 2)
    query_low = low(rotate(qkv_lin[:, 0].reshape(row_count, HEADS, HEAD), cosine_table, sine_table, ROT // 2))
    key_low = low(rotate(qkv_lin[:, 1].reshape(row_count, HEADS, HEAD), cosine_table, sine_table, ROT // 2))
    value_low = low(qkv_lin[:, 2].reshape(row_count, HEADS, HEAD))
    scale_value = HEAD ** (-0.5)
    scores = low_back(jnp.einsum('qhe,khe->hqk', query_low, key_low, precision=highest) * scale_value)
    row_ids = jnp.arange(row_count)
    visible = (row_ids[None, :] <= row_ids[:, None]) & (row_ids[:, None] - row_ids[None, :] <= slot_positions[:, None])
    scores = jnp.where(visible[None], scores, masked_score)
    row_max = lax.optimization_barrier(jnp.max(scores, -1, keepdims=True))
    exp_scores = jnp.exp(scores - row_max)
    soft_low = low(exp_scores / lax.optimization_barrier(jnp.sum(exp_scores, -1, keepdims=True)))
    attended = low(low_back(jnp.einsum('hqk,khe->qhe', soft_low, value_low, precision=highest)))
    attn_branch = jnp.dot(attended.reshape(row_count, HEADS * HEAD), low(out_weight), precision=highest) + vector_table[5]
    up_lin = low_back(jnp.dot(hidden_low, low(up_weight), precision=highest) + vector_table[7:].reshape(-1))
    activated = low(gelu_tanh(up_lin))
    mlp_branch = jnp.dot(activated, low(down_weight), precision=highest) + vector_table[6]
    return residual + attn_branch + mlp_branch

def column_blocks(matrix):
    return matrix.reshape(matrix.shape[0], -1, BR).transpose(1, 2, 0)

def column_restore(blocks, shape):
    return blocks.transpose(2, 0, 1).reshape(shape)

def orthogonalize(blocks):
    norms = jnp.sqrt(lax.optimization_barrier(jnp.sum(blocks * blocks, axis=(1, 2), keepdims=True)))
    current = blocks / (norms + ortho_epsilon)
    for sweep_index in range(SWEEPS):
        gram_matrix = jnp.einsum('bik,bjk->bij', current, current, precision=highest)
        polynomial = coef_square * gram_matrix + coef_cubic * jnp.einsum('bij,bjk->bik', gram_matrix, gram_matrix, precision=highest)
        current = coef_linear * current + jnp.einsum('bij,bjk->bik', polynomial, current, precision=highest)
    return current

def muon_update(weight, moment, grad, rate, by_columns):
    moment_new = muon_decay * moment + grad
    nesterov = grad + muon_decay * moment_new
    flattened = nesterov.reshape(nesterov.shape[0], -1)
    if by_columns:
        update = column_restore(orthogonalize(column_blocks(flattened)), flattened.shape)
    else:
        update = orthogonalize(flattened.reshape(-1, BR, flattened.shape[1])).reshape(flattened.shape)
    weight_new = weight * (1.0 - decay_factor * rate) - rate * update.reshape(weight.shape)
    return (weight_new, moment_new)

def reference(inputs, cotangent, positions, qkv_weight, out_weight, up_weight, down_weight, qkv_moment, out_moment, up_moment, down_moment, vectors, vector_first, vector_second):
    slot_total = TOKENS // ROWS
    residual_all = inputs.astype(jnp.float32).reshape(slot_total, ROWS, D)
    cot_all = cotangent.astype(jnp.float32).reshape(slot_total, ROWS, D)
    position_all = positions.reshape(slot_total, ROWS)
    params = (qkv_weight, out_weight, up_weight, down_weight, vectors)

    def one_slot(totals, slot_data):
        residual, cot_slot, slot_positions = slot_data
        result, pullback = jax.vjp(lambda r, p: slot_forward(r, p, slot_positions), residual, params)
        grad_residual, grad_params = pullback(cot_slot)
        totals = jax.tree.map(lambda a, b: a + b, totals, grad_params)
        return (totals, (result, grad_residual))
    zero_grads = jax.tree.map(jnp.zeros_like, params)
    totals, (results, grad_list) = lax.scan(one_slot, zero_grads, (residual_all, cot_all, position_all))
    grad_qkv, grad_out, grad_up, grad_down, vector_grad = totals
    layer_out = results.reshape(TOKENS, D).astype(jnp.bfloat16)
    input_grad = grad_list.reshape(TOKENS, D)
    qkv_new, qkv_moment_new = muon_update(qkv_weight, qkv_moment, grad_qkv, rate_qkv, True)
    out_new, out_moment_new = muon_update(out_weight, out_moment, grad_out, rate_out, False)
    up_new, up_moment_new = muon_update(up_weight, up_moment, grad_up, rate_up, True)
    down_new, down_moment_new = muon_update(down_weight, down_moment, grad_down, rate_down, False)
    first_new = first_decay * vector_first + (1.0 - first_decay) * vector_grad
    second_new = second_decay * vector_second + (1.0 - second_decay) * vector_grad * vector_grad
    first_hat = first_new / (1.0 - first_decay ** STEP)
    second_hat = second_new / (1.0 - second_decay ** STEP)
    vectors_new = vectors - adam_rate * first_hat / (jnp.sqrt(second_hat) + adam_epsilon)
    return (layer_out, input_grad, qkv_new, out_new, up_new, down_new, qkv_moment_new, out_moment_new, up_moment_new, down_moment_new, first_new, second_new, vectors_new)
```

```python
import jax
import jax.numpy as jnp
from jax import lax
from jax.sharding import Mesh
from jax.sharding import PartitionSpec as P

HEAD = 64
ROT = 32
BR = 256
SWEEPS = 5
STEP = 10

highest = lax.Precision.HIGHEST
norm_epsilon = 1e-05
ortho_epsilon = 1e-07
masked_score = -1e30
rotary_base = 10000.0
muon_decay = 0.95
coef_linear = 3.4445
coef_square = -4.775
coef_cubic = 2.0315
decay_factor = 0.01
rate_qkv = 1.0
rate_out = 4.0
rate_up = 0.8
rate_down = 0.4
adam_rate = 0.2
first_decay = 0.9
second_decay = 0.95
adam_epsilon = 1e-08

f32 = jnp.float32
bf16 = jnp.bfloat16
PLANE = ("x", "y")
GROUP = ("core", "tensor")
DP = ("x", "y", "core")
ALL = ("x", "y", "core", "tensor")


def rotary_tables(positions, half_rot):
    freq_index = jnp.arange(half_rot).astype(f32)
    inverse_freq = rotary_base ** (-2.0 * freq_index / (2 * half_rot))
    angles = positions.astype(f32)[:, None] * inverse_freq[None, :]
    return (jnp.cos(angles)[:, None, :], jnp.sin(angles)[:, None, :])


def rotate(vectors_in, cosine_table, sine_table, half_rot):
    first_half = vectors_in[..., :half_rot]
    second = vectors_in[..., half_rot : 2 * half_rot]
    remainder = vectors_in[..., 2 * half_rot :]
    return jnp.concatenate(
        [
            first_half * cosine_table - second * sine_table,
            second * cosine_table + first_half * sine_table,
            remainder,
        ],
        -1,
    )


def unrotate(grads_in, cosine_table, sine_table, half_rot):
    first_half = grads_in[..., :half_rot]
    second = grads_in[..., half_rot : 2 * half_rot]
    remainder = grads_in[..., 2 * half_rot :]
    return jnp.concatenate(
        [
            first_half * cosine_table + second * sine_table,
            second * cosine_table - first_half * sine_table,
            remainder,
        ],
        -1,
    )


def gelu_tanh(values):
    return jax.nn.gelu(values, approximate=True)


def fold_in(qkv, up):
    rows = qkv.shape[0]
    halves = qkv.shape[2] // 2
    qkv_part = qkv.reshape(rows, 3, 2, halves).transpose(2, 0, 1, 3).reshape(2, rows, 3 * halves)
    up_part = up.reshape(rows, 2, -1).transpose(1, 0, 2)
    return jnp.concatenate([qkv_part, up_part], -1)


def fold_out(out, down):
    width = out.shape[1]
    out_part = out.reshape(2, -1, width).transpose(0, 2, 1)
    down_part = down.reshape(2, -1, width).transpose(0, 2, 1)
    return jnp.concatenate([out_part, down_part], -1)


def unfold_in(both, qkv_shape, up_shape):
    rows = both.shape[1]
    halves = qkv_shape[2] // 2
    qkv = both[:, :, : 3 * halves].reshape(2, rows, 3, halves).transpose(1, 2, 0, 3)
    up = both[:, :, 3 * halves :].transpose(1, 0, 2)
    return qkv.reshape(qkv_shape), up.reshape(up_shape)


def unfold_out(both, out_shape, down_shape):
    out_rows = out_shape[0] // 2
    out = both[:, :, :out_rows].transpose(0, 2, 1).reshape(out_shape)
    down = both[:, :, out_rows:].transpose(0, 2, 1).reshape(down_shape)
    return out, down


def orthogonalize(tall):
    norm = jnp.sqrt(jnp.sum(tall * tall))
    current = tall / (norm + ortho_epsilon)
    for sweep_index in range(SWEEPS):
        gram = jnp.einsum("ki,kj->ij", current, current, precision=highest)
        polynomial = coef_square * gram + coef_cubic * jnp.dot(gram, gram, precision=highest)
        current = coef_linear * current + jnp.dot(current, polynomial, precision=highest)
    return current


def gather_weights(low):
    mine = lax.all_to_all(low, "core", split_axis=0, concat_axis=0, tiled=True)
    mine = mine.reshape(2 * low.shape[1], low.shape[2])
    return lax.all_gather(mine, PLANE, axis=0, tiled=True)


def reduce_weights(grad):
    mine = lax.psum_scatter(grad, PLANE, scatter_dimension=0, tiled=True)
    mine = mine.reshape(2, mine.shape[0] // 2, mine.shape[1])
    return lax.all_to_all(mine, "core", split_axis=0, concat_axis=0, tiled=True)


def local(
    inputs,
    cotangent,
    positions,
    qkv_weight,
    out_weight,
    up_weight,
    down_weight,
    qkv_moment,
    out_moment,
    up_moment,
    down_moment,
    vectors,
    vector_first,
    vector_second,
):
    core = lax.axis_index("core")
    tensor_rank = lax.axis_index("tensor")
    device_rank = lax.axis_index(ALL)
    feature = inputs.shape[1]

    in_full = gather_weights(fold_in(qkv_weight, up_weight).astype(bf16))
    out_full = gather_weights(fold_out(out_weight, down_weight).astype(bf16))
    tokens = lax.all_gather(inputs, GROUP, axis=0, tiled=True)
    cot_full = lax.all_gather(cotangent, GROUP, axis=0, tiled=True)
    position_full = lax.all_gather(positions, "core", axis=0, tiled=True)

    vector_rows, vector_width = vectors.shape
    packed = jnp.pad(vectors.reshape(1, -1), ((0, 0), (0, 256 - vector_rows * vector_width)))
    packed = lax.all_gather(packed, ALL, axis=0, tiled=True)
    vector_table = (
        packed[:, : vector_rows * vector_width]
        .reshape(-1, vector_rows, vector_width)
        .transpose(1, 0, 2)
        .reshape(vector_rows, feature)
    )

    head_width = qkv_weight.shape[2] // 2
    hidden_width = up_weight.shape[1] // 2
    part = tensor_rank * 2 + core
    qkv_bias = lax.dynamic_slice_in_dim(vector_table[2:5], part * head_width, head_width, 1)
    up_bias = lax.dynamic_slice_in_dim(
        vector_table[7:].reshape(-1), part * hidden_width, hidden_width, 0
    )
    norm_gain = vector_table[0]
    norm_shift = vector_table[1]

    def standardize(rows):
        residual = rows.astype(f32)
        center = residual - jnp.mean(residual, -1, keepdims=True)
        variance = jnp.mean(center * center, -1, keepdims=True)
        scale_inv = lax.rsqrt(variance + norm_epsilon)
        return residual, center * scale_inv, scale_inv

    hidden = (standardize(tokens)[1] * norm_gain + norm_shift).astype(bf16)
    row_count = hidden.shape[0]
    heads = head_width // HEAD
    groups = 2
    group_rows = row_count // groups

    in_lin = jnp.dot(hidden, in_full, preferred_element_type=f32)
    qkv_lin = in_lin[:, : 3 * head_width].reshape(row_count, 3, head_width) + qkv_bias[None]
    up_lin = in_lin[:, 3 * head_width :] + up_bias
    cosine_table, sine_table = rotary_tables(position_full, ROT // 2)

    def headed(part_in):
        return part_in.reshape(row_count, heads, HEAD)

    def grouped(part_in):
        return part_in.reshape(groups, group_rows, heads, HEAD)

    query_low = grouped(
        rotate(headed(qkv_lin[:, 0]), cosine_table, sine_table, ROT // 2).astype(bf16)
    )
    key_low = grouped(
        rotate(headed(qkv_lin[:, 1]), cosine_table, sine_table, ROT // 2).astype(bf16)
    )
    value_low = grouped(headed(qkv_lin[:, 2]).astype(bf16))
    scale_value = HEAD ** (-0.5)
    ids = jnp.arange(group_rows)
    position_group = position_full.reshape(groups, group_rows)
    visible = (ids[None, None, :] <= ids[None, :, None]) & (
        ids[None, :, None] - ids[None, None, :] <= position_group[:, :, None]
    )
    scores = (
        jnp.einsum("gqhe,gkhe->ghqk", query_low, key_low, preferred_element_type=f32)
        * scale_value
    )
    scores = jnp.where(visible[:, None], scores, masked_score)
    row_max = jnp.max(scores, -1, keepdims=True)
    exp_scores = jnp.exp(scores - row_max)
    soft = exp_scores / jnp.sum(exp_scores, -1, keepdims=True)
    soft_low = soft.astype(bf16)
    attended = jnp.einsum(
        "ghqk,gkhe->gqhe", soft_low, value_low, preferred_element_type=f32
    ).astype(bf16)
    activated, gelu_back = jax.vjp(gelu_tanh, up_lin)
    middle = jnp.concatenate(
        [attended.reshape(row_count, head_width), activated.astype(bf16)], -1
    )
    partial_sum = lax.dot_general(
        middle, out_full, (((1,), (1,)), ((), ())), preferred_element_type=f32
    )
    summed = lax.psum_scatter(
        partial_sum.astype(bf16), GROUP, scatter_dimension=0, tiled=True
    ).astype(f32)

    grad_middle = jnp.dot(cot_full, out_full, preferred_element_type=f32)
    grad_up_lin = gelu_back(grad_middle[:, head_width:])[0].astype(bf16)
    grad_attended = grouped(headed(grad_middle[:, :head_width].astype(bf16)))
    grad_out_full = lax.dot_general(
        cot_full, middle, (((0,), (0,)), ((), ())), preferred_element_type=f32
    )

    grad_values = jnp.einsum(
        "ghqk,gqhe->gkhe", soft_low, grad_attended, preferred_element_type=f32
    )
    grad_soft = jnp.einsum(
        "gqhe,gkhe->ghqk", grad_attended, value_low, preferred_element_type=f32
    )
    row_delta = jnp.sum(soft * grad_soft, -1, keepdims=True)
    grad_scores = (soft * (grad_soft - row_delta)).astype(bf16)
    grad_query = (
        jnp.einsum("ghqk,gkhe->gqhe", grad_scores, key_low, preferred_element_type=f32)
        * scale_value
    )
    grad_keys = (
        jnp.einsum("ghqk,gqhe->gkhe", grad_scores, query_low, preferred_element_type=f32)
        * scale_value
    )

    def flat(part_in):
        return part_in.reshape(row_count, heads, HEAD)

    grad_in = jnp.concatenate(
        [
            unrotate(flat(grad_query), cosine_table, sine_table, ROT // 2)
            .reshape(row_count, head_width)
            .astype(bf16),
            unrotate(flat(grad_keys), cosine_table, sine_table, ROT // 2)
            .reshape(row_count, head_width)
            .astype(bf16),
            grad_values.reshape(row_count, head_width).astype(bf16),
            grad_up_lin,
        ],
        -1,
    )
    grad_in_full = lax.dot_general(
        hidden, grad_in, (((0,), (0,)), ((), ())), preferred_element_type=f32
    )
    bias_grad = jnp.sum(grad_in.astype(f32), 0)
    reduced_in = reduce_weights(grad_in_full.astype(bf16)).astype(f32)
    reduced_out = reduce_weights(grad_out_full.astype(bf16)).astype(f32)

    grad_hidden_part = lax.dot_general(
        grad_in, in_full, (((1,), (1,)), ((), ())), preferred_element_type=f32
    )
    grad_hidden = lax.psum_scatter(
        grad_hidden_part.astype(bf16), GROUP, scatter_dimension=0, tiled=True
    ).astype(f32)

    residual, normed, scale_inv = standardize(inputs)
    layer_out = (residual + summed + vector_table[5] + vector_table[6]).astype(bf16)
    cot_local = cotangent.astype(f32)
    grad_hat = grad_hidden * norm_gain
    input_grad = cot_local + scale_inv * (
        grad_hat
        - jnp.mean(grad_hat, -1, keepdims=True)
        - normed * jnp.mean(grad_hat * normed, -1, keepdims=True)
    )
    gain_grad = jnp.sum(grad_hidden * normed, 0)
    shift_grad = jnp.sum(grad_hidden, 0)
    out_bias_grad = jnp.sum(cot_local, 0)
    qkv_rows = lax.dynamic_update_slice(
        jnp.zeros((3, feature), f32),
        bias_grad[: 3 * head_width].reshape(3, head_width),
        (0, part * head_width),
    )
    up_row = lax.dynamic_update_slice(
        jnp.zeros(((vector_rows - 7) * feature,), f32),
        bias_grad[3 * head_width :],
        (part * hidden_width,),
    )
    vector_part = jnp.concatenate(
        [
            gain_grad[None],
            shift_grad[None],
            qkv_rows,
            out_bias_grad[None],
            out_bias_grad[None],
            up_row.reshape(-1, feature),
        ],
        0,
    )
    vector_sum = lax.psum(vector_part, ALL)
    vector_grad = lax.dynamic_slice_in_dim(vector_sum, device_rank * vector_width, vector_width, 1)
    first_new = first_decay * vector_first + (1.0 - first_decay) * vector_grad
    second_new = second_decay * vector_second + (1.0 - second_decay) * vector_grad * vector_grad
    first_hat = first_new / (1.0 - first_decay**STEP)
    second_hat = second_new / (1.0 - second_decay**STEP)
    vectors_new = vectors - adam_rate * first_hat / (jnp.sqrt(second_hat) + adam_epsilon)

    moment_in = muon_decay * fold_in(qkv_moment, up_moment) + reduced_in
    moment_out = muon_decay * fold_out(out_moment, down_moment) + reduced_out
    nesterov_in = reduced_in + muon_decay * moment_in
    nesterov_out = reduced_out + muon_decay * moment_out

    def cut(both):
        halves, rows, columns = both.shape
        return both.reshape(halves, rows, columns // BR, BR).transpose(0, 2, 1, 3).reshape(
            -1, rows, BR
        )

    def paste(pieces):
        rows = pieces.shape[1]
        return (
            pieces.reshape(2, -1, rows, BR).transpose(0, 2, 1, 3).reshape(2, rows, -1)
        )

    pieces = jnp.concatenate([cut(nesterov_in), cut(nesterov_out)], 0).astype(bf16)
    piece_count = pieces.shape[0]
    count_in = 2 * nesterov_in.shape[2] // BR
    rank_count = lax.axis_size(DP)
    outgoing = jnp.concatenate(
        [pieces, jnp.zeros((rank_count - piece_count,) + pieces.shape[1:], bf16)], 0
    )
    received = lax.all_to_all(outgoing, DP, split_axis=0, concat_axis=0, tiled=True)
    orthogonal = orthogonalize(received.reshape(-1, BR).astype(f32))
    returned = lax.all_to_all(
        orthogonal.astype(bf16).reshape(received.shape), DP, split_axis=0, concat_axis=0, tiled=True
    ).astype(f32)
    update_qkv, update_up = unfold_in(paste(returned[:count_in]), qkv_weight.shape, up_weight.shape)
    update_out, update_down = unfold_out(
        paste(returned[count_in:piece_count]), out_weight.shape, down_weight.shape
    )
    qkv_moment_new, up_moment_new = unfold_in(moment_in, qkv_weight.shape, up_weight.shape)
    out_moment_new, down_moment_new = unfold_out(moment_out, out_weight.shape, down_weight.shape)
    qkv_new = qkv_weight * (1.0 - decay_factor * rate_qkv) - rate_qkv * update_qkv
    out_new = out_weight * (1.0 - decay_factor * rate_out) - rate_out * update_out
    up_new = up_weight * (1.0 - decay_factor * rate_up) - rate_up * update_up
    down_new = down_weight * (1.0 - decay_factor * rate_down) - rate_down * update_down
    return (
        layer_out,
        input_grad,
        qkv_new,
        out_new,
        up_new,
        down_new,
        qkv_moment_new,
        out_moment_new,
        up_moment_new,
        down_moment_new,
        first_new,
        second_new,
        vectors_new,
    )


def solution(mesh):
    wide = Mesh(mesh.devices.reshape(4, 4, 2, 4), ALL)
    in_specs = (
        P(ALL, None),
        P(ALL, None),
        P(DP),
        P(DP, None, "tensor"),
        P("tensor", DP),
        P(DP, "tensor"),
        P("tensor", DP),
        P(DP, None, "tensor"),
        P("tensor", DP),
        P(DP, "tensor"),
        P("tensor", DP),
        P(None, ALL),
        P(None, ALL),
        P(None, ALL),
    )
    out_specs = (
        P(ALL, None),
        P(ALL, None),
        P(DP, None, "tensor"),
        P("tensor", DP),
        P(DP, "tensor"),
        P("tensor", DP),
        P(DP, None, "tensor"),
        P("tensor", DP),
        P(DP, "tensor"),
        P("tensor", DP),
        P(None, ALL),
        P(None, ALL),
        P(None, ALL),
    )
    return jax.shard_map(local, mesh=wide, in_specs=in_specs, out_specs=out_specs, check_vma=False)
```

```python
import jax
import jax.numpy as jnp
from jax import lax
from jax.experimental import pallas as pl
from jax.experimental.pallas import tpu as pltpu
from jax.sharding import Mesh
from jax.sharding import PartitionSpec as P

STEP = 10

rotary_base = 10000.0
decay_factor = 0.01
rate_qkv = 1.0
rate_out = 4.0
rate_up = 0.8
rate_down = 0.4
adam_rate = 0.2
first_decay = 0.9
second_decay = 0.95
adam_epsilon = 1e-08

f32 = jnp.float32
bf16 = jnp.bfloat16
DP = ("x", "y", "core")
ALL = ("x", "y", "core", "tensor")

MESH = pl.DeviceIdType.MESH
RING = 4
WIRES = 140


def turn(index, step, size=RING):
    return lax.rem(index + (step % size), size)


class Wire:
    def __init__(self, send_sem, recv_sem):
        self.send_sem, self.recv_sem, self.sent = send_sem, recv_sem, []

    def copy(self, src, dst, device):
        number = len(self.sent)
        remote = pltpu.make_async_remote_copy(
            src_ref=src,
            dst_ref=dst,
            send_sem=self.send_sem.at[number],
            recv_sem=self.recv_sem.at[number],
            device_id=device,
            device_id_type=MESH,
        )
        remote.start()
        self.sent.append(remote)
        return remote

    def drain(self):
        for remote in self.sent:
            remote.wait_send()


def rows_at(start, size):
    return pl.ds(pl.multiple_of(start, 16), size)


def greet(peers):
    barrier = pltpu.get_barrier_semaphore()
    for peer in peers:
        pl.semaphore_signal(barrier, inc=1, device_id=peer, device_id_type=MESH)
    pl.semaphore_wait(barrier, len(peers))


def plane_peers():
    place = lax.axis_index("x") * RING + lax.axis_index("y")
    peers = []
    for step in range(1, RING * RING):
        other = turn(place, step, RING * RING)
        peers.append({"x": other // RING, "y": lax.rem(other, RING)})
    return peers


def column_peers():
    place = lax.axis_index("core") * RING + lax.axis_index("tensor")
    peers = []
    for step in range(1, 2 * RING):
        other = turn(place, step, 2 * RING)
        peers.append({"core": other // RING, "tensor": lax.rem(other, RING)})
    return peers


def spread_rows(wire, table, half, rows, first, second, own=None):
    here_first, here_second = lax.axis_index(first), lax.axis_index(second)
    quarter = rows // 2

    def block(step_first, step_second, low, size):
        index = {first: turn(here_first, step_first), second: turn(here_second, step_second)}
        chip = index["x"] * RING + index["y"]
        return table.at[rows_at(chip * 2 * rows + half * rows + low, size)]

    def send(step_first, step_second, low, size, axis, direction):
        ref = src = block(step_first, step_second, low, size)
        if own is not None and step_first == 0 and step_second == 0:
            src = own
        here = here_first if axis == first else here_second
        return wire.copy(src, ref, {axis: turn(here, direction)})

    def both(step_first):
        return [send(step_first, 0, 0, rows, second, way) for way in (1, -1)]

    ahead = send(0, 0, 0, rows, first, 1)
    back = send(0, 0, 0, rows, first, -1)
    lines = {0: both(0)}
    yield
    ahead.wait_recv()
    tail_ahead = send(-1, 0, 0, quarter, first, 1)
    lines[-1] = both(-1)
    yield
    back.wait_recv()
    tail_back = send(1, 0, quarter, quarter, first, -1)
    lines[1] = both(1)
    tails = []

    def relay(step_first):
        from_back, from_ahead = lines[step_first]
        from_back.wait_recv()
        tails.append(send(step_first, -1, 0, quarter, second, 1))
        from_ahead.wait_recv()
        tails.append(send(step_first, 1, quarter, quarter, second, -1))

    yield
    relay(0)
    yield
    tail_ahead.wait_recv()
    tail_back.wait_recv()
    lines[2] = both(2)
    yield
    relay(-1)
    yield
    relay(1)
    yield
    relay(2)
    yield
    for tail in tails:
        tail.wait_recv()


def spread_tokens(wire, table, rows, own=None):
    here, core = lax.axis_index("tensor"), lax.axis_index("core")
    half = rows // 2

    def send(step, low, size, device):
        ref = table.at[rows_at((core * RING + turn(here, step)) * rows + low, size)]
        src = own if own is not None and step == 0 else ref
        return wire.copy(src, ref, device)

    sibling = {"core": 1 - core}
    ahead = send(0, 0, rows, {"tensor": turn(here, 1)})
    back = send(0, 0, rows, {"tensor": turn(here, -1)})
    across = [send(0, 0, rows, sibling)]
    yield
    ahead.wait_recv()
    tail_ahead = send(-1, 0, half, {"tensor": turn(here, 1)})
    across.append(send(-1, 0, rows, sibling))
    yield
    back.wait_recv()
    tail_back = send(1, half, half, {"tensor": turn(here, -1)})
    across.append(send(1, 0, rows, sibling))
    yield
    tail_ahead.wait_recv()
    tail_back.wait_recv()
    across.append(send(2, 0, rows, sibling))
    yield
    for remote in across:
        remote.wait_recv()


TILE = 16


def add_rows(target, sources, dtype=None):
    rows = target.shape[0]

    def body(step, carry):
        at = pl.ds(pl.multiple_of(step * TILE, TILE), TILE)
        total = sources[0][at, :].astype(f32)
        for source in sources[1:]:
            total = total + source[at, :].astype(f32)
        target[at, :] = total.astype(target.dtype)
        return carry

    lax.fori_loop(0, rows // TILE, body, 0)


def reduce_rows(wire, grad, half, rows, first, second, up1, down1, up2, down2, result):
    here_first, here_second = lax.axis_index(first), lax.axis_index(second)
    part = rows // 2
    top, bottom = pl.ds(0, part), pl.ds(part, part)

    def block(step_first, step_second, low, size):
        index = {first: turn(here_first, step_first), second: turn(here_second, step_second)}
        chip = index["x"] * RING + index["y"]
        return grad.at[rows_at(chip * 2 * rows + half * rows + low, size)]

    ahead, back = {first: turn(here_first, 1)}, {first: turn(here_first, -1)}
    order = (2, 1, -1, 0)
    far, near = {}, {}
    for slot, ss in enumerate(order):
        far[ss] = (
            wire.copy(block(2, ss, 0, part), up1.at[slot], ahead),
            wire.copy(block(2, ss, part, part), down1.at[slot], back),
        )
        near[ss] = [
            wire.copy(block(1, ss, part, part), up2.at[slot, bottom], ahead),
            wire.copy(block(-1, ss, 0, part), down2.at[slot, top], back),
        ]
    yield
    for slot, ss in enumerate(order):
        far[ss][0].wait_recv()
        add_rows(up1.at[slot], [up1.at[slot], block(1, ss, 0, part)])
        near[ss].append(wire.copy(up1.at[slot], up2.at[slot, top], ahead))
        far[ss][1].wait_recv()
        add_rows(down1.at[slot], [down1.at[slot], block(-1, ss, part, part)])
        near[ss].append(wire.copy(down1.at[slot], down2.at[slot, bottom], back))
        yield
    ahead, back = {second: turn(here_second, 1)}, {second: turn(here_second, -1)}
    last = []
    for slot, ss in enumerate(order):
        for remote in near[ss]:
            remote.wait_recv()
        if ss == 0:
            break
        add_rows(up2.at[slot], [up2.at[slot], down2.at[slot], block(0, ss, 0, rows)])
        total = up2.at[slot]
        if ss == 2:
            across = (
                wire.copy(total.at[top], up1.at[4], ahead),
                wire.copy(total.at[bottom], down1.at[4], back),
            )
        elif ss == 1:
            last.append(wire.copy(total.at[bottom], up2.at[4, bottom], ahead))
            across[0].wait_recv()
            add_rows(up1.at[4], [up1.at[4], total.at[top]])
            last.append(wire.copy(up1.at[4], up2.at[4, top], ahead))
        else:
            last.append(wire.copy(total.at[top], down2.at[4, top], back))
            across[1].wait_recv()
            add_rows(down1.at[4], [down1.at[4], total.at[bottom]])
            last.append(wire.copy(down1.at[4], down2.at[4, bottom], back))
        yield
    for remote in last:
        remote.wait_recv()
    add_rows(result, [up2.at[3], down2.at[3], block(0, 0, 0, rows), up2.at[4], down2.at[4]])


def reduce_tokens(wire, partial, rows, pair, up1, down1, up2, down2, result):
    here, core = lax.axis_index("tensor"), lax.axis_index("core")
    part = rows // 2
    top, bottom = pl.ds(0, part), pl.ds(part, part)
    ahead, back = {"tensor": turn(here, 1)}, {"tensor": turn(here, -1)}

    def block(side, step):
        return partial.at[rows_at((side * RING + turn(here, step)) * rows, rows)]

    order = (2, 1, -1, 0)
    across = [
        wire.copy(block(1 - core, step), pair.at[slot], {"core": 1 - core})
        for slot, step in enumerate(order)
    ]
    yield
    near = []
    for slot, step in enumerate(order):
        across[slot].wait_recv()
        if step == 0:
            break
        add_rows(pair.at[slot], [pair.at[slot], block(core, step)])
        total = pair.at[slot]
        if step == 2:
            far = (
                wire.copy(total.at[top], up1, ahead),
                wire.copy(total.at[bottom], down1, back),
            )
        elif step == 1:
            near.append(wire.copy(total.at[bottom], up2.at[bottom], ahead))
        else:
            near.append(wire.copy(total.at[top], down2.at[top], back))
        yield
    far[0].wait_recv()
    add_rows(up1, [up1, pair.at[1, top]])
    near.append(wire.copy(up1, up2.at[top], ahead))
    far[1].wait_recv()
    add_rows(down1, [down1, pair.at[2, bottom]])
    near.append(wire.copy(down1, down2.at[bottom], back))
    yield
    for remote in near:
        remote.wait_recv()
    add_rows(result, [pair.at[3], block(core, 0), up2, down2])


HEAD = 64
ROT = 32
norm_epsilon = 1e-05
masked_score = -1e30
GROUP_ROWS = 512
LANES = 128
WIDE = 256
gelu_scale = 0.7978845608028654
gelu_cubic = 0.044715
scale_value = HEAD ** (-0.5)
ROWS_CROSS = ((1,), (1,))
COLUMNS_CROSS = ((0,), (0,))


def matmul(left, right, contract=((1,), (0,))):
    return lax.dot_general(left, right, (contract, ((), ())), preferred_element_type=f32)


def lane_ids(rows, width):
    return lax.broadcasted_iota(jnp.int32, (rows, width), 1)


def swap_halves(values):
    width = values.shape[1]
    lane = lax.rem(lane_ids(*values.shape), HEAD)
    half = ROT // 2
    return jnp.where(
        lane < half, pltpu.roll(values, width - half, 1), pltpu.roll(values, half, 1)
    )


def turned(values, cosine, sine):
    return values * cosine + swap_halves(values) * sine


def head_lanes(values, side):
    keep = lane_ids(*values.shape) // HEAD == side
    return jnp.where(keep, values, jnp.zeros_like(values))


def visible_block(start, row_low, row_count, column_count):
    rows = lax.broadcasted_iota(jnp.int32, (row_count, column_count), 0) + row_low
    columns = lax.broadcasted_iota(jnp.int32, (row_count, column_count), 1)
    return (columns <= rows) & (columns.astype(f32) >= start)


def normalize(rows, gain, shift):
    residual = rows.astype(f32)
    center = residual - jnp.mean(residual, -1, keepdims=True)
    variance = jnp.mean(center * center, -1, keepdims=True)
    return center * lax.rsqrt(variance + norm_epsilon) * gain + shift


def norm_pieces(tokens, hidden, table, pieces):
    count = tokens.shape[0] // pieces
    step_rows = 16
    for piece in range(pieces):

        def body(step, carry):
            at = pl.ds(pl.multiple_of(piece * count + step * step_rows, step_rows), step_rows)
            hidden[at, :] = normalize(tokens[at, :], table[0:1, :], table[1:2, :]).astype(bf16)
            return carry

        lax.fori_loop(0, count // step_rows, body, 0)
        yield


def project_pieces(hidden, in_full, table, cosine, sine, qkv, middle, gelu_slope):
    part = lax.axis_index("tensor") * 2 + lax.axis_index("core")
    rows = hidden.shape[0]
    half = rows // 2
    for index in range(3):
        at = pl.ds(index * WIDE, WIDE)
        bias = table[2 + index : 3 + index, pl.ds(pl.multiple_of(part * WIDE, WIDE), WIDE)]

        def body(step, carry):
            down = pl.ds(pl.multiple_of(step * half, half), half)
            values = matmul(hidden[down, :], in_full[:, at]) + bias
            if index < 2:
                wide = [jnp.concatenate([t[down, :]] * 2, 1) for t in (cosine, sine)]
                values = turned(values, *wide)
            qkv[down, at] = values.astype(bf16)
            return carry

        lax.fori_loop(0, 2, body, 0)
        yield
    hidden_units = in_full.shape[1] - 3 * WIDE
    for index in range(hidden_units // WIDE):
        at = pl.ds(3 * WIDE + index * WIDE, WIDE)
        to = pl.ds(WIDE + index * WIDE, WIDE)
        slope_at = pl.ds(index * WIDE, WIDE)
        core, row = lax.axis_index("core"), 7 + lax.axis_index("tensor")
        low = pl.multiple_of(core * hidden_units + index * WIDE, WIDE)
        bias = table[pl.ds(row, 1), pl.ds(low, WIDE)]

        def body(step, carry):
            down = pl.ds(pl.multiple_of(step * half, half), half)
            unit = matmul(hidden[down, :], in_full[:, at]) + bias
            square = unit * unit
            curve = jnp.tanh(gelu_scale * (unit + gelu_cubic * unit * square))
            rise = 0.5 * (1.0 + curve)
            middle[down, to] = (unit * rise).astype(bf16)
            bend = 0.5 * gelu_scale * unit * (1.0 + 3.0 * gelu_cubic * square)
            gelu_slope[down, slope_at] = rise + bend * (1.0 - curve * curve)
            return carry

        lax.fori_loop(0, 2, body, 0)
        yield


def attend_pieces(qkv, start, middle, lse):
    for group in range(2):
        base = group * GROUP_ROWS
        for pair in range(2):
            for tile in range(2):
                low, count = tile * WIDE, (tile + 1) * WIDE
                down = pl.ds(base + low, WIDE)
                keys_at = pl.ds(base, count)
                queries = qkv[down, pl.ds(pair * LANES, LANES)]
                keys = qkv[keys_at, pl.ds(WIDE + pair * LANES, LANES)]
                values = qkv[keys_at, pl.ds(2 * WIDE + pair * LANES, LANES)]
                visible = visible_block(start[down, 0:1], low, WIDE, count)
                outs = []
                for side in range(2):
                    scores = matmul(head_lanes(queries, side), keys, ROWS_CROSS) * scale_value
                    scores = jnp.where(visible, scores, masked_score)
                    top = jnp.max(scores, -1, keepdims=True)
                    raised = jnp.exp(scores - top)
                    total = jnp.sum(raised, -1, keepdims=True)
                    soft = (raised / total).astype(bf16)
                    outs.append(matmul(soft, values))
                    head = pair * 2 + side
                    here = lane_ids(WIDE, LANES) == head
                    lse[down, :] = jnp.where(here, top + jnp.log(total), lse[down, :])
                first = lane_ids(WIDE, LANES) < HEAD
                middle[down, pl.ds(pair * LANES, LANES)] = jnp.where(
                    first, outs[0], outs[1]
                ).astype(bf16)
            yield


def outer_pieces(left, right, at, target):
    for step in range(left.shape[1] // WIDE):
        down = pl.ds(step * WIDE, WIDE)
        target[down, :] = matmul(left[:, down], right[:, at], COLUMNS_CROSS).astype(bf16)
        yield


def in_turn(processes):
    waiting = list(processes)
    while waiting:
        for process in list(waiting):
            if next(process, waiting) is waiting:
                waiting.remove(process)
            yield


def weave(work, wire_steps, per_piece):
    debt = 0.0
    for _ in work:
        debt += per_piece
        while debt >= 1.0:
            debt -= 1.0
            next(wire_steps, None)


def chained(*parts):
    for part in parts:
        yield from part


def forward_kernel(
    in_low, out_low, tokens, cotangent, turns, vector, in_moment, out_moment,
    in_save, out_save, cot_save, hidden_save, qkv_save, lse_save, slope_save, middle_save,
    grad_save, turns_save, in_cross, out_cross, table,
    in_full, out_full, tokens_full, cot_full, hidden, qkv, lse, slope, middle, grad_out,
    turns_full, slots, mine, send_sem, recv_sem, local_sem, save_sem,
):
    core = lax.axis_index("core")
    chip = lax.axis_index("x") * RING + lax.axis_index("y")
    column = core * RING + lax.axis_index("tensor")
    rows = in_low.shape[1]
    token_rows = tokens.shape[0]
    sibling = {"core": 1 - core}
    greet(plane_peers() + column_peers())
    wire = Wire(send_sem, recv_sem)
    saves = []

    def save(src, dst):
        copy = pltpu.make_async_copy(src, dst, save_sem.at[len(saves)])
        copy.start()
        saves.append(copy)

    own_rows = rows_at(chip * 2 * rows + core * rows, rows)
    own_tokens = rows_at(column * token_rows, token_rows)
    own_turns = rows_at(core * GROUP_ROWS, GROUP_ROWS)
    cross_in = wire.copy(in_low.at[1 - core], in_full.at[own_rows], sibling)
    vector_in = [wire.copy(vector, slots.at[column], peer) for peer in column_peers()]
    pairs = [
        (in_low.at[core], in_full.at[own_rows]),
        (out_low.at[core], out_full.at[own_rows]),
        (tokens, tokens_full.at[own_tokens]),
        (cotangent, cot_full.at[own_tokens]),
        (turns, turns_full.at[:, own_turns]),
        (vector, slots.at[column]),
    ]
    here = [
        pltpu.make_async_copy(src, dst, local_sem.at[number])
        for number, (src, dst) in enumerate(pairs)
    ]
    for copy in here:
        copy.start()
    token_steps = spread_tokens(wire, tokens_full, token_rows, tokens)
    next(token_steps)
    cross_out = wire.copy(out_low.at[1 - core], out_full.at[own_rows], sibling)
    cross_turns = wire.copy(turns, turns_full.at[:, own_turns], sibling)
    cross_moments = [
        wire.copy(in_moment.at[1 - core], in_cross, sibling),
        wire.copy(out_moment.at[1 - core], out_cross, sibling),
    ]
    here[0].wait()
    cross_in.wait_recv()
    weights_in = [
        spread_rows(wire, in_full, 0, rows, "x", "y"),
        spread_rows(wire, in_full, 1, rows, "y", "x"),
    ]
    for process in weights_in:
        next(process)
    for copy in here[1:]:
        copy.wait()
    cross_out.wait_recv()
    cross_turns.wait_recv()
    weights_out = [
        spread_rows(wire, out_full, 0, rows, "x", "y"),
        spread_rows(wire, out_full, 1, rows, "y", "x"),
    ]
    cot_steps = spread_tokens(wire, cot_full, token_rows, cotangent)
    for remote in vector_in:
        remote.wait_recv()
    mine[...] = jnp.sum(slots[...], axis=0)
    width = mine.shape[1]
    lanes = pl.ds(pl.multiple_of(chip * width, width), width)
    vector_out = [wire.copy(mine, table.at[:, lanes], peer) for peer in plane_peers()]
    table[:, lanes] = mine[...]
    in_steps = in_turn(weights_in)
    save(turns_full, turns_save)
    for _ in token_steps:
        next(in_steps)
        next(in_steps)
    next(cot_steps)
    for process in weights_out:
        next(process)
    for remote in vector_out:
        remote.wait_recv()
    weave(norm_pieces(tokens_full, hidden, table, 8), in_turn([*weights_in, cot_steps]), 1.0)
    save(hidden, hidden_save)
    for _ in in_turn([*weights_in, cot_steps]):
        pass
    save(in_full, in_save)
    save(cot_full, cot_save)
    out_steps = in_turn(weights_out)
    lse[...] = jnp.zeros_like(lse)
    work = chained(
        project_pieces(
            hidden, in_full, table, turns_full.at[0], turns_full.at[1], qkv, middle, slope
        ),
        attend_pieces(qkv, turns_full.at[2], middle, lse),
        outer_pieces(cot_full, middle, slice(None), grad_out),
    )
    weave(work, out_steps, 1.0)
    for source, target in (
        (qkv, qkv_save), (lse, lse_save), (slope, slope_save), (middle, middle_save),
        (grad_out, grad_save),
    ):
        save(source, target)
    for _ in out_steps:
        pass
    save(out_full, out_save)
    for remote in cross_moments:
        remote.wait_recv()
    wire.drain()
    for copy in saves:
        copy.wait()


def forward_all(in_low, out_low, tokens, cotangent, turns, vector, in_moment, out_moment):
    rows = in_low.shape[1]
    full = 2 * RING * RING * rows
    token_full, feature = 2 * RING * tokens.shape[0], tokens.shape[1]
    wide_in, wide_out = in_low.shape[2], out_low.shape[2]
    hidden_units = wide_out - WIDE
    any_spec = pl.BlockSpec(memory_space=pl.ANY)
    vmem = pl.BlockSpec(memory_space=pltpu.VMEM)
    kept = [
        ((full, wide_in), bf16),
        ((full, wide_out), bf16),
        ((token_full, feature), bf16),
        ((token_full, feature), bf16),
        ((token_full, 3 * WIDE), bf16),
        ((token_full, LANES), f32),
        ((token_full, hidden_units), f32),
        ((token_full, wide_out), bf16),
        ((full, wide_out), bf16),
        ((3, 2 * GROUP_ROWS, LANES), f32),
    ]
    scratch = kept[:2] + [((token_full, feature), bf16)] + kept[2:]
    table = (vector.shape[0], RING * RING * vector.shape[1])
    return pl.pallas_call(
        forward_kernel,
        out_shape=tuple(jax.ShapeDtypeStruct(*entry) for entry in kept)
        + tuple(jax.ShapeDtypeStruct(m.shape[1:], f32) for m in (in_moment, out_moment))
        + (jax.ShapeDtypeStruct(table, f32),),
        in_specs=[vmem] * 6 + [any_spec] * 2,
        out_specs=(any_spec,) * (len(kept) + 2) + (vmem,),
        scratch_shapes=[pltpu.VMEM(*entry) for entry in scratch]
        + [
            pltpu.VMEM((2 * RING,) + vector.shape, f32),
            pltpu.VMEM(vector.shape, f32),
            pltpu.SemaphoreType.DMA((WIRES,)),
            pltpu.SemaphoreType.DMA((WIRES,)),
            pltpu.SemaphoreType.DMA((6,)),
            pltpu.SemaphoreType.DMA((len(kept),)),
        ],
        compiler_params=pltpu.CompilerParams(
            collective_id=0, has_side_effects=True, vmem_limit_bytes=60 * 2**20
        ),
    )(in_low, out_low, tokens, cotangent, turns, vector, in_moment, out_moment)


REDUCES = 180
TOKEN_REDUCES = 10


class Pump:
    def __init__(self):
        self.lines, self.flip = [], 0

    def add(self, *lines):
        for line in lines:
            next(line)
            self.lines.append(line)

    def step(self):
        if self.lines:
            self.flip = (self.flip + 1) % 2
            line = self.lines[self.flip % len(self.lines)]
            if next(line, self) is self:
                self.lines.remove(line)

    def drive(self, work, per_piece):
        debt = 0.0
        for _ in work:
            debt += per_piece
            while debt >= 1.0:
                debt -= 1.0
                self.step()

    def finish(self):
        while self.lines:
            self.step()


class Stream:
    def __init__(self, tiles, slots, sems):
        self.tiles, self.slots, self.sems, self.copies = tiles, slots, sems, []
        for _ in range(2):
            self.fetch()

    def fetch(self):
        number = len(self.copies)
        if number < len(self.tiles):
            copy = pltpu.make_async_copy(
                self.tiles[number], self.slots[number % 2], self.sems.at[number % 2]
            )
            copy.start()
            self.copies.append(copy)

    def take(self, number):
        self.copies[number].wait()
        return self.slots[number % 2]


def middle_grad_pieces(cot, weights, slopes, grad_attended, lin_grad, count):
    for index in range(count):
        tile = weights.take(index)
        if index == 0:
            grad_attended[...] = matmul(cot[...], tile[...]).astype(bf16)
        else:
            slope = slopes.take(index - 1)
            half = cot.shape[0] // 2

            def body(step, carry):
                down = pl.ds(pl.multiple_of(step * half, half), half)
                values = matmul(cot[down, :], tile[...]) * slope[down, :]
                lin_grad[down, pl.ds(3 * WIDE + (index - 1) * WIDE, WIDE)] = values.astype(bf16)
                return carry

            lax.fori_loop(0, 2, body, 0)
            slopes.fetch()
        weights.fetch()
        yield


def back_pieces(left, weights, target, count):
    for index in range(count):
        tile = weights.take(index)
        target[:, pl.ds(index * WIDE, WIDE)] = matmul(left[...], tile[...], ROWS_CROSS).astype(
            bf16
        )
        weights.fetch()
        yield


def attend_back_pieces(qkv, turns, lse, grad_attended, lin_grad, key_sum, value_sum):
    cosine, sine, start = turns.at[0], turns.at[1], turns.at[2]

    def unturned(values, at):
        values = values * scale_value
        return (values * cosine[at, :] - swap_halves(values) * sine[at, :]).astype(bf16)

    for group in range(2):
        base = group * GROUP_ROWS
        for pair in range(2):
            lanes = pair * LANES
            for tile in (1, 0):
                low, count = tile * WIDE, (tile + 1) * WIDE
                down = pl.ds(base + low, WIDE)
                keys_at = pl.ds(base, count)
                queries = qkv[down, pl.ds(lanes, LANES)]
                keys = qkv[keys_at, pl.ds(WIDE + lanes, LANES)]
                values = qkv[keys_at, pl.ds(2 * WIDE + lanes, LANES)]
                grads = grad_attended[down, pl.ds(lanes, LANES)]
                visible = visible_block(start[down, 0:1], low, WIDE, count)
                query_grad = jnp.zeros((WIDE, LANES), f32)
                key_grad = jnp.zeros((count, LANES), f32)
                value_grad = jnp.zeros((count, LANES), f32)
                for side in range(2):
                    query, grad = head_lanes(queries, side), head_lanes(grads, side)
                    scores = matmul(query, keys, ROWS_CROSS) * scale_value
                    scores = jnp.where(visible, scores, masked_score)
                    head = pair * 2 + side
                    soft = jnp.exp(scores - lse[down, head : head + 1])
                    grad_soft = matmul(grad, values, ROWS_CROSS)
                    delta = jnp.sum(soft * grad_soft, -1, keepdims=True)
                    grad_scores = (soft * (grad_soft - delta)).astype(bf16)
                    query_grad += matmul(grad_scores, head_lanes(keys, side))
                    key_grad += matmul(grad_scores, query, COLUMNS_CROSS)
                    value_grad += matmul(soft.astype(bf16), grad, COLUMNS_CROSS)
                lin_grad[down, pl.ds(lanes, LANES)] = unturned(query_grad, down)
                if tile == 1:
                    key_sum[...] = key_grad
                    value_sum[...] = value_grad
                else:
                    key_sum[0:WIDE, :] += key_grad
                    value_sum[0:WIDE, :] += value_grad
                yield
            all_rows = pl.ds(base, GROUP_ROWS)
            lin_grad[all_rows, pl.ds(WIDE + lanes, LANES)] = unturned(key_sum[...], all_rows)
            lin_grad[all_rows, pl.ds(2 * WIDE + lanes, LANES)] = value_sum[...].astype(bf16)


def backward_kernel(
    in_save, out_save, cot_save, hidden_save, qkv_save, lse_save, slope_save, middle_save,
    grad_save, turns_save,
    in_result, out_result, first_sum, second_sum, bias_sum,
    token_matrix, columns_low, columns_high, rows_low, rows_high, slope_low, slope_high,
    qkv, lse, turns, middle, grad_out, grad_in, lin_grad, grad_attended, summand,
    key_sum, value_sum,
    out_up1, out_down1, out_up2, out_down2,
    up_up1, up_down1, up_up2, up_down2,
    qkv_up1, qkv_down1, qkv_up2, qkv_down2,
    pair, up1, down1, up2, down2,
    send_sem, recv_sem, token_send, token_recv, load_sem, stream_sem, credit,
):
    core = lax.axis_index("core")
    z = lax.axis_index("tensor")
    rows = in_result.shape[1]
    token_rows = first_sum.shape[0]
    hidden_units = slope_save.shape[1]
    qkv_width = qkv.shape[1]
    feature = token_matrix.shape[1]

    def load(number, source, target):
        copy = pltpu.make_async_copy(source, target, load_sem.at[number])
        copy.start()
        return copy

    grad_load = load(0, grad_save, grad_out)
    cot_load = load(1, cot_save, token_matrix)
    out_tiles = Stream(
        [out_save.at[:, pl.ds(index * WIDE, WIDE)] for index in range(1 + hidden_units // WIDE)],
        [columns_low, columns_high],
        stream_sem.at[0],
    )
    slopes = Stream(
        [slope_save.at[:, pl.ds(index * WIDE, WIDE)] for index in range(hidden_units // WIDE)],
        [slope_low, slope_high],
        stream_sem.at[1],
    )
    other_loads = [
        load(2, middle_save, middle),
        load(3, qkv_save, qkv),
        load(4, lse_save, lse),
        load(5, turns_save, turns),
    ]
    plane = [{axis: turn(lax.axis_index(axis), way)} for axis in ("x", "y") for way in (1, -1)]
    column = [{"tensor": turn(z, 1)}, {"tensor": turn(z, -1)}, {"core": 1 - core}]
    greet(plane + column)
    wire = Wire(send_sem, recv_sem)
    first_wire = Wire(token_send.at[0], token_recv.at[0])
    second_wire = Wire(token_send.at[1], token_recv.at[1])
    pump = Pump()

    def halves(grad, landing, result):
        return [
            reduce_rows(
                wire, grad, half, rows, *axes, *[buffer.at[half] for buffer in landing],
                result.at[half],
            )
            for half, axes in enumerate((("x", "y"), ("y", "x")))
        ]

    def sum_tokens(token_wire, result):
        return reduce_tokens(
            token_wire, summand, token_rows, pair, up1, down1, up2, down2, result
        )

    grad_load.wait()
    pump.add(*halves(grad_out, (out_up1, out_down1, out_up2, out_down2), out_result))
    cot_load.wait()
    pump.drive(
        middle_grad_pieces(
            token_matrix, out_tiles, slopes, grad_attended, lin_grad, 1 + hidden_units // WIDE
        ),
        0.6,
    )
    hidden_load = load(6, hidden_save, token_matrix)
    for copy in other_loads:
        copy.wait()
    out_rows = Stream(
        [out_save.at[pl.ds(index * WIDE, WIDE), :] for index in range(feature // WIDE)],
        [
            rows_low.at[:, pl.ds(0, out_save.shape[1])],
            rows_high.at[:, pl.ds(0, out_save.shape[1])],
        ],
        stream_sem.at[2],
    )
    pump.drive(back_pieces(middle, out_rows, summand, feature // WIDE), 0.6)
    first_tokens = sum_tokens(first_wire, first_sum)
    next(first_tokens)
    hidden_load.wait()
    up_at, qkv_at = pl.ds(qkv_width, hidden_units), pl.ds(0, qkv_width)
    pump.drive(outer_pieces(token_matrix, lin_grad, up_at, grad_in.at[:, up_at]), 0.5)
    next(first_tokens)
    pump.add(
        *halves(
            grad_in.at[:, up_at],
            (up_up1, up_down1, up_up2, up_down2),
            in_result.at[:, :, up_at],
        )
    )
    in_rows = Stream(
        [in_save.at[pl.ds(index * WIDE, WIDE), :] for index in range(feature // WIDE)],
        [rows_low, rows_high],
        stream_sem.at[3],
    )

    def with_tokens(work, tokens):
        for _ in work:
            next(tokens, None)
            yield

    pump.drive(
        with_tokens(
            attend_back_pieces(qkv, turns, lse, grad_attended, lin_grad, key_sum, value_sum),
            first_tokens,
        ),
        1.5,
    )
    pump.drive(outer_pieces(token_matrix, lin_grad, qkv_at, grad_in.at[:, qkv_at]), 0.5)
    pump.add(
        *halves(
            grad_in.at[:, qkv_at],
            (qkv_up1, qkv_down1, qkv_up2, qkv_down2),
            in_result.at[:, :, qkv_at],
        )
    )
    for _ in first_tokens:
        pass
    first_wire.drain()
    for peer in column:
        pl.semaphore_signal(credit, inc=1, device_id=peer, device_id_type=MESH)
    pump.drive(back_pieces(lin_grad, in_rows, summand, feature // WIDE), 0.75)
    pl.semaphore_wait(credit, len(column))
    second_tokens = sum_tokens(second_wire, second_sum)
    next(second_tokens)
    ones = jnp.ones((8, lin_grad.shape[0]), bf16)
    bias_sum[...] = matmul(ones, lin_grad[...])
    while pump.lines:
        pump.step()
        pump.step()
        next(second_tokens, None)
    for _ in second_tokens:
        pass
    second_wire.drain()
    wire.drain()


def backward_all(saved, rows):
    in_save, out_save, cot_save, hidden_save, qkv_save, lse_save, slope_save, middle_save = saved[:8]
    token_full, feature = cot_save.shape
    wide_in, wide_out = in_save.shape[1], out_save.shape[1]
    hidden_units = slope_save.shape[1]
    token_rows = token_full // (2 * RING)
    any_spec = pl.BlockSpec(memory_space=pl.ANY)
    vmem = pl.BlockSpec(memory_space=pltpu.VMEM)

    def landing(width):
        return [
            pltpu.VMEM((2, 5, rows // 2, width), bf16),
            pltpu.VMEM((2, 5, rows // 2, width), bf16),
            pltpu.VMEM((2, 5, rows, width), bf16),
            pltpu.VMEM((2, 5, rows, width), bf16),
        ]

    return pl.pallas_call(
        backward_kernel,
        out_shape=(
            jax.ShapeDtypeStruct((2, rows, wide_in), f32),
            jax.ShapeDtypeStruct((2, rows, wide_out), f32),
            jax.ShapeDtypeStruct((token_rows, feature), f32),
            jax.ShapeDtypeStruct((token_rows, feature), f32),
            jax.ShapeDtypeStruct((8, wide_in), f32),
        ),
        in_specs=[any_spec] * 10,
        out_specs=(vmem,) * 5,
        scratch_shapes=[
            pltpu.VMEM((token_full, feature), bf16),
            pltpu.VMEM((feature, WIDE), bf16),
            pltpu.VMEM((feature, WIDE), bf16),
            pltpu.VMEM((WIDE, wide_in), bf16),
            pltpu.VMEM((WIDE, wide_in), bf16),
            pltpu.VMEM((token_full, WIDE), f32),
            pltpu.VMEM((token_full, WIDE), f32),
            pltpu.VMEM((token_full, 3 * WIDE), bf16),
            pltpu.VMEM((token_full, LANES), f32),
            pltpu.VMEM((3, token_full, LANES), f32),
            pltpu.VMEM((token_full, wide_out), bf16),
            pltpu.VMEM((feature, wide_out), bf16),
            pltpu.VMEM((feature, wide_in), bf16),
            pltpu.VMEM((token_full, wide_in), bf16),
            pltpu.VMEM((token_full, WIDE), bf16),
            pltpu.VMEM((token_full, feature), bf16),
            pltpu.VMEM((GROUP_ROWS, LANES), f32),
            pltpu.VMEM((GROUP_ROWS, LANES), f32),
            *landing(wide_out),
            *landing(hidden_units),
            *landing(3 * WIDE),
            pltpu.VMEM((4, token_rows, feature), bf16),
            pltpu.VMEM((token_rows // 2, feature), bf16),
            pltpu.VMEM((token_rows // 2, feature), bf16),
            pltpu.VMEM((token_rows, feature), bf16),
            pltpu.VMEM((token_rows, feature), bf16),
            pltpu.SemaphoreType.DMA((REDUCES,)),
            pltpu.SemaphoreType.DMA((REDUCES,)),
            pltpu.SemaphoreType.DMA((2, TOKEN_REDUCES)),
            pltpu.SemaphoreType.DMA((2, TOKEN_REDUCES)),
            pltpu.SemaphoreType.DMA((7,)),
            pltpu.SemaphoreType.DMA((4, 2)),
            pltpu.SemaphoreType.REGULAR,
        ],
        compiler_params=pltpu.CompilerParams(
            collective_id=1, has_side_effects=True, vmem_limit_bytes=62 * 2**20
        ),
    )(*saved)


BR = 256
SWEEPS = 5
ortho_epsilon = 1e-07
coef_linear = 3.4445
coef_square = -4.775
coef_cubic = 2.0315


def split(value):
    high = value.astype(bf16)
    return high, (value - high.astype(f32)).astype(bf16)


def triple(left, right, contract):
    dims = (contract, ((), ()))
    (left_high, left_low), (right_high, right_low) = left, right

    def dot(a, b):
        return lax.dot_general(a, b, dims, preferred_element_type=f32)

    return dot(left_high, right_high) + (dot(left_high, right_low) + dot(left_low, right_high))


def sweep_block(current, high, low):
    columns = current.shape[1]
    chunk = 512

    def part(index):
        return pl.ds(pl.multiple_of(index * chunk, chunk), chunk)

    def square(index, total):
        values = current[:, part(index)]
        return total + values * values

    total = lax.fori_loop(0, columns // chunk, square, jnp.zeros((current.shape[0], chunk), f32))
    inverse = 1.0 / (jnp.sqrt(jnp.sum(total)) + ortho_epsilon)

    def scale(index, carry):
        at = part(index)
        values = current[:, at] * inverse
        current[:, at] = values
        high[:, at], low[:, at] = split(values)
        return carry

    lax.fori_loop(0, columns // chunk, scale, 0)

    def sweep(index, carry):
        rows = ((1,), (1,))
        whole = (high[...], low[...])
        gram = triple(whole, whole, rows)
        halves = split(gram)
        polynomial = coef_square * gram + coef_cubic * triple(halves, halves, ((1,), (0,)))
        factor = split(polynomial)

        def apply(index, carry):
            at = part(index)
            values = coef_linear * current[:, at] + triple(
                factor, (high[:, at], low[:, at]), ((1,), (0,))
            )
            current[:, at] = values
            high[:, at], low[:, at] = split(values)
            return carry

        lax.fori_loop(0, columns // chunk, apply, 0)
        return carry

    lax.fori_loop(0, SWEEPS, sweep, 0)


muon_decay = 0.95


def finish_tokens(tokens, cotangent, first_sum, second_sum, table, layer_out, input_grad, sums):
    step_rows = 16
    sums[...] = jnp.zeros_like(sums)
    gain = table[0:1, :]
    bias = table[5:6, :] + table[6:7, :]

    def fold(values):
        return values[0:8] + values[8:16]

    def body(step, carry):
        at = pl.ds(pl.multiple_of(step * step_rows, step_rows), step_rows)
        residual = tokens[at, :].astype(f32)
        center = residual - jnp.mean(residual, -1, keepdims=True)
        variance = jnp.mean(center * center, -1, keepdims=True)
        scale_inv = lax.rsqrt(variance + norm_epsilon)
        normed = center * scale_inv
        layer_out[at, :] = (residual + first_sum[at, :] + bias).astype(bf16)
        grad_hidden = second_sum[at, :]
        cot = cotangent[at, :].astype(f32)
        grad_hat = grad_hidden * gain
        input_grad[at, :] = cot + scale_inv * (
            grad_hat
            - jnp.mean(grad_hat, -1, keepdims=True)
            - normed * jnp.mean(grad_hat * normed, -1, keepdims=True)
        )
        sums[0:8, :] += fold(grad_hidden * normed)
        sums[8:16, :] += fold(grad_hidden)
        sums[16:24, :] += fold(cot)
        return carry

    lax.fori_loop(0, tokens.shape[0] // step_rows, body, 0)


def finish_kernel(
    in_result, out_result, in_moment, out_moment, in_cross, out_cross,
    tokens, cotangent, first_sum, second_sum, bias_sum, table,
    in_sum, out_sum, update, layer_out, input_grad, vector_sum,
    nesterov, land, back, whole, current, high, low, sums, vector,
    plane_slots, mine, column_slots,
    out_send, out_recv, back_send, back_recv, plane_send, plane_recv, column_send, column_recv,
    cross_send, cross_recv,
):
    core = lax.axis_index("core")
    z = lax.axis_index("tensor")
    chip = lax.axis_index("x") * RING + lax.axis_index("y")
    column = core * RING + z
    chips = RING * RING
    owners = nesterov.shape[1] // BR
    rows = nesterov.shape[0]
    half = rows // 2
    wide_in = in_result.shape[2]
    sibling = {"core": 1 - core}
    greet(plane_peers() + column_peers())

    def cross(number, source, target):
        remote = pltpu.make_async_remote_copy(
            src_ref=source,
            dst_ref=target,
            send_sem=cross_send.at[number],
            recv_sem=cross_recv.at[number],
            device_id=sibling,
            device_id_type=MESH,
        )
        remote.start()
        return remote

    def lanes(owner):
        return pl.ds(pl.multiple_of(owner * BR, BR), BR)

    def other(step):
        index = turn(chip, step, chips)
        return index, {"x": index // RING, "y": lax.rem(index, RING)}

    def outward(step):
        index, device = other(step)
        owner = jnp.minimum(index, owners - 1)
        return index, pltpu.make_async_remote_copy(
            src_ref=nesterov.at[:, lanes(owner)],
            dst_ref=land.at[chip],
            send_sem=out_send.at[step],
            recv_sem=out_recv.at[step],
            device_id=device,
            device_id_type=MESH,
        )

    def homeward(step):
        index, device = other(step)
        owner = jnp.minimum(chip, owners - 1)
        return index, pltpu.make_async_remote_copy(
            src_ref=back.at[index],
            dst_ref=whole.at[:, lanes(owner)],
            send_sem=back_send.at[step],
            recv_sem=back_recv.at[step],
            device_id=device,
            device_id_type=MESH,
        )

    def blend(result, moment, at):
        down = rows_at(at * half, half)
        for source, own, low in ((result[0], moment[0], 0), (result[1], moment[1], wide_in)):
            grad = source[at]
            values = grad + muon_decay * (muon_decay * own + grad)
            nesterov[down, low : low + grad.shape[1]] = values.astype(bf16)

    results = (in_result, out_result)
    blend(results, (in_moment[core], out_moment[core]), core)
    blend(results, (in_cross[...], out_cross[...]), 1 - core)
    for step in range(1, chips):
        index, remote = outward(step)
        pl.when(index < owners)(remote.start)

    @pl.when(chip < owners)
    def own_piece():
        land[chip] = nesterov[:, lanes(chip)]

    crosses = [
        cross(0, out_result.at[1 - core], out_sum.at[core]),
        cross(1, in_result.at[1 - core], in_sum.at[core]),
    ]
    finish_tokens(
        tokens, cotangent, first_sum, second_sum, table, layer_out, input_grad, sums
    )
    vector[...] = jnp.zeros_like(vector)
    vector[0:1, :] = jnp.sum(sums[0:8, :], 0, keepdims=True)
    vector[1:2, :] = jnp.sum(sums[8:16, :], 0, keepdims=True)
    cot_sum = jnp.sum(sums[16:24, :], 0, keepdims=True)
    vector[5:6, :] = cot_sum
    vector[6:7, :] = cot_sum
    part = z * 2 + core
    for index in range(3):
        vector[2 + index : 3 + index, lanes(part)] = bias_sum[0:1, index * BR : (index + 1) * BR]
    hidden_units = wide_in - 3 * BR
    vector[pl.ds(7 + z, 1), pl.ds(pl.multiple_of(core * hidden_units, BR), hidden_units)] = (
        bias_sum[0:1, 3 * BR :]
    )
    width = mine.shape[1]

    def strip(place):
        return pl.ds(pl.multiple_of(place * width, width), width)

    plane_copies = []
    for step in range(1, chips):
        index, device = other(step)
        remote = pltpu.make_async_remote_copy(
            src_ref=vector.at[:, strip(index)],
            dst_ref=plane_slots.at[chip],
            send_sem=plane_send.at[step],
            recv_sem=plane_recv.at[step],
            device_id=device,
            device_id_type=MESH,
        )
        remote.start()
        plane_copies.append(remote)
    plane_slots[chip] = vector[:, strip(chip)]
    in_sum[core] = in_result[core]
    out_sum[core] = out_result[core]
    for remote in plane_copies:
        remote.wait_recv()
    mine[...] = jnp.sum(plane_slots[...], axis=0)
    column_slots[column] = mine[...]
    column_copies = []
    for step, peer in enumerate(column_peers()):
        remote = pltpu.make_async_remote_copy(
            src_ref=mine,
            dst_ref=column_slots.at[column],
            send_sem=column_send.at[step],
            recv_sem=column_recv.at[step],
            device_id=peer,
            device_id_type=MESH,
        )
        remote.start()
        column_copies.append(remote)

    @pl.when(chip < owners)
    def own_block():
        for step in range(1, chips):
            outward(step)[1].wait_recv()
        for place in range(chips):
            current[:, place * rows : (place + 1) * rows] = land[place].astype(f32).T
        sweep_block(current, high, low)
        for place in range(chips):
            back[place] = current[:, place * rows : (place + 1) * rows].T.astype(bf16)
        for step in range(1, chips):
            homeward(step)[1].start()
        whole[:, lanes(chip)] = back[chip]

    for remote in column_copies:
        remote.wait_recv()
    vector_sum[...] = jnp.sum(column_slots[...], axis=0)
    for step in range(1, chips):
        index, remote = homeward(step)
        sender = turn(chip, -step, chips)
        pl.when(sender < owners)(remote.wait_recv)
    crosses.append(cross(2, whole.at[rows_at((1 - core) * half, half)], update.at[core]))
    update[core] = whole[rows_at(core * half, half), :]
    for step in range(1, chips):
        index, remote = outward(step)
        pl.when(index < owners)(remote.wait_send)

    @pl.when(chip < owners)
    def sent_back():
        for step in range(1, chips):
            homeward(step)[1].wait_send()

    for remote in plane_copies + column_copies:
        remote.wait_send()
    for remote in crosses:
        remote.wait()


def finish_all(
    in_result, out_result, in_moment, out_moment, in_cross, out_cross,
    tokens, cotangent, first_sum, second_sum, bias_sum, table,
):
    half, columns = in_result.shape[1], in_result.shape[2] + out_result.shape[2]
    rows = 2 * half
    token_rows, feature = tokens.shape
    chips = RING * RING
    small = (table.shape[0], feature // chips)
    vmem = pl.BlockSpec(memory_space=pltpu.VMEM)
    return pl.pallas_call(
        finish_kernel,
        out_shape=(
            jax.ShapeDtypeStruct(in_result.shape, f32),
            jax.ShapeDtypeStruct(out_result.shape, f32),
            jax.ShapeDtypeStruct((2, half, columns), bf16),
            jax.ShapeDtypeStruct((token_rows, feature), bf16),
            jax.ShapeDtypeStruct((token_rows, feature), f32),
            jax.ShapeDtypeStruct(small, f32),
        ),
        in_specs=[vmem] * 12,
        out_specs=(vmem,) * 6,
        scratch_shapes=[
            pltpu.VMEM((rows, columns), bf16),
            pltpu.VMEM((chips, rows, BR), bf16),
            pltpu.VMEM((chips, rows, BR), bf16),
            pltpu.VMEM((rows, columns), bf16),
            pltpu.VMEM((BR, chips * rows), f32),
            pltpu.VMEM((BR, chips * rows), bf16),
            pltpu.VMEM((BR, chips * rows), bf16),
            pltpu.VMEM((24, feature), f32),
            pltpu.VMEM(table.shape, f32),
            pltpu.VMEM((chips,) + small, f32),
            pltpu.VMEM(small, f32),
            pltpu.VMEM((2 * RING,) + small, f32),
            *[pltpu.SemaphoreType.DMA((chips,)) for _ in range(6)],
            *[pltpu.SemaphoreType.DMA((2 * RING,)) for _ in range(2)],
            pltpu.SemaphoreType.DMA((3,)),
            pltpu.SemaphoreType.DMA((3,)),
        ],
        compiler_params=pltpu.CompilerParams(
            collective_id=2, has_side_effects=True, vmem_limit_bytes=48 * 2**20
        ),
    )(
        in_result, out_result, in_moment, out_moment, in_cross, out_cross,
        tokens, cotangent, first_sum, second_sum, bias_sum, table,
    )


def fold_in(qkv, up):
    rows = qkv.shape[0]
    halves = qkv.shape[2] // 2
    qkv_part = qkv.reshape(rows, 3, 2, halves).transpose(2, 0, 1, 3).reshape(2, rows, 3 * halves)
    up_part = up.reshape(rows, 2, -1).transpose(1, 0, 2)
    return jnp.concatenate([qkv_part, up_part], -1)


def fold_out(out, down):
    width = out.shape[1]
    out_part = out.reshape(2, -1, width).transpose(0, 2, 1)
    down_part = down.reshape(2, -1, width).transpose(0, 2, 1)
    return jnp.concatenate([out_part, down_part], -1)


def unfold_in(both, qkv_shape, up_shape):
    rows = both.shape[1]
    halves = qkv_shape[2] // 2
    qkv = both[:, :, : 3 * halves].reshape(2, rows, 3, halves).transpose(1, 2, 0, 3)
    up = both[:, :, 3 * halves :].transpose(1, 0, 2)
    return qkv.reshape(qkv_shape), up.reshape(up_shape)


def unfold_out(both, out_shape, down_shape):
    out_rows = out_shape[0] // 2
    out = both[:, :, :out_rows].transpose(0, 2, 1).reshape(out_shape)
    down = both[:, :, out_rows:].transpose(0, 2, 1).reshape(down_shape)
    return out, down


def turn_tables(positions):
    half = ROT // 2
    count = positions.shape[0]
    inverse_freq = rotary_base ** (-2.0 * jnp.arange(half).astype(f32) / ROT)
    angles = positions.astype(f32)[:, None] * inverse_freq[None, :]
    cosine, sine = jnp.cos(angles), jnp.sin(angles)
    rest = jnp.ones((count, HEAD - ROT), f32)
    one_cosine = jnp.concatenate([cosine, cosine, rest], 1)
    one_sine = jnp.concatenate([-sine, sine, 0.0 * rest], 1)
    start = (jnp.arange(count) - positions).astype(f32)[:, None]
    return jnp.stack(
        [
            jnp.concatenate([one_cosine, one_cosine], 1),
            jnp.concatenate([one_sine, one_sine], 1),
            jnp.broadcast_to(start, (count, LANES)),
        ]
    )


def local(
    inputs,
    cotangent,
    positions,
    qkv_weight,
    out_weight,
    up_weight,
    down_weight,
    qkv_moment,
    out_moment,
    up_moment,
    down_moment,
    vectors,
    vector_first,
    vector_second,
):
    vector_rows, vector_width = vectors.shape
    column = lax.axis_index("core") * RING + lax.axis_index("tensor")
    vector_mine = lax.dynamic_update_slice(
        jnp.zeros((16, 2 * RING * vector_width), f32), vectors, (0, column * vector_width)
    )
    in_moment = fold_in(qkv_moment, up_moment)
    both_moment = fold_out(out_moment, down_moment)
    *saved, in_cross, out_cross, table = forward_all(
        fold_in(qkv_weight, up_weight).astype(bf16),
        fold_out(out_weight, down_weight).astype(bf16),
        inputs,
        cotangent,
        turn_tables(positions),
        vector_mine,
        in_moment,
        both_moment,
    )
    in_result, out_result, first_sum, second_sum, bias_sum = backward_all(
        saved, in_moment.shape[1]
    )
    in_sum, out_sum, update, layer_out, input_grad, vector_sum = finish_all(
        in_result, out_result, in_moment, both_moment, in_cross, out_cross,
        inputs, cotangent, first_sum, second_sum, bias_sum, table,
    )
    vector_grad = lax.dynamic_slice(
        vector_sum, (0, column * vector_width), (vector_rows, vector_width)
    )
    first_new = first_decay * vector_first + (1.0 - first_decay) * vector_grad
    second_new = second_decay * vector_second + (1.0 - second_decay) * vector_grad * vector_grad
    first_hat = first_new / (1.0 - first_decay**STEP)
    second_hat = second_new / (1.0 - second_decay**STEP)
    vectors_new = vectors - adam_rate * first_hat / (jnp.sqrt(second_hat) + adam_epsilon)

    reduced_qkv, reduced_up = unfold_in(in_sum, qkv_weight.shape, up_weight.shape)
    reduced_out, reduced_down = unfold_out(out_sum, out_weight.shape, down_weight.shape)
    qkv_moment_new = muon_decay * qkv_moment + reduced_qkv
    out_moment_new = muon_decay * out_moment + reduced_out
    up_moment_new = muon_decay * up_moment + reduced_up
    down_moment_new = muon_decay * down_moment + reduced_down
    wide_in = in_sum.shape[2]
    update = update.astype(f32)
    update_qkv, update_up = unfold_in(update[:, :, :wide_in], qkv_weight.shape, up_weight.shape)
    update_out, update_down = unfold_out(
        update[:, :, wide_in:], out_weight.shape, down_weight.shape
    )
    qkv_new = qkv_weight * (1.0 - decay_factor * rate_qkv) - rate_qkv * update_qkv
    out_new = out_weight * (1.0 - decay_factor * rate_out) - rate_out * update_out
    up_new = up_weight * (1.0 - decay_factor * rate_up) - rate_up * update_up
    down_new = down_weight * (1.0 - decay_factor * rate_down) - rate_down * update_down
    return (
        layer_out,
        input_grad,
        qkv_new,
        out_new,
        up_new,
        down_new,
        qkv_moment_new,
        out_moment_new,
        up_moment_new,
        down_moment_new,
        first_new,
        second_new,
        vectors_new,
    )


def solution(mesh):
    wide = Mesh(mesh.devices.reshape(4, 4, 2, 4), ALL)
    in_specs = (
        P(ALL, None),
        P(ALL, None),
        P(DP),
        P(DP, None, "tensor"),
        P("tensor", DP),
        P(DP, "tensor"),
        P("tensor", DP),
        P(DP, None, "tensor"),
        P("tensor", DP),
        P(DP, "tensor"),
        P("tensor", DP),
        P(None, ALL),
        P(None, ALL),
        P(None, ALL),
    )
    out_specs = (
        P(ALL, None),
        P(ALL, None),
        P(DP, None, "tensor"),
        P("tensor", DP),
        P(DP, "tensor"),
        P("tensor", DP),
        P(DP, None, "tensor"),
        P("tensor", DP),
        P(DP, "tensor"),
        P("tensor", DP),
        P(None, ALL),
        P(None, ALL),
        P(None, ALL),
    )
    return jax.shard_map(local, mesh=wide, in_specs=in_specs, out_specs=out_specs, check_vma=False)
```

```python
import jax
import jax.numpy as jnp
from jax import lax
from jax.experimental import pallas as pl
from jax.experimental.pallas import tpu as pltpu
from jax.sharding import Mesh
from jax.sharding import PartitionSpec as P

STEP = 10

rotary_base = 10000.0
adam_rate = 0.2
first_decay = 0.9
second_decay = 0.95
adam_epsilon = 1e-08

f32 = jnp.float32
bf16 = jnp.bfloat16
DP = ("x", "y", "core")
ALL = ("x", "y", "core", "tensor")

MESH = pl.DeviceIdType.MESH
RING = 4
WIRES = 180


def turn(index, step, size=RING):
    return lax.rem(index + (step % size), size)


class Wire:
    def __init__(self, send_sem, recv_sem):
        self.send_sem, self.recv_sem, self.sent = send_sem, recv_sem, []

    def copy(self, src, dst, device):
        number = len(self.sent)
        remote = pltpu.make_async_remote_copy(
            src_ref=src,
            dst_ref=dst,
            send_sem=self.send_sem.at[number],
            recv_sem=self.recv_sem.at[number],
            device_id=device,
            device_id_type=MESH,
        )
        remote.start()
        self.sent.append(remote)
        return remote

    def drain(self):
        for remote in self.sent:
            remote.wait_send()


def rows_at(start, size):
    return pl.ds(pl.multiple_of(start, 16), size)


def greet(peers):
    barrier = pltpu.get_barrier_semaphore()
    for peer in peers:
        pl.semaphore_signal(barrier, inc=1, device_id=peer, device_id_type=MESH)
    pl.semaphore_wait(barrier, len(peers))


def plane_peers():
    place = lax.axis_index("x") * RING + lax.axis_index("y")
    peers = []
    for step in range(1, RING * RING):
        other = turn(place, step, RING * RING)
        peers.append({"x": other // RING, "y": lax.rem(other, RING)})
    return peers


def column_peers():
    place = lax.axis_index("core") * RING + lax.axis_index("tensor")
    peers = []
    for step in range(1, 2 * RING):
        other = turn(place, step, 2 * RING)
        peers.append({"core": other // RING, "tensor": lax.rem(other, RING)})
    return peers


def spread_rows(wire, table, half, rows, first, second, own=None):
    here_first, here_second = lax.axis_index(first), lax.axis_index(second)
    quarter = rows // 2

    def block(step_first, step_second, low, size):
        index = {first: turn(here_first, step_first), second: turn(here_second, step_second)}
        chip = index["x"] * RING + index["y"]
        return table.at[rows_at(chip * 2 * rows + half * rows + low, size)]

    def send(step_first, step_second, low, size, axis, direction):
        ref = src = block(step_first, step_second, low, size)
        if own is not None and step_first == 0 and step_second == 0:
            src = own
        here = here_first if axis == first else here_second
        return wire.copy(src, ref, {axis: turn(here, direction)})

    def both(step_first):
        return [send(step_first, 0, 0, rows, second, way) for way in (1, -1)]

    ahead = send(0, 0, 0, rows, first, 1)
    back = send(0, 0, 0, rows, first, -1)
    lines = {0: both(0)}
    yield
    ahead.wait_recv()
    tail_ahead = send(-1, 0, 0, quarter, first, 1)
    lines[-1] = both(-1)
    yield
    back.wait_recv()
    tail_back = send(1, 0, quarter, quarter, first, -1)
    lines[1] = both(1)
    tails = []

    def relay(step_first):
        from_back, from_ahead = lines[step_first]
        from_back.wait_recv()
        tails.append(send(step_first, -1, 0, quarter, second, 1))
        from_ahead.wait_recv()
        tails.append(send(step_first, 1, quarter, quarter, second, -1))

    yield
    relay(0)
    yield
    tail_ahead.wait_recv()
    tail_back.wait_recv()
    lines[2] = both(2)
    yield
    relay(-1)
    yield
    relay(1)
    yield
    relay(2)
    yield
    for tail in tails:
        tail.wait_recv()


def spread_tokens(wire, table, rows, own=None):
    here, core = lax.axis_index("tensor"), lax.axis_index("core")
    half = rows // 2

    def send(step, low, size, device):
        ref = table.at[rows_at((core * RING + turn(here, step)) * rows + low, size)]
        src = own if own is not None and step == 0 else ref
        return wire.copy(src, ref, device)

    sibling = {"core": 1 - core}
    ahead = send(0, 0, rows, {"tensor": turn(here, 1)})
    back = send(0, 0, rows, {"tensor": turn(here, -1)})
    across = [send(0, 0, rows, sibling)]
    yield
    ahead.wait_recv()
    tail_ahead = send(-1, 0, half, {"tensor": turn(here, 1)})
    across.append(send(-1, 0, rows, sibling))
    yield
    back.wait_recv()
    tail_back = send(1, half, half, {"tensor": turn(here, -1)})
    across.append(send(1, 0, rows, sibling))
    yield
    tail_ahead.wait_recv()
    tail_back.wait_recv()
    across.append(send(2, 0, rows, sibling))
    yield
    for remote in across:
        remote.wait_recv()


TILE = 16


def add_rows(target, sources):
    rows = target.shape[0]
    step_rows = min(rows, 2 * TILE)

    def body(step, carry):
        at = pl.ds(pl.multiple_of(step * step_rows, step_rows), step_rows)
        if len(sources) == 2 and target.dtype == bf16:
            target[at, :] = sources[0][at, :] + sources[1][at, :]
            return carry
        total = sources[0][at, :].astype(f32)
        for source in sources[1:]:
            total = total + source[at, :].astype(f32)
        target[at, :] = total.astype(target.dtype)
        return carry

    if rows == step_rows:
        body(0, 0)
    else:
        lax.fori_loop(0, rows // step_rows, body, 0)


def reduce_rows(wire, grad, half, rows, first, second, up1, down1, up2, down2, result):
    here_first, here_second = lax.axis_index(first), lax.axis_index(second)
    part = rows // 2
    top, bottom = pl.ds(0, part), pl.ds(part, part)

    def block(step_first, step_second, low, size):
        index = {first: turn(here_first, step_first), second: turn(here_second, step_second)}
        chip = index["x"] * RING + index["y"]
        return grad.at[rows_at(chip * 2 * rows + half * rows + low, size)]

    ahead, back = {first: turn(here_first, 1)}, {first: turn(here_first, -1)}
    order = (2, 1, -1, 0)
    far, near = {}, {}
    for slot, ss in enumerate(order):
        far[ss] = (
            wire.copy(block(2, ss, 0, part), up1.at[slot], ahead),
            wire.copy(block(2, ss, part, part), down1.at[slot], back),
        )
        near[ss] = [
            wire.copy(block(1, ss, part, part), up2.at[slot, bottom], ahead),
            wire.copy(block(-1, ss, 0, part), down2.at[slot, top], back),
        ]
    yield
    for slot, ss in enumerate(order):
        far[ss][0].wait_recv()
        add_rows(up1.at[slot], [up1.at[slot], block(1, ss, 0, part)])
        near[ss].append(wire.copy(up1.at[slot], up2.at[slot, top], ahead))
        far[ss][1].wait_recv()
        add_rows(down1.at[slot], [down1.at[slot], block(-1, ss, part, part)])
        near[ss].append(wire.copy(down1.at[slot], down2.at[slot, bottom], back))
        yield
    ahead, back = {second: turn(here_second, 1)}, {second: turn(here_second, -1)}
    last = []
    for slot, ss in enumerate(order):
        for remote in near[ss]:
            remote.wait_recv()
        if ss == 0:
            break
        add_rows(up2.at[slot], [up2.at[slot], down2.at[slot], block(0, ss, 0, rows)])
        total = up2.at[slot]
        if ss == 2:
            across = (
                wire.copy(total.at[top], up1.at[4], ahead),
                wire.copy(total.at[bottom], down1.at[4], back),
            )
        elif ss == 1:
            last.append(wire.copy(total.at[bottom], up2.at[4, bottom], ahead))
            across[0].wait_recv()
            add_rows(up1.at[4], [up1.at[4], total.at[top]])
            last.append(wire.copy(up1.at[4], up2.at[4, top], ahead))
        else:
            last.append(wire.copy(total.at[top], down2.at[4, top], back))
            across[1].wait_recv()
            add_rows(down1.at[4], [down1.at[4], total.at[bottom]])
            last.append(wire.copy(down1.at[4], down2.at[4, bottom], back))
        yield
    for remote in last:
        remote.wait_recv()
    add_rows(result, [up2.at[3], down2.at[3], block(0, 0, 0, rows), up2.at[4], down2.at[4]])


def reduce_tokens(wire, partial, rows, pair, up1, down1, up2, down2, result):
    here, core = lax.axis_index("tensor"), lax.axis_index("core")
    part = rows // 2
    top, bottom = pl.ds(0, part), pl.ds(part, part)
    ahead, back = {"tensor": turn(here, 1)}, {"tensor": turn(here, -1)}

    def block(side, step):
        return partial.at[rows_at((side * RING + turn(here, step)) * rows, rows)]

    order = (2, 1, -1, 0)
    across = [
        wire.copy(block(1 - core, step), pair.at[slot], {"core": 1 - core})
        for slot, step in enumerate(order)
    ]
    yield
    near = []
    for slot, step in enumerate(order):
        across[slot].wait_recv()
        if step == 0:
            break
        add_rows(pair.at[slot], [pair.at[slot], block(core, step)])
        total = pair.at[slot]
        if step == 2:
            far = (
                wire.copy(total.at[top], up1, ahead),
                wire.copy(total.at[bottom], down1, back),
            )
        elif step == 1:
            near.append(wire.copy(total.at[bottom], up2.at[bottom], ahead))
        else:
            near.append(wire.copy(total.at[top], down2.at[top], back))
        yield
    far[0].wait_recv()
    add_rows(up1, [up1, pair.at[1, top]])
    near.append(wire.copy(up1, up2.at[top], ahead))
    far[1].wait_recv()
    add_rows(down1, [down1, pair.at[2, bottom]])
    near.append(wire.copy(down1, down2.at[bottom], back))
    yield
    for remote in near:
        remote.wait_recv()
    add_rows(result, [pair.at[3], block(core, 0), up2, down2])


HEAD = 64
ROT = 32
norm_epsilon = 1e-05
masked_score = -1e30
GROUP_ROWS = 512
LANES = 128
WIDE = 256
gelu_scale = 0.7978845608028654
gelu_cubic = 0.044715
scale_value = HEAD ** (-0.5)
ROWS_CROSS = ((1,), (1,))
COLUMNS_CROSS = ((0,), (0,))


def matmul(left, right, contract=((1,), (0,))):
    return lax.dot_general(left, right, (contract, ((), ())), preferred_element_type=f32)


def lane_ids(rows, width):
    return lax.broadcasted_iota(jnp.int32, (rows, width), 1)


def swap_halves(values):
    width = values.shape[1]
    lane = lax.rem(lane_ids(*values.shape), HEAD)
    half = ROT // 2
    return jnp.where(
        lane < half, pltpu.roll(values, width - half, 1), pltpu.roll(values, half, 1)
    )


def turned(values, cosine, sine):
    return values * cosine + swap_halves(values) * sine


def head_lanes(values, side):
    keep = lane_ids(*values.shape) // HEAD == side
    return jnp.where(keep, values, jnp.zeros_like(values))


def visible_block(start, row_low, row_count, column_count):
    rows = lax.broadcasted_iota(jnp.int32, (row_count, column_count), 0) + row_low
    columns = lax.broadcasted_iota(jnp.int32, (row_count, column_count), 1)
    return (columns <= rows) & (columns.astype(f32) >= start)


def normalize(rows, gain, shift):
    residual = rows.astype(f32)
    center = residual - jnp.mean(residual, -1, keepdims=True)
    variance = jnp.mean(center * center, -1, keepdims=True)
    return center * lax.rsqrt(variance + norm_epsilon) * gain + shift


def norm_pieces(tokens, hidden, table, pieces):
    count = tokens.shape[0] // pieces
    step_rows = 32
    for piece in range(pieces):

        def body(step, carry):
            at = pl.ds(pl.multiple_of(piece * count + step * step_rows, step_rows), step_rows)
            hidden[at, :] = normalize(tokens[at, :], table[0:1, :], table[1:2, :]).astype(bf16)
            return carry

        lax.fori_loop(0, count // step_rows, body, 0)
        yield


def project_pieces(hidden, in_full, table, cosine, sine, qkv, middle, gelu_slope):
    part = lax.axis_index("tensor") * 2 + lax.axis_index("core")
    rows = hidden.shape[0]
    half = rows // 2
    for index in range(3):
        at = pl.ds(index * WIDE, WIDE)
        bias = table[2 + index : 3 + index, pl.ds(pl.multiple_of(part * WIDE, WIDE), WIDE)]

        def body(step, carry):
            down = pl.ds(pl.multiple_of(step * half, half), half)
            values = matmul(hidden[down, :], in_full[:, at]) + bias
            if index < 2:
                wide = [jnp.concatenate([t[down, :]] * 2, 1) for t in (cosine, sine)]
                values = turned(values, *wide)
            qkv[down, at] = values.astype(bf16)
            return carry

        lax.fori_loop(0, 2, body, 0)
        yield
    hidden_units = in_full.shape[1] - 3 * WIDE
    for index in range(hidden_units // WIDE):
        at = pl.ds(3 * WIDE + index * WIDE, WIDE)
        to = pl.ds(WIDE + index * WIDE, WIDE)
        slope_at = pl.ds(index * WIDE, WIDE)
        core, row = lax.axis_index("core"), 7 + lax.axis_index("tensor")
        low = pl.multiple_of(core * hidden_units + index * WIDE, WIDE)
        bias = table[pl.ds(row, 1), pl.ds(low, WIDE)]

        def body(step, carry):
            down = pl.ds(pl.multiple_of(step * half, half), half)
            unit = matmul(hidden[down, :], in_full[:, at]) + bias
            square = unit * unit
            curve = jnp.tanh(gelu_scale * (unit + gelu_cubic * unit * square))
            rise = 0.5 * (1.0 + curve)
            middle[down, to] = (unit * rise).astype(bf16)
            bend = 0.5 * gelu_scale * unit * (1.0 + 3.0 * gelu_cubic * square)
            gelu_slope[down, slope_at] = rise + bend * (1.0 - curve * curve)
            return carry

        lax.fori_loop(0, 2, body, 0)
        yield


def attend_pieces(qkv, start, middle, lse):
    for group in range(2):
        base = group * GROUP_ROWS
        for pair in range(2):
            for tile in range(2):
                low, count = tile * WIDE, (tile + 1) * WIDE
                down = pl.ds(base + low, WIDE)
                keys_at = pl.ds(base, count)
                queries = qkv[down, pl.ds(pair * LANES, LANES)]
                keys = qkv[keys_at, pl.ds(WIDE + pair * LANES, LANES)]
                values = qkv[keys_at, pl.ds(2 * WIDE + pair * LANES, LANES)]
                visible = visible_block(start[down, 0:1], low, WIDE, count)
                outs = []
                for side in range(2):
                    scores = matmul(head_lanes(queries, side), keys, ROWS_CROSS) * scale_value
                    scores = jnp.where(visible, scores, masked_score)
                    top = jnp.max(scores, -1, keepdims=True)
                    raised = jnp.exp(scores - top)
                    total = jnp.sum(raised, -1, keepdims=True)
                    soft = (raised / total).astype(bf16)
                    outs.append(matmul(soft, values))
                    head = pair * 2 + side
                    here = lane_ids(WIDE, LANES) == head
                    lse[down, :] = jnp.where(here, top + jnp.log(total), lse[down, :])
                first = lane_ids(WIDE, LANES) < HEAD
                middle[down, pl.ds(pair * LANES, LANES)] = jnp.where(
                    first, outs[0], outs[1]
                ).astype(bf16)
                yield


def outer_pieces(left, right, at, target):
    for step in range(left.shape[1] // WIDE):
        down = pl.ds(step * WIDE, WIDE)
        target[down, :] = matmul(left[:, down], right[:, at], COLUMNS_CROSS).astype(bf16)
        yield


def in_turn(processes):
    waiting = list(processes)
    while waiting:
        for process in list(waiting):
            if next(process, waiting) is waiting:
                waiting.remove(process)
            yield


def weave(work, wire_steps, per_piece):
    debt = 0.0
    for _ in work:
        debt += per_piece
        while debt >= 1.0:
            debt -= 1.0
            next(wire_steps, None)


def chained(*parts):
    for part in parts:
        for item in part:
            yield item


def fold_rows(at, qkv, out, up, down):
    def part(size):
        return pl.ds(pl.multiple_of(at * size, size), size)

    heads, units = part(qkv.shape[2] // 2), part(up.shape[1] // 2)
    inward = [qkv[index, :, heads] for index in range(3)] + [up[:, units]]
    return inward, [out[:, part(out.shape[1] // 2)], down[:, part(down.shape[1] // 2)]]


def forward_kernel(
    qkv_weight, out_weight, up_weight, down_weight, tokens, cotangent, turns, vector,
    qkv_moment, out_moment, up_moment, down_moment,
    in_save, out_save, cot_save, hidden_save, qkv_save, lse_save, slope_save, middle_save,
    grad_save, turns_save, qkv_cross, out_cross, up_cross, down_cross, table,
    in_low, out_low, in_full, out_full, tokens_full, cot_full, hidden, qkv, lse, slope, middle, grad_out,
    turns_full, slots, mine, send_sem, recv_sem, local_sem, save_sem,
):
    core = lax.axis_index("core")
    chip = lax.axis_index("x") * RING + lax.axis_index("y")
    column = core * RING + lax.axis_index("tensor")
    rows = in_low.shape[1]
    token_rows = tokens.shape[0]
    sibling = {"core": 1 - core}
    for half in range(2):
        inward, outward = fold_rows(half, qkv_weight, out_weight, up_weight, down_weight)
        for low, blocks in ((in_low, inward), (out_low, outward)):
            column_at = 0
            for block in blocks:
                low[half, :, column_at : column_at + block.shape[1]] = block.astype(bf16)
                column_at += block.shape[1]
    greet(plane_peers() + column_peers())
    wire = Wire(send_sem, recv_sem)
    saves = []

    def save(src, dst):
        copy = pltpu.make_async_copy(src, dst, save_sem.at[len(saves)])
        copy.start()
        saves.append(copy)

    own_rows = rows_at(chip * 2 * rows + core * rows, rows)
    own_tokens = rows_at(column * token_rows, token_rows)
    own_turns = rows_at(core * GROUP_ROWS, GROUP_ROWS)
    wide_in = in_low.shape[2]
    parts = [
        (in_low.at[:, :, pl.ds(0, 3 * WIDE)], in_full.at[:, pl.ds(0, 3 * WIDE)]),
        (
            in_low.at[:, :, pl.ds(3 * WIDE, wide_in - 3 * WIDE)],
            in_full.at[:, pl.ds(3 * WIDE, wide_in - 3 * WIDE)],
        ),
        (out_low, out_full),
    ]
    crosses = [wire.copy(low.at[1 - core], full.at[own_rows], sibling) for low, full in parts[:1]]
    pairs = [(low.at[core], full.at[own_rows]) for low, full in parts] + [
        (tokens, tokens_full.at[own_tokens]),
        (cotangent, cot_full.at[own_tokens]),
        (turns, turns_full.at[:, own_turns]),
        (vector, slots.at[column]),
    ]
    here = [
        pltpu.make_async_copy(src, dst, local_sem.at[number])
        for number, (src, dst) in enumerate(pairs)
    ]
    for copy in here:
        copy.start()
    token_steps = spread_tokens(wire, tokens_full, token_rows, tokens)
    next(token_steps)
    crosses += [wire.copy(low.at[1 - core], full.at[own_rows], sibling) for low, full in parts[1:]]
    vector_in = [wire.copy(vector, slots.at[column], peer) for peer in column_peers()]
    spreads = []

    def begin(number):
        here[number].wait()
        crosses[number].wait_recv()
        full = parts[number][1]
        spreads.append(
            [
                spread_rows(wire, full, 0, rows, "x", "y"),
                spread_rows(wire, full, 1, rows, "y", "x"),
            ]
        )
        for process in spreads[-1]:
            next(process)

    begin(0)
    cross_turns = wire.copy(turns, turns_full.at[:, own_turns], sibling)
    theirs = 1 - core

    def their_part(size):
        return pl.ds(pl.multiple_of(theirs * size, size), size)

    cross_moments = [
        wire.copy(qkv_moment.at[:, :, their_part(qkv_cross.shape[2])], qkv_cross, sibling)
    ] + [
        wire.copy(moment.at[:, their_part(target.shape[1])], target, sibling)
        for moment, target in (
            (out_moment, out_cross), (up_moment, up_cross), (down_moment, down_cross),
        )
    ]
    cot_steps = spread_tokens(wire, cot_full, token_rows, cotangent)
    done = set()

    def script():
        first = in_turn(spreads[0])
        for _ in range(4):
            next(first)
            yield
        begin(1)
        yield
        second = in_turn(spreads[1])
        for copy in here[3:]:
            copy.wait()
        for remote in vector_in:
            remote.wait_recv()
        mine[...] = jnp.sum(slots[...], axis=0)
        width = mine.shape[1]
        lanes = pl.ds(pl.multiple_of(chip * width, width), width)
        vector_out = [wire.copy(mine, table.at[:, lanes], peer) for peer in plane_peers()]
        table[:, lanes] = mine[...]
        for _ in range(4):
            next(first)
            yield
        next(token_steps)
        yield
        next(token_steps)
        next(cot_steps)
        yield
        for _ in range(4):
            next(first)
            yield
        for _ in range(4):
            next(first)
            yield
            next(second)
            yield
        for _ in first:
            pass
        done.add("first")
        for _ in token_steps:
            yield
        for remote in vector_out:
            remote.wait_recv()
        cross_turns.wait_recv()
        done.add("tokens")
        for _ in range(2):
            next(second)
            yield
        begin(2)
        yield
        third = in_turn(spreads[2])
        for _ in range(2):
            next(second)
            yield
        next(cot_steps)
        yield
        next(cot_steps)
        yield
        for _ in range(4):
            next(second)
            yield
        for _ in range(4):
            next(second)
            yield
            next(third)
            yield
        for _ in second:
            pass
        done.add("second")
        for _ in cot_steps:
            yield
        done.add("cotangent")
        for _ in third:
            yield

    steps = script()

    def until(mark):
        while mark not in done:
            next(steps)

    until("tokens")
    save(turns_full, turns_save)
    weave(norm_pieces(tokens_full, hidden, table, 8), steps, 1.5)
    save(hidden, hidden_save)
    lse[...] = jnp.zeros_like(lse)
    until("first")
    project = project_pieces(
        hidden, in_full, table, turns_full.at[0], turns_full.at[1], qkv, middle, slope
    )
    for _ in range(3):
        next(project)
        next(steps, None)
    weave(attend_pieces(qkv, turns_full.at[2], middle, lse), steps, 0.75)
    until("second")
    save(in_full, in_save)
    for _ in range(wide_in // WIDE - 3):
        next(project)
        next(steps, None)
        next(steps, None)
    until("cotangent")
    save(cot_full, cot_save)
    for source, target in ((qkv, qkv_save), (lse, lse_save), (slope, slope_save)):
        save(source, target)
    weave(outer_pieces(cot_full, middle, slice(None), grad_out), steps, 0.75)
    save(middle, middle_save)
    save(grad_out, grad_save)
    for _ in steps:
        pass
    save(out_full, out_save)
    for remote in cross_moments:
        remote.wait_recv()
    wire.drain()
    for copy in saves:
        copy.wait()


def forward_all(weights, tokens, cotangent, turns, vector, moments):
    qkv, out, up, down = weights
    rows = qkv.shape[1]
    full = 2 * RING * RING * rows
    token_full, feature = 2 * RING * tokens.shape[0], tokens.shape[1]
    wide_in = (3 * qkv.shape[2] + up.shape[1]) // 2
    wide_out = (out.shape[1] + down.shape[1]) // 2
    hidden_units = wide_out - WIDE
    any_spec = pl.BlockSpec(memory_space=pl.ANY)
    vmem = pl.BlockSpec(memory_space=pltpu.VMEM)
    kept = [
        ((full, wide_in), bf16),
        ((full, wide_out), bf16),
        ((token_full, feature), bf16),
        ((token_full, feature), bf16),
        ((token_full, 3 * WIDE), bf16),
        ((token_full, LANES), f32),
        ((token_full, hidden_units), f32),
        ((token_full, wide_out), bf16),
        ((full, wide_out), bf16),
        ((3, 2 * GROUP_ROWS, LANES), f32),
    ]
    crossed = [(m.shape[:-1] + (m.shape[-1] // 2,), f32) for m in moments]
    scratch = [((2, rows, wide_in), bf16), ((2, rows, wide_out), bf16)]
    scratch += kept[:2] + [((token_full, feature), bf16)] + kept[2:]
    table = (vector.shape[0], RING * RING * vector.shape[1])
    return pl.pallas_call(
        forward_kernel,
        out_shape=tuple(jax.ShapeDtypeStruct(*entry) for entry in kept + crossed)
        + (jax.ShapeDtypeStruct(table, f32),),
        in_specs=[vmem] * 8 + [any_spec] * 4,
        out_specs=(any_spec,) * (len(kept) + len(crossed)) + (vmem,),
        scratch_shapes=[pltpu.VMEM(*entry) for entry in scratch]
        + [
            pltpu.VMEM((2 * RING,) + vector.shape, f32),
            pltpu.VMEM(vector.shape, f32),
            pltpu.SemaphoreType.DMA((WIRES,)),
            pltpu.SemaphoreType.DMA((WIRES,)),
            pltpu.SemaphoreType.DMA((7,)),
            pltpu.SemaphoreType.DMA((len(kept),)),
        ],
        compiler_params=pltpu.CompilerParams(
            collective_id=0, has_side_effects=True, vmem_limit_bytes=60 * 2**20
        ),
    )(*weights, tokens, cotangent, turns, vector, *moments)


REDUCES = 180
TOKEN_REDUCES = 10
RATES = (0.75, 0.6, 0.5, 1.0, 0.4, 1.25)


class Pump:
    def __init__(self):
        self.lines = []

    def add(self, *lines):
        for line in lines:
            next(line)
        self.lines += lines

    def step(self):
        if self.lines:
            line = self.lines.pop(0)
            if next(line, self) is not self:
                self.lines.append(line)

    def drive(self, work, per_piece):
        debt = 0.0
        for _ in work:
            debt += per_piece
            while debt >= 1.0:
                debt -= 1.0
                self.step()


class Stream:
    def __init__(self, tiles, slots, sems):
        self.tiles, self.slots, self.sems, self.copies = tiles, slots, sems, []
        for _ in range(2):
            self.fetch()

    def fetch(self):
        number = len(self.copies)
        if number < len(self.tiles):
            copy = pltpu.make_async_copy(
                self.tiles[number], self.slots[number % 2], self.sems.at[number % 2]
            )
            copy.start()
            self.copies.append(copy)

    def take(self, number):
        self.copies[number].wait()
        return self.slots[number % 2]


def middle_grad_pieces(cot, weights, slopes, grad_attended, lin_grad, count):
    for index in range(count):
        tile = weights.at[:, pl.ds(index * WIDE, WIDE)]
        if index == 0:
            grad_attended[...] = matmul(cot[...], tile[...]).astype(bf16)
        else:
            slope = slopes.take(index - 1)
            half = cot.shape[0] // 2

            def body(step, carry):
                down = pl.ds(pl.multiple_of(step * half, half), half)
                values = matmul(cot[down, :], tile[...]) * slope[down, :]
                lin_grad[down, pl.ds(3 * WIDE + (index - 1) * WIDE, WIDE)] = values.astype(bf16)
                return carry

            lax.fori_loop(0, 2, body, 0)
            slopes.fetch()
        yield


def back_pieces(left, weights, target, count):
    streamed = isinstance(weights, Stream)
    for index in range(count):
        at = pl.ds(index * WIDE, WIDE)
        tile = weights.take(index) if streamed else weights.at[at, :]
        target[:, at] = matmul(left[...], tile[...], ROWS_CROSS).astype(bf16)
        if streamed:
            weights.fetch()
        yield


def attend_back_pieces(qkv, turns, lse, grad_attended, lin_grad, key_sum, value_sum):
    cosine, sine, start = turns.at[0], turns.at[1], turns.at[2]

    def unturned(values, at):
        values = values * scale_value
        return (values * cosine[at, :] - swap_halves(values) * sine[at, :]).astype(bf16)

    for group in range(2):
        base = group * GROUP_ROWS
        for pair in range(2):
            lanes = pair * LANES
            for tile in (1, 0):
                low, count = tile * WIDE, (tile + 1) * WIDE
                down = pl.ds(base + low, WIDE)
                keys_at = pl.ds(base, count)
                queries = qkv[down, pl.ds(lanes, LANES)]
                keys = qkv[keys_at, pl.ds(WIDE + lanes, LANES)]
                values = qkv[keys_at, pl.ds(2 * WIDE + lanes, LANES)]
                grads = grad_attended[down, pl.ds(lanes, LANES)]
                visible = visible_block(start[down, 0:1], low, WIDE, count)
                query_grad = jnp.zeros((WIDE, LANES), f32)
                key_grad = jnp.zeros((count, LANES), f32)
                value_grad = jnp.zeros((count, LANES), f32)
                for side in range(2):
                    query, grad = head_lanes(queries, side), head_lanes(grads, side)
                    scores = matmul(query, keys, ROWS_CROSS) * scale_value
                    scores = jnp.where(visible, scores, masked_score)
                    head = pair * 2 + side
                    soft = jnp.exp(scores - lse[down, head : head + 1])
                    grad_soft = matmul(grad, values, ROWS_CROSS)
                    delta = jnp.sum(soft * grad_soft, -1, keepdims=True)
                    grad_scores = (soft * (grad_soft - delta)).astype(bf16)
                    query_grad += matmul(grad_scores, head_lanes(keys, side))
                    key_grad += matmul(grad_scores, query, COLUMNS_CROSS)
                    value_grad += matmul(soft.astype(bf16), grad, COLUMNS_CROSS)
                lin_grad[down, pl.ds(lanes, LANES)] = unturned(query_grad, down)
                if tile == 1:
                    key_sum[...] = key_grad
                    value_sum[...] = value_grad
                else:
                    key_sum[0:WIDE, :] += key_grad
                    value_sum[0:WIDE, :] += value_grad
                yield
            all_rows = pl.ds(base, GROUP_ROWS)
            lin_grad[all_rows, pl.ds(WIDE + lanes, LANES)] = unturned(key_sum[...], all_rows)
            lin_grad[all_rows, pl.ds(2 * WIDE + lanes, LANES)] = value_sum[...].astype(bf16)


def backward_kernel(
    in_save, out_save, cot_save, hidden_save, qkv_save, lse_save, slope_save, middle_save,
    grad_save, turns_save,
    in_result, out_result, first_sum, second_sum, bias_sum,
    token_matrix, out_full, rows_low, rows_high, slope_low, slope_high,
    qkv, lse, turns, middle, grad_out, grad_in, lin_grad, grad_attended, summand,
    key_sum, value_sum,
    out_up1, out_down1, out_up2, out_down2,
    up_up1, up_down1, up_up2, up_down2,
    qkv_up1, qkv_down1, qkv_up2, qkv_down2,
    pair, up1, down1, up2, down2,
    send_sem, recv_sem, token_send, token_recv, load_sem, stream_sem, credit,
):
    core = lax.axis_index("core")
    z = lax.axis_index("tensor")
    rows = in_result.shape[1]
    token_rows = first_sum.shape[0]
    hidden_units = slope_save.shape[1]
    qkv_width = qkv.shape[1]
    feature = token_matrix.shape[1]

    def load(number, source, target):
        copy = pltpu.make_async_copy(source, target, load_sem.at[number])
        copy.start()
        return copy

    grad_load = load(0, grad_save, grad_out)
    plane = [{axis: turn(lax.axis_index(axis), way)} for axis in ("x", "y") for way in (1, -1)]
    column = [{"tensor": turn(z, 1)}, {"tensor": turn(z, -1)}, {"core": 1 - core}]
    greet(plane + column)
    cot_load = load(1, cot_save, token_matrix)
    out_load = load(7, out_save, out_full)
    slopes = Stream(
        [slope_save.at[:, pl.ds(index * WIDE, WIDE)] for index in range(hidden_units // WIDE)],
        [slope_low, slope_high],
        stream_sem.at[0],
    )
    other_loads = [
        load(2, middle_save, middle),
        load(3, qkv_save, qkv),
        load(4, lse_save, lse),
        load(5, turns_save, turns),
    ]
    wire = Wire(send_sem, recv_sem)
    first_wire = Wire(token_send.at[0], token_recv.at[0])
    second_wires = [Wire(token_send.at[1], token_recv.at[1]), Wire(token_send.at[2], token_recv.at[2])]
    pump = Pump()

    def halves(grad, landing, result):
        return [
            reduce_rows(
                wire, grad, half, rows, *axes, *[buffer.at[half] for buffer in landing],
                result.at[half],
            )
            for half, axes in enumerate((("x", "y"), ("y", "x")))
        ]

    def sum_tokens(token_wire, result):
        return reduce_tokens(
            token_wire, summand, token_rows, pair, up1, down1, up2, down2, result
        )

    grad_load.wait()
    pump.add(*halves(grad_out, (out_up1, out_down1, out_up2, out_down2), out_result))
    cot_load.wait()
    out_load.wait()
    pump.drive(
        middle_grad_pieces(
            token_matrix, out_full, slopes, grad_attended, lin_grad, 1 + hidden_units // WIDE
        ),
        RATES[0],
    )
    hidden_load = load(6, hidden_save, token_matrix)
    for copy in other_loads:
        copy.wait()
    in_rows = Stream(
        [in_save.at[pl.ds(index * WIDE, WIDE), :] for index in range(feature // WIDE)],
        [rows_low, rows_high],
        stream_sem.at[1],
    )
    pump.drive(back_pieces(middle, out_full, summand, feature // WIDE), RATES[1])
    first_tokens = sum_tokens(first_wire, first_sum)
    next(first_tokens)
    hidden_load.wait()
    up_at, qkv_at = pl.ds(qkv_width, hidden_units), pl.ds(0, qkv_width)
    pump.drive(outer_pieces(token_matrix, lin_grad, up_at, grad_in.at[:, up_at]), RATES[2])
    pump.add(
        *halves(
            grad_in.at[:, up_at],
            (up_up1, up_down1, up_up2, up_down2),
            in_result.at[:, :, up_at],
        )
    )
    next(first_tokens)
    work = attend_back_pieces(qkv, turns, lse, grad_attended, lin_grad, key_sum, value_sum)
    debt = 0.0
    for number, _ in enumerate(work):
        debt += RATES[3]
        while debt >= 1.0:
            debt -= 1.0
            pump.step()
        if number in (0, 1, 5):
            next(first_tokens)
    pump.drive(outer_pieces(token_matrix, lin_grad, qkv_at, grad_in.at[:, qkv_at]), RATES[4])
    pump.add(
        *halves(
            grad_in.at[:, qkv_at],
            (qkv_up1, qkv_down1, qkv_up2, qkv_down2),
            in_result.at[:, :, qkv_at],
        )
    )
    pump.step()
    pump.step()
    for _ in first_tokens:
        pass
    first_wire.drain()
    for peer in column:
        pl.semaphore_signal(credit, inc=1, device_id=peer, device_id_type=MESH)
    span = feature // 2
    seconds = [
        reduce_tokens(
            token_wire, summand.at[:, at], token_rows, pair.at[:, :, at],
            up1.at[:, at], down1.at[:, at], up2.at[:, at], down2.at[:, at], second_sum.at[:, at],
        )
        for token_wire, at in zip(second_wires, (pl.ds(0, span), pl.ds(span, span)))
    ]
    debt = 0.0
    for number, _ in enumerate(back_pieces(lin_grad, in_rows, summand, feature // WIDE)):
        debt += RATES[5]
        while debt >= 1.0:
            debt -= 1.0
            pump.step()
        if number == feature // WIDE // 2 - 1:
            pl.semaphore_wait(credit, len(column))
            next(seconds[0])
        elif number > feature // WIDE // 2:
            next(seconds[0])
    next(seconds[1])
    ones = jnp.ones((8, lin_grad.shape[0]), bf16)
    bias_sum[...] = matmul(ones, lin_grad[...])
    pump.step()
    for _ in range(3):
        next(seconds[1])
        pump.step()
        pump.step()
    rest = in_turn(seconds)
    while pump.lines:
        pump.step()
        pump.step()
        next(rest, None)
    for _ in rest:
        pass
    for token_wire in second_wires:
        token_wire.drain()
    wire.drain()


def backward_all(saved, rows):
    in_save, out_save, cot_save, hidden_save, qkv_save, lse_save, slope_save, middle_save = saved[:8]
    token_full, feature = cot_save.shape
    wide_in, wide_out = in_save.shape[1], out_save.shape[1]
    hidden_units = slope_save.shape[1]
    token_rows = token_full // (2 * RING)
    any_spec = pl.BlockSpec(memory_space=pl.ANY)
    vmem = pl.BlockSpec(memory_space=pltpu.VMEM)

    def landing(width):
        return [
            pltpu.VMEM((2, 5, rows // 2, width), bf16),
            pltpu.VMEM((2, 5, rows // 2, width), bf16),
            pltpu.VMEM((2, 5, rows, width), bf16),
            pltpu.VMEM((2, 5, rows, width), bf16),
        ]

    return pl.pallas_call(
        backward_kernel,
        out_shape=(
            jax.ShapeDtypeStruct((2, rows, wide_in), f32),
            jax.ShapeDtypeStruct((2, rows, wide_out), f32),
            jax.ShapeDtypeStruct((token_rows, feature), f32),
            jax.ShapeDtypeStruct((token_rows, feature), f32),
            jax.ShapeDtypeStruct((8, wide_in), f32),
        ),
        in_specs=[any_spec] * 10,
        out_specs=(vmem,) * 5,
        scratch_shapes=[
            pltpu.VMEM((token_full, feature), bf16),
            pltpu.VMEM((feature, wide_out), bf16),
            pltpu.VMEM((WIDE, wide_in), bf16),
            pltpu.VMEM((WIDE, wide_in), bf16),
            pltpu.VMEM((token_full, WIDE), f32),
            pltpu.VMEM((token_full, WIDE), f32),
            pltpu.VMEM((token_full, 3 * WIDE), bf16),
            pltpu.VMEM((token_full, LANES), f32),
            pltpu.VMEM((3, token_full, LANES), f32),
            pltpu.VMEM((token_full, wide_out), bf16),
            pltpu.VMEM((feature, wide_out), bf16),
            pltpu.VMEM((feature, wide_in), bf16),
            pltpu.VMEM((token_full, wide_in), bf16),
            pltpu.VMEM((token_full, WIDE), bf16),
            pltpu.VMEM((token_full, feature), bf16),
            pltpu.VMEM((GROUP_ROWS, LANES), f32),
            pltpu.VMEM((GROUP_ROWS, LANES), f32),
            *landing(wide_out),
            *landing(hidden_units),
            *landing(3 * WIDE),
            pltpu.VMEM((4, token_rows, feature), bf16),
            pltpu.VMEM((token_rows // 2, feature), bf16),
            pltpu.VMEM((token_rows // 2, feature), bf16),
            pltpu.VMEM((token_rows, feature), bf16),
            pltpu.VMEM((token_rows, feature), bf16),
            pltpu.SemaphoreType.DMA((REDUCES,)),
            pltpu.SemaphoreType.DMA((REDUCES,)),
            pltpu.SemaphoreType.DMA((3, TOKEN_REDUCES)),
            pltpu.SemaphoreType.DMA((3, TOKEN_REDUCES)),
            pltpu.SemaphoreType.DMA((8,)),
            pltpu.SemaphoreType.DMA((2, 2)),
            pltpu.SemaphoreType.REGULAR,
        ],
        compiler_params=pltpu.CompilerParams(
            collective_id=1, has_side_effects=True, vmem_limit_bytes=62 * 2**20
        ),
    )(*saved)


BR = 256
SWEEPS = 5
ortho_epsilon = 1e-07
coef_linear = 3.4445
coef_square = -4.775
coef_cubic = 2.0315


def split(value):
    high = value.astype(bf16)
    return high, (value - high.astype(f32)).astype(bf16)


def triple(left, right, contract):
    dims = (contract, ((), ()))
    (left_high, left_low), (right_high, right_low) = left, right

    def dot(a, b):
        return lax.dot_general(a, b, dims, preferred_element_type=f32)

    return dot(left_high, right_high) + (dot(left_high, right_low) + dot(left_low, right_high))


def sweep_block(current, high, low):
    columns = current.shape[1]
    chunk = 512

    def part(index):
        return pl.ds(pl.multiple_of(index * chunk, chunk), chunk)

    def square(index, total):
        values = current[:, part(index)]
        return total + values * values

    total = lax.fori_loop(0, columns // chunk, square, jnp.zeros((current.shape[0], chunk), f32))
    inverse = 1.0 / (jnp.sqrt(jnp.sum(total)) + ortho_epsilon)

    def scale(index, carry):
        at = part(index)
        values = current[:, at] * inverse
        current[:, at] = values
        high[:, at], low[:, at] = split(values)
        return carry

    lax.fori_loop(0, columns // chunk, scale, 0)

    def sweep(index, carry):
        rows = ((1,), (1,))
        whole = (high[...], low[...])
        gram = triple(whole, whole, rows)
        halves = split(gram)
        polynomial = coef_square * gram + coef_cubic * triple(halves, halves, ((1,), (0,)))
        factor = split(polynomial)

        def apply(index, carry):
            at = part(index)
            values = coef_linear * current[:, at] + triple(
                factor, (high[:, at], low[:, at]), ((1,), (0,))
            )
            current[:, at] = values
            high[:, at], low[:, at] = split(values)
            return carry

        lax.fori_loop(0, columns // chunk, apply, 0)
        return carry

    lax.fori_loop(0, SWEEPS, sweep, 0)


muon_decay = 0.95
decay_factor = 0.01
rate_qkv = 1.0
rate_out = 4.0
rate_up = 0.8
rate_down = 0.4


def finish_tokens(tokens, cotangent, first_sum, second_sum, table, layer_out, input_grad, sums):
    step_rows = 16
    sums[...] = jnp.zeros_like(sums)
    gain = table[0:1, :]
    bias = table[5:6, :] + table[6:7, :]

    def fold(values):
        return values[0:8] + values[8:16]

    def body(step, carry):
        at = pl.ds(pl.multiple_of(step * step_rows, step_rows), step_rows)
        residual = tokens[at, :].astype(f32)
        center = residual - jnp.mean(residual, -1, keepdims=True)
        variance = jnp.mean(center * center, -1, keepdims=True)
        scale_inv = lax.rsqrt(variance + norm_epsilon)
        normed = center * scale_inv
        layer_out[at, :] = (residual + first_sum[at, :] + bias).astype(bf16)
        grad_hidden = second_sum[at, :]
        cot = cotangent[at, :].astype(f32)
        grad_hat = grad_hidden * gain
        input_grad[at, :] = cot + scale_inv * (
            grad_hat
            - jnp.mean(grad_hat, -1, keepdims=True)
            - normed * jnp.mean(grad_hat * normed, -1, keepdims=True)
        )
        sums[0:8, :] += fold(grad_hidden * normed)
        sums[8:16, :] += fold(grad_hidden)
        sums[16:24, :] += fold(cot)
        return carry

    lax.fori_loop(0, tokens.shape[0] // step_rows, body, 0)


def finish_kernel(
    in_save, out_save, first_save, second_save,
    qkv_moment, out_moment, up_moment, down_moment, qkv_cross, out_cross, up_cross, down_cross,
    tokens, cotangent, bias_sum, table,
    in_sum, out_sum, update, layer_out, input_grad, vector_sum,
    in_result, out_result, first_sum, second_sum, nesterov, land, back, whole, current, high, low, sums, vector,
    plane_slots, mine, column_slots,
    out_send, out_recv, back_send, back_recv, plane_send, plane_recv, column_send, column_recv,
    cross_send, cross_recv, load_sem,
):
    loads = [
        pltpu.make_async_copy(source, target, load_sem.at[number])
        for number, (source, target) in enumerate(
            (
                (in_save, in_result),
                (out_save, out_result),
                (first_save, first_sum),
                (second_save, second_sum),
            )
        )
    ]
    for copy in loads:
        copy.start()
    core = lax.axis_index("core")
    z = lax.axis_index("tensor")
    chip = lax.axis_index("x") * RING + lax.axis_index("y")
    column = core * RING + z
    chips = RING * RING
    owners = nesterov.shape[1] // BR
    rows = nesterov.shape[0]
    half = rows // 2
    wide_in = in_result.shape[2]
    sibling = {"core": 1 - core}
    greet(plane_peers() + column_peers())

    def cross(number, source, target):
        remote = pltpu.make_async_remote_copy(
            src_ref=source,
            dst_ref=target,
            send_sem=cross_send.at[number],
            recv_sem=cross_recv.at[number],
            device_id=sibling,
            device_id_type=MESH,
        )
        remote.start()
        return remote

    def lanes(owner):
        return pl.ds(pl.multiple_of(owner * BR, BR), BR)

    def other(step):
        index = turn(chip, step, chips)
        return index, {"x": index // RING, "y": lax.rem(index, RING)}

    def outward(step):
        index, device = other(step)
        owner = jnp.minimum(index, owners - 1)
        return index, pltpu.make_async_remote_copy(
            src_ref=nesterov.at[:, lanes(owner)],
            dst_ref=land.at[chip],
            send_sem=out_send.at[step],
            recv_sem=out_recv.at[step],
            device_id=device,
            device_id_type=MESH,
        )

    def homeward(step):
        index, device = other(step)
        owner = jnp.minimum(chip, owners - 1)
        return index, pltpu.make_async_remote_copy(
            src_ref=back.at[index],
            dst_ref=whole.at[:, lanes(owner)],
            send_sem=back_send.at[step],
            recv_sem=back_recv.at[step],
            device_id=device,
            device_id_type=MESH,
        )

    def blend(at, moments):
        down = rows_at(at * half, half)
        column_at = 0
        for result, blocks in zip((in_result, out_result), moments):
            result_at = 0
            for own in blocks:
                width = own.shape[1]
                grad = result[at, :, result_at : result_at + width]
                values = grad + muon_decay * (muon_decay * own + grad)
                nesterov[down, column_at : column_at + width] = values.astype(bf16)
                column_at += width
                result_at += width

    loads[0].wait()
    loads[1].wait()
    blend(core, fold_rows(core, qkv_moment, out_moment, up_moment, down_moment))
    blend(
        1 - core,
        (
            [qkv_cross[0], qkv_cross[1], qkv_cross[2], up_cross[...]],
            [out_cross[...], down_cross[...]],
        ),
    )
    for step in range(1, chips):
        index, remote = outward(step)
        pl.when(index < owners)(remote.start)

    @pl.when(chip < owners)
    def own_piece():
        land[chip] = nesterov[:, lanes(chip)]

    crosses = [
        cross(0, out_result.at[1 - core], out_sum.at[core]),
        cross(1, in_result.at[1 - core], in_sum.at[core]),
    ]
    loads[2].wait()
    loads[3].wait()
    finish_tokens(
        tokens, cotangent, first_sum, second_sum, table, layer_out, input_grad, sums
    )
    vector[...] = jnp.zeros_like(vector)
    vector[0:1, :] = jnp.sum(sums[0:8, :], 0, keepdims=True)
    vector[1:2, :] = jnp.sum(sums[8:16, :], 0, keepdims=True)
    cot_sum = jnp.sum(sums[16:24, :], 0, keepdims=True)
    vector[5:6, :] = cot_sum
    vector[6:7, :] = cot_sum
    part = z * 2 + core
    for index in range(3):
        vector[2 + index : 3 + index, lanes(part)] = bias_sum[0:1, index * BR : (index + 1) * BR]
    hidden_units = wide_in - 3 * BR
    vector[pl.ds(7 + z, 1), pl.ds(pl.multiple_of(core * hidden_units, BR), hidden_units)] = (
        bias_sum[0:1, 3 * BR :]
    )
    width = mine.shape[1]

    def strip(place):
        return pl.ds(pl.multiple_of(place * width, width), width)

    plane_copies = []
    for step in range(1, chips):
        index, device = other(step)
        remote = pltpu.make_async_remote_copy(
            src_ref=vector.at[:, strip(index)],
            dst_ref=plane_slots.at[chip],
            send_sem=plane_send.at[step],
            recv_sem=plane_recv.at[step],
            device_id=device,
            device_id_type=MESH,
        )
        remote.start()
        plane_copies.append(remote)
    plane_slots[chip] = vector[:, strip(chip)]
    in_sum[core] = in_result[core]
    out_sum[core] = out_result[core]
    for remote in plane_copies:
        remote.wait_recv()
    mine[...] = jnp.sum(plane_slots[...], axis=0)
    column_slots[column] = mine[...]
    column_copies = []
    for step, peer in enumerate(column_peers()):
        remote = pltpu.make_async_remote_copy(
            src_ref=mine,
            dst_ref=column_slots.at[column],
            send_sem=column_send.at[step],
            recv_sem=column_recv.at[step],
            device_id=peer,
            device_id_type=MESH,
        )
        remote.start()
        column_copies.append(remote)

    @pl.when(chip < owners)
    def own_block():
        for step in range(1, chips):
            outward(step)[1].wait_recv()
        for place in range(chips):
            current[:, place * rows : (place + 1) * rows] = land[place].astype(f32).T
        sweep_block(current, high, low)
        for place in range(chips):
            back[place] = current[:, place * rows : (place + 1) * rows].T.astype(bf16)
        for step in range(1, chips):
            homeward(step)[1].start()
        whole[:, lanes(chip)] = back[chip]

    for remote in column_copies:
        remote.wait_recv()
    vector_sum[...] = jnp.sum(column_slots[...], axis=0)
    for step in range(1, chips):
        index, remote = homeward(step)
        sender = turn(chip, -step, chips)
        pl.when(sender < owners)(remote.wait_recv)
    crosses.append(cross(2, whole.at[rows_at((1 - core) * half, half)], update.at[core]))
    update[core] = whole[rows_at(core * half, half), :]
    for step in range(1, chips):
        index, remote = outward(step)
        pl.when(index < owners)(remote.wait_send)

    @pl.when(chip < owners)
    def sent_back():
        for step in range(1, chips):
            homeward(step)[1].wait_send()

    for remote in plane_copies + column_copies:
        remote.wait_send()
    for remote in crosses:
        remote.wait()


def finish_all(results, moments, crosses, tokens, cotangent, bias_sum, table):
    half = results[0].shape[1]
    columns = results[0].shape[2] + results[1].shape[2]
    rows = 2 * half
    token_rows, feature = tokens.shape
    chips = RING * RING
    small = (table.shape[0], feature // chips)
    vmem = pl.BlockSpec(memory_space=pltpu.VMEM)
    any_spec = pl.BlockSpec(memory_space=pl.ANY)
    return pl.pallas_call(
        finish_kernel,
        out_shape=(
            jax.ShapeDtypeStruct(results[0].shape, f32),
            jax.ShapeDtypeStruct(results[1].shape, f32),
            jax.ShapeDtypeStruct((2, half, columns), bf16),
            jax.ShapeDtypeStruct((token_rows, feature), bf16),
            jax.ShapeDtypeStruct((token_rows, feature), f32),
            jax.ShapeDtypeStruct(small, f32),
        ),
        in_specs=[any_spec] * 4 + [vmem] * 12,
        out_specs=(vmem,) * 6,
        scratch_shapes=[pltpu.VMEM(result.shape, f32) for result in results]
        + [
            pltpu.VMEM((rows, columns), bf16),
            pltpu.VMEM((chips, rows, BR), bf16),
            pltpu.VMEM((chips, rows, BR), bf16),
            pltpu.VMEM((rows, columns), bf16),
            pltpu.VMEM((BR, chips * rows), f32),
            pltpu.VMEM((BR, chips * rows), bf16),
            pltpu.VMEM((BR, chips * rows), bf16),
            pltpu.VMEM((24, feature), f32),
            pltpu.VMEM(table.shape, f32),
            pltpu.VMEM((chips,) + small, f32),
            pltpu.VMEM(small, f32),
            pltpu.VMEM((2 * RING,) + small, f32),
            *[pltpu.SemaphoreType.DMA((chips,)) for _ in range(6)],
            *[pltpu.SemaphoreType.DMA((2 * RING,)) for _ in range(2)],
            pltpu.SemaphoreType.DMA((3,)),
            pltpu.SemaphoreType.DMA((3,)),
            pltpu.SemaphoreType.DMA((4,)),
        ],
        compiler_params=pltpu.CompilerParams(
            collective_id=2, has_side_effects=True, vmem_limit_bytes=56 * 2**20
        ),
    )(*results, *moments, *crosses, tokens, cotangent, bias_sum, table)


def apply_kernel(
    in_save, out_save, update_save,
    qkv_weight, out_weight, up_weight, down_weight,
    qkv_moment, out_moment, up_moment, down_moment,
    qkv_new, out_new, up_new, down_new,
    qkv_moment_new, out_moment_new, up_moment_new, down_moment_new,
    in_sum, out_sum, update, load_sem,
):
    loads = [
        pltpu.make_async_copy(source, target, load_sem.at[number])
        for number, (source, target) in enumerate(
            ((in_save, in_sum), (out_save, out_sum), (update_save, update))
        )
    ]
    for copy in loads:
        copy.start()
    for copy in loads:
        copy.wait()
    heads, units = qkv_weight.shape[2] // 2, up_weight.shape[1] // 2
    outs, downs = out_weight.shape[1] // 2, down_weight.shape[1] // 2
    wide_in = in_sum.shape[2]

    def step(at, weight, moment, new, moment_new, grad, orthogonal, rate):
        moment_new[at] = muon_decay * moment[at] + grad
        new[at] = weight[at] * (1.0 - decay_factor * rate) - rate * orthogonal.astype(f32)

    for half in range(2):

        def lanes(size):
            return (slice(None), slice(half * size, (half + 1) * size))

        for index in range(3):
            from_at = slice(index * heads, (index + 1) * heads)
            step(
                (index,) + lanes(heads), qkv_weight, qkv_moment, qkv_new, qkv_moment_new,
                in_sum[half, :, from_at], update[half, :, from_at], rate_qkv,
            )
        step(
            lanes(units), up_weight, up_moment, up_new, up_moment_new,
            in_sum[half, :, 3 * heads :], update[half, :, 3 * heads : wide_in], rate_up,
        )
        step(
            lanes(outs), out_weight, out_moment, out_new, out_moment_new,
            out_sum[half, :, :outs], update[half, :, wide_in : wide_in + outs], rate_out,
        )
        step(
            lanes(downs), down_weight, down_moment, down_new, down_moment_new,
            out_sum[half, :, outs:], update[half, :, wide_in + outs :], rate_down,
        )


def apply_all(in_sum, out_sum, update, weights, moments):
    vmem = pl.BlockSpec(memory_space=pltpu.VMEM)
    any_spec = pl.BlockSpec(memory_space=pl.ANY)
    return pl.pallas_call(
        apply_kernel,
        out_shape=tuple(jax.ShapeDtypeStruct(w.shape, f32) for w in (*weights, *moments)),
        in_specs=[any_spec] * 3 + [vmem] * 8,
        out_specs=(vmem,) * 8,
        scratch_shapes=[
            pltpu.VMEM(in_sum.shape, f32),
            pltpu.VMEM(out_sum.shape, f32),
            pltpu.VMEM(update.shape, bf16),
            pltpu.SemaphoreType.DMA((3,)),
        ],
        compiler_params=pltpu.CompilerParams(vmem_limit_bytes=48 * 2**20),
    )(in_sum, out_sum, update, *weights, *moments)


def turn_tables(positions):
    half = ROT // 2
    count = positions.shape[0]
    lane = jnp.arange(LANES)[None, None, :]
    kind = jnp.arange(3)[:, None, None]
    place = positions.astype(f32)[None, :, None]
    within = lane % HEAD
    angle = place * rotary_base ** (-2.0 * (lane % half).astype(f32) / ROT)
    sign = jnp.where(within < half, -1.0, 1.0)
    turns = within < ROT
    start = jnp.arange(count).astype(f32)[None, :, None] - place
    cosine = jnp.where(turns, jnp.cos(angle), 1.0)
    sine = jnp.where(turns, jnp.sin(angle) * sign, 0.0)
    return jnp.where(kind == 0, cosine, jnp.where(kind == 1, sine, start))


def local(
    inputs,
    cotangent,
    positions,
    qkv_weight,
    out_weight,
    up_weight,
    down_weight,
    qkv_moment,
    out_moment,
    up_moment,
    down_moment,
    vectors,
    vector_first,
    vector_second,
):
    vector_rows, vector_width = vectors.shape
    column = lax.axis_index("core") * RING + lax.axis_index("tensor")
    spread = jnp.tile(jnp.pad(vectors, ((0, 16 - vector_rows), (0, 0))), (1, 2 * RING))
    mine = jnp.arange(spread.shape[1])[None, :] // vector_width == column
    vector_mine = jnp.where(mine, spread, 0.0)
    rows = qkv_weight.shape[0]

    def turned_over(qkv, out, up, down):
        return (qkv.transpose(1, 0, 2), out.T, up, down.T)

    weights = turned_over(qkv_weight, out_weight, up_weight, down_weight)
    moments = turned_over(qkv_moment, out_moment, up_moment, down_moment)
    kept = forward_all(weights, inputs, cotangent, turn_tables(positions), vector_mine, moments)
    saved, crosses, table = kept[:10], kept[10:14], kept[14]
    *results, bias_sum = backward_all(saved, rows)
    in_sum, out_sum, update, layer_out, input_grad, vector_sum = finish_all(
        results, moments, crosses, inputs, cotangent, bias_sum, table
    )
    vector_grad = lax.dynamic_slice(
        vector_sum, (0, column * vector_width), (vector_rows, vector_width)
    )
    first_new = first_decay * vector_first + (1.0 - first_decay) * vector_grad
    second_new = second_decay * vector_second + (1.0 - second_decay) * vector_grad * vector_grad
    first_hat = first_new / (1.0 - first_decay**STEP)
    second_hat = second_new / (1.0 - second_decay**STEP)
    vectors_new = vectors - adam_rate * first_hat / (jnp.sqrt(second_hat) + adam_epsilon)

    applied = apply_all(in_sum, out_sum, update, weights, moments)
    qkv_new, out_new, up_new, down_new = turned_over(*applied[:4])
    qkv_moment_new, out_moment_new, up_moment_new, down_moment_new = turned_over(*applied[4:])
    return (
        layer_out,
        input_grad,
        qkv_new,
        out_new,
        up_new,
        down_new,
        qkv_moment_new,
        out_moment_new,
        up_moment_new,
        down_moment_new,
        first_new,
        second_new,
        vectors_new,
    )


def solution(mesh):
    wide = Mesh(mesh.devices.reshape(4, 4, 2, 4), ALL)
    in_specs = (
        P(ALL, None),
        P(ALL, None),
        P(DP),
        P(DP, None, "tensor"),
        P("tensor", DP),
        P(DP, "tensor"),
        P("tensor", DP),
        P(DP, None, "tensor"),
        P("tensor", DP),
        P(DP, "tensor"),
        P("tensor", DP),
        P(None, ALL),
        P(None, ALL),
        P(None, ALL),
    )
    out_specs = (
        P(ALL, None),
        P(ALL, None),
        P(DP, None, "tensor"),
        P("tensor", DP),
        P(DP, "tensor"),
        P("tensor", DP),
        P(DP, None, "tensor"),
        P("tensor", DP),
        P(DP, "tensor"),
        P("tensor", DP),
        P(None, ALL),
        P(None, ALL),
        P(None, ALL),
    )
    return jax.shard_map(local, mesh=wide, in_specs=in_specs, out_specs=out_specs, check_vma=False)
```

```python
import itertools

import jax
import jax.numpy as jnp
from jax import lax
from jax.experimental import pallas as pl
from jax.experimental.pallas import tpu as pltpu
from jax.sharding import Mesh
from jax.sharding import PartitionSpec as P

STEP = 10

rotary_base = 10000.0
adam_rate = 0.2
first_decay = 0.9
second_decay = 0.95
adam_epsilon = 1e-08

f32 = jnp.float32
bf16 = jnp.bfloat16
DP = ("x", "y", "core")
ALL = ("x", "y", "core", "tensor")

MESH = pl.DeviceIdType.MESH
RING = 4
WIRES = 180


def turn(index, step, size=RING):
    return lax.rem(index + (step % size), size)


class Wire:
    def __init__(self, send_sem, recv_sem):
        self.send_sem, self.recv_sem, self.sent = send_sem, recv_sem, []

    def copy(self, src, dst, device):
        number = len(self.sent)
        remote = pltpu.make_async_remote_copy(
            src_ref=src,
            dst_ref=dst,
            send_sem=self.send_sem.at[number],
            recv_sem=self.recv_sem.at[number],
            device_id=device,
            device_id_type=MESH,
        )
        remote.start()
        self.sent.append(remote)
        return remote

    def drain(self):
        for remote in self.sent:
            remote.wait_send()


def rows_at(start, size):
    return pl.ds(pl.multiple_of(start, 16), size)


def greet(peers):
    barrier = pltpu.get_barrier_semaphore()
    for peer in peers:
        pl.semaphore_signal(barrier, inc=1, device_id=peer, device_id_type=MESH)
    pl.semaphore_wait(barrier, len(peers))


def plane_peers():
    place = lax.axis_index("x") * RING + lax.axis_index("y")
    peers = []
    for step in range(1, RING * RING):
        other = turn(place, step, RING * RING)
        peers.append({"x": other // RING, "y": lax.rem(other, RING)})
    return peers


def column_peers():
    place = lax.axis_index("core") * RING + lax.axis_index("tensor")
    peers = []
    for step in range(1, 2 * RING):
        other = turn(place, step, 2 * RING)
        peers.append({"core": other // RING, "tensor": lax.rem(other, RING)})
    return peers


def spread_rows(wire, table, half, rows, first, second, own=None):
    here_first, here_second = lax.axis_index(first), lax.axis_index(second)
    quarter = rows // 2

    def block(step_first, step_second, low, size):
        index = {first: turn(here_first, step_first), second: turn(here_second, step_second)}
        chip = index["x"] * RING + index["y"]
        return table.at[rows_at(chip * 2 * rows + half * rows + low, size)]

    def send(step_first, step_second, low, size, axis, direction):
        ref = src = block(step_first, step_second, low, size)
        if own is not None and step_first == 0 and step_second == 0:
            src = own
        here = here_first if axis == first else here_second
        return wire.copy(src, ref, {axis: turn(here, direction)})

    def both(step_first):
        return [send(step_first, 0, 0, rows, second, way) for way in (1, -1)]

    ahead = send(0, 0, 0, rows, first, 1)
    back = send(0, 0, 0, rows, first, -1)
    lines = {0: both(0)}
    yield
    ahead.wait_recv()
    tail_ahead = send(-1, 0, 0, quarter, first, 1)
    lines[-1] = both(-1)
    yield
    back.wait_recv()
    tail_back = send(1, 0, quarter, quarter, first, -1)
    lines[1] = both(1)
    tails = []

    def relay(step_first):
        from_back, from_ahead = lines[step_first]
        from_back.wait_recv()
        tails.append(send(step_first, -1, 0, quarter, second, 1))
        from_ahead.wait_recv()
        tails.append(send(step_first, 1, quarter, quarter, second, -1))

    yield
    relay(0)
    yield
    tail_ahead.wait_recv()
    tail_back.wait_recv()
    lines[2] = both(2)
    yield
    relay(-1)
    yield
    relay(1)
    yield
    relay(2)
    yield
    for tail in tails:
        tail.wait_recv()


def spread_tokens(wire, table, rows, own=None):
    here, core = lax.axis_index("tensor"), lax.axis_index("core")
    half = rows // 2

    def send(step, low, size, device):
        ref = table.at[rows_at((core * RING + turn(here, step)) * rows + low, size)]
        src = own if own is not None and step == 0 else ref
        return wire.copy(src, ref, device)

    sibling = {"core": 1 - core}
    ahead = send(0, 0, rows, {"tensor": turn(here, 1)})
    back = send(0, 0, rows, {"tensor": turn(here, -1)})
    across = [send(0, 0, rows, sibling)]
    yield
    ahead.wait_recv()
    tail_ahead = send(-1, 0, half, {"tensor": turn(here, 1)})
    across.append(send(-1, 0, rows, sibling))
    yield
    back.wait_recv()
    tail_back = send(1, half, half, {"tensor": turn(here, -1)})
    across.append(send(1, 0, rows, sibling))
    yield
    tail_ahead.wait_recv()
    tail_back.wait_recv()
    across.append(send(2, 0, rows, sibling))
    yield
    for remote in across:
        remote.wait_recv()


TILE = 16


def add_rows(target, sources):
    rows = target.shape[0]
    step_rows = min(rows, 2 * TILE)

    def body(step, carry):
        at = pl.ds(pl.multiple_of(step * step_rows, step_rows), step_rows)
        if len(sources) == 2 and target.dtype == bf16:
            target[at, :] = sources[0][at, :] + sources[1][at, :]
            return carry
        total = sources[0][at, :].astype(f32)
        for source in sources[1:]:
            total = total + source[at, :].astype(f32)
        target[at, :] = total.astype(target.dtype)
        return carry

    if rows == step_rows:
        body(0, 0)
    else:
        lax.fori_loop(0, rows // step_rows, body, 0)


def reduce_rows(
    wire, grad, half, rows, first, second, up1, down1, up2, down2, result, origin=None
):
    here_first, here_second = lax.axis_index(first), lax.axis_index(second)
    part = rows // 2
    top, bottom = pl.ds(0, part), pl.ds(part, part)

    def block(step_first, step_second, low, size, table=grad):
        index = {first: turn(here_first, step_first), second: turn(here_second, step_second)}
        chip = index["x"] * RING + index["y"]
        return table.at[rows_at(chip * 2 * rows + half * rows + low, size)]

    origin = grad if origin is None else origin
    ahead, back = {first: turn(here_first, 1)}, {first: turn(here_first, -1)}
    order = (2, 1, -1, 0)
    far, near = {}, {}
    for slot, ss in enumerate(order):
        far[ss] = (
            wire.copy(block(2, ss, 0, part, origin), up1.at[slot], ahead),
            wire.copy(block(2, ss, part, part, origin), down1.at[slot], back),
        )
        near[ss] = [
            wire.copy(block(1, ss, part, part, origin), up2.at[slot, bottom], ahead),
            wire.copy(block(-1, ss, 0, part, origin), down2.at[slot, top], back),
        ]
    yield
    for slot, ss in enumerate(order):
        far[ss][0].wait_recv()
        add_rows(up1.at[slot], [up1.at[slot], block(1, ss, 0, part)])
        near[ss].append(wire.copy(up1.at[slot], up2.at[slot, top], ahead))
        far[ss][1].wait_recv()
        add_rows(down1.at[slot], [down1.at[slot], block(-1, ss, part, part)])
        near[ss].append(wire.copy(down1.at[slot], down2.at[slot, bottom], back))
        yield
    ahead, back = {second: turn(here_second, 1)}, {second: turn(here_second, -1)}
    last = []
    for slot, ss in enumerate(order):
        for remote in near[ss]:
            remote.wait_recv()
        if ss == 0:
            break
        add_rows(up2.at[slot], [up2.at[slot], down2.at[slot], block(0, ss, 0, rows)])
        total = up2.at[slot]
        if ss == 2:
            across = (
                wire.copy(total.at[top], up1.at[4], ahead),
                wire.copy(total.at[bottom], down1.at[4], back),
            )
        elif ss == 1:
            last.append(wire.copy(total.at[bottom], up2.at[4, bottom], ahead))
            across[0].wait_recv()
            add_rows(up1.at[4], [up1.at[4], total.at[top]])
            last.append(wire.copy(up1.at[4], up2.at[4, top], ahead))
        else:
            last.append(wire.copy(total.at[top], down2.at[4, top], back))
            across[1].wait_recv()
            add_rows(down1.at[4], [down1.at[4], total.at[bottom]])
            last.append(wire.copy(down1.at[4], down2.at[4, bottom], back))
        yield
    for remote in last:
        remote.wait_recv()
    add_rows(result, [up2.at[3], down2.at[3], block(0, 0, 0, rows), up2.at[4], down2.at[4]])


def reduce_tokens(wire, partial, rows, pair, up1, down1, up2, down2, result):
    here, core = lax.axis_index("tensor"), lax.axis_index("core")
    part = rows // 2
    top, bottom = pl.ds(0, part), pl.ds(part, part)
    ahead, back = {"tensor": turn(here, 1)}, {"tensor": turn(here, -1)}

    def block(side, step):
        return partial.at[rows_at((side * RING + turn(here, step)) * rows, rows)]

    order = (2, 1, -1, 0)
    across = [
        wire.copy(block(1 - core, step), pair.at[slot], {"core": 1 - core})
        for slot, step in enumerate(order)
    ]
    yield
    near = []
    for slot, step in enumerate(order):
        across[slot].wait_recv()
        if step == 0:
            break
        add_rows(pair.at[slot], [pair.at[slot], block(core, step)])
        total = pair.at[slot]
        if step == 2:
            far = (
                wire.copy(total.at[top], up1, ahead),
                wire.copy(total.at[bottom], down1, back),
            )
        elif step == 1:
            near.append(wire.copy(total.at[bottom], up2.at[bottom], ahead))
        else:
            near.append(wire.copy(total.at[top], down2.at[top], back))
        yield
    far[0].wait_recv()
    add_rows(up1, [up1, pair.at[1, top]])
    near.append(wire.copy(up1, up2.at[top], ahead))
    far[1].wait_recv()
    add_rows(down1, [down1, pair.at[2, bottom]])
    near.append(wire.copy(down1, down2.at[bottom], back))
    yield
    for remote in near:
        remote.wait_recv()
    add_rows(result, [pair.at[3], block(core, 0), up2, down2])


HEAD = 64
ROT = 32
norm_epsilon = 1e-05
masked_score = -1e30
GROUP_ROWS = 512
ORDER = "".join(
    (
        "FFFF1vFFFFttcFFFFFSFSFSFSfttVS",
        "S2SSccSSSSSTSTSTSTsccCTTTTTTTTTTTTe",
    )
)
LANES = 128
WIDE = 256
gelu_scale = 0.7978845608028654
gelu_cubic = 0.044715
scale_value = HEAD ** (-0.5)
ROWS_CROSS = ((1,), (1,))
COLUMNS_CROSS = ((0,), (0,))


def matmul(left, right, contract=((1,), (0,))):
    return lax.dot_general(left, right, (contract, ((), ())), preferred_element_type=f32)


def lane_ids(rows, width):
    return lax.broadcasted_iota(jnp.int32, (rows, width), 1)


def swap_halves(values):
    width = values.shape[1]
    lane = lax.rem(lane_ids(*values.shape), HEAD)
    half = ROT // 2
    return jnp.where(
        lane < half, pltpu.roll(values, width - half, 1), pltpu.roll(values, half, 1)
    )


def turned(values, cosine, sine):
    return values * cosine + swap_halves(values) * sine


def head_lanes(values, side):
    keep = lane_ids(*values.shape) // HEAD == side
    return jnp.where(keep, values, jnp.zeros_like(values))


def visible_block(start, row_low, row_count, column_count):
    rows = lax.broadcasted_iota(jnp.int32, (row_count, column_count), 0) + row_low
    columns = lax.broadcasted_iota(jnp.int32, (row_count, column_count), 1)
    return (columns <= rows) & (columns.astype(f32) >= start)


def normalize(rows, gain, shift):
    residual = rows.astype(f32)
    center = residual - jnp.mean(residual, -1, keepdims=True)
    variance = jnp.mean(center * center, -1, keepdims=True)
    return center * lax.rsqrt(variance + norm_epsilon) * gain + shift


def norm_pieces(tokens, hidden, table, pieces):
    count = tokens.shape[0] // pieces
    step_rows = 32
    for piece in range(pieces):

        def body(step, carry):
            at = pl.ds(pl.multiple_of(piece * count + step * step_rows, step_rows), step_rows)
            hidden[at, :] = normalize(tokens[at, :], table[0:1, :], table[1:2, :]).astype(bf16)
            return carry

        lax.fori_loop(0, count // step_rows, body, 0)
        yield


def project_pieces(hidden, in_full, table, cosine, sine, qkv, middle, gelu_slope):
    part = lax.axis_index("tensor") * 2 + lax.axis_index("core")
    rows = hidden.shape[0]
    half = rows // 2
    for index in range(3):
        at = pl.ds(index * WIDE, WIDE)
        bias = table[2 + index : 3 + index, pl.ds(pl.multiple_of(part * WIDE, WIDE), WIDE)]

        def body(step, carry):
            down = pl.ds(pl.multiple_of(step * half, half), half)
            values = matmul(hidden[down, :], in_full[:, at]) + bias
            if index < 2:
                wide = [jnp.concatenate([t[down, :]] * 2, 1) for t in (cosine, sine)]
                values = turned(values, *wide)
            qkv[down, at] = values.astype(bf16)
            return carry

        lax.fori_loop(0, 2, body, 0)
        yield
    hidden_units = in_full.shape[1] - 3 * WIDE
    for index in range(hidden_units // WIDE):
        at = pl.ds(3 * WIDE + index * WIDE, WIDE)
        to = pl.ds(WIDE + index * WIDE, WIDE)
        slope_at = pl.ds(index * WIDE, WIDE)
        core, row = lax.axis_index("core"), 7 + lax.axis_index("tensor")
        low = pl.multiple_of(core * hidden_units + index * WIDE, WIDE)
        bias = table[pl.ds(row, 1), pl.ds(low, WIDE)]

        def body(step, carry):
            down = pl.ds(pl.multiple_of(step * half, half), half)
            unit = matmul(hidden[down, :], in_full[:, at]) + bias
            square = unit * unit
            curve = jnp.tanh(gelu_scale * (unit + gelu_cubic * unit * square))
            rise = 0.5 * (1.0 + curve)
            middle[down, to] = (unit * rise).astype(bf16)
            bend = 0.5 * gelu_scale * unit * (1.0 + 3.0 * gelu_cubic * square)
            gelu_slope[down, slope_at] = rise + bend * (1.0 - curve * curve)
            return carry

        lax.fori_loop(0, 2, body, 0)
        yield


def attend_pieces(qkv, start, middle, lse):
    for group in range(2):
        base = group * GROUP_ROWS
        for pair in range(2):
            for tile in range(2):
                low, count = tile * WIDE, (tile + 1) * WIDE
                down = pl.ds(base + low, WIDE)
                keys_at = pl.ds(base, count)
                queries = qkv[down, pl.ds(pair * LANES, LANES)]
                keys = qkv[keys_at, pl.ds(WIDE + pair * LANES, LANES)]
                values = qkv[keys_at, pl.ds(2 * WIDE + pair * LANES, LANES)]
                visible = visible_block(start[down, 0:1], low, WIDE, count)
                outs = []
                for side in range(2):
                    scores = matmul(head_lanes(queries, side), keys, ROWS_CROSS) * scale_value
                    scores = jnp.where(visible, scores, masked_score)
                    top = jnp.max(scores, -1, keepdims=True)
                    raised = jnp.exp(scores - top)
                    total = jnp.sum(raised, -1, keepdims=True)
                    soft = (raised / total).astype(bf16)
                    outs.append(matmul(soft, values))
                    head = pair * 2 + side
                    here = lane_ids(WIDE, LANES) == head
                    lse[down, :] = jnp.where(here, top + jnp.log(total), lse[down, :])
                first = lane_ids(WIDE, LANES) < HEAD
                middle[down, pl.ds(pair * LANES, LANES)] = jnp.where(
                    first, outs[0], outs[1]
                ).astype(bf16)
                yield


def outer_pieces(left, right, at, target):
    for step in range(left.shape[1] // WIDE):
        down = pl.ds(step * WIDE, WIDE)
        target[down, :] = matmul(left[:, down], right[:, at], COLUMNS_CROSS).astype(bf16)
        yield


def in_turn(processes):
    waiting = list(processes)
    while waiting:
        for process in list(waiting):
            if next(process, waiting) is waiting:
                waiting.remove(process)
            yield


def weave(work, wire_steps, per_piece):
    debt = 0.0
    for _ in work:
        debt += per_piece
        while debt >= 1.0:
            debt -= 1.0
            next(wire_steps, None)


def chained(*parts):
    for part in parts:
        for item in part:
            yield item


def fold_rows(at, qkv, out, up, down):
    def part(size):
        return pl.ds(pl.multiple_of(at * size, size), size)

    heads, units = part(qkv.shape[2] // 2), part(up.shape[1] // 2)
    inward = [qkv[index, :, heads] for index in range(3)] + [up[:, units]]
    return inward, [out[:, part(out.shape[1] // 2)], down[:, part(down.shape[1] // 2)]]


def forward_kernel(
    qkv_weight, out_weight, up_weight, down_weight, tokens, cotangent, turns, vector,
    qkv_moment, out_moment, up_moment, down_moment,
    in_save, out_save, cot_save, hidden_save, qkv_save, lse_save, slope_save, middle_save,
    grad_save, turns_save, qkv_cross, out_cross, up_cross, down_cross, table,
    in_low, out_low, in_full, out_full, tokens_full, cot_full, hidden, qkv, lse, slope, middle, grad_out,
    turns_full, slots, mine, send_sem, recv_sem, local_sem, save_sem,
):
    core = lax.axis_index("core")
    chip = lax.axis_index("x") * RING + lax.axis_index("y")
    column = core * RING + lax.axis_index("tensor")
    rows = in_low.shape[1]
    token_rows = tokens.shape[0]
    sibling = {"core": 1 - core}
    for half in range(2):
        inward, outward = fold_rows(half, qkv_weight, out_weight, up_weight, down_weight)
        for low, blocks in ((in_low, inward), (out_low, outward)):
            column_at = 0
            for block in blocks:
                low[half, :, column_at : column_at + block.shape[1]] = block.astype(bf16)
                column_at += block.shape[1]
    greet(plane_peers() + column_peers())
    wire = Wire(send_sem, recv_sem)
    saves = []

    def save(src, dst):
        copy = pltpu.make_async_copy(src, dst, save_sem.at[len(saves)])
        copy.start()
        saves.append(copy)

    own_rows = rows_at(chip * 2 * rows + core * rows, rows)
    own_tokens = rows_at(column * token_rows, token_rows)
    own_turns = rows_at(core * GROUP_ROWS, GROUP_ROWS)
    wide_in = in_low.shape[2]
    parts = [
        (in_low.at[:, :, pl.ds(0, 3 * WIDE)], in_full.at[:, pl.ds(0, 3 * WIDE)]),
        (
            in_low.at[:, :, pl.ds(3 * WIDE, wide_in - 3 * WIDE)],
            in_full.at[:, pl.ds(3 * WIDE, wide_in - 3 * WIDE)],
        ),
        (out_low, out_full),
    ]
    crosses = [wire.copy(low.at[1 - core], full.at[own_rows], sibling) for low, full in parts[:1]]
    pairs = [(low.at[core], full.at[own_rows]) for low, full in parts] + [
        (tokens, tokens_full.at[own_tokens]),
        (cotangent, cot_full.at[own_tokens]),
        (turns, turns_full.at[:, own_turns]),
        (vector, slots.at[column]),
    ]
    here = [
        pltpu.make_async_copy(src, dst, local_sem.at[number])
        for number, (src, dst) in enumerate(pairs)
    ]
    for copy in here:
        copy.start()
    token_steps = spread_tokens(wire, tokens_full, token_rows, tokens)
    next(token_steps)
    crosses += [wire.copy(low.at[1 - core], full.at[own_rows], sibling) for low, full in parts[1:]]
    vector_in = [wire.copy(vector, slots.at[column], peer) for peer in column_peers()]
    spreads = []

    def begin(number):
        here[number].wait()
        crosses[number].wait_recv()
        full = parts[number][1]
        spreads.append(
            [
                spread_rows(wire, full, 0, rows, "x", "y"),
                spread_rows(wire, full, 1, rows, "y", "x"),
            ]
        )
        for process in spreads[-1]:
            next(process)

    begin(0)
    cross_turns = wire.copy(turns, turns_full.at[:, own_turns], sibling)
    theirs = 1 - core

    def their_part(size):
        return pl.ds(pl.multiple_of(theirs * size, size), size)

    cross_moments = [
        wire.copy(qkv_moment.at[:, :, their_part(qkv_cross.shape[2])], qkv_cross, sibling)
    ] + [
        wire.copy(moment.at[:, their_part(target.shape[1])], target, sibling)
        for moment, target in (
            (out_moment, out_cross), (up_moment, up_cross), (down_moment, down_cross),
        )
    ]
    cot_steps = spread_tokens(wire, cot_full, token_rows, cotangent)
    done = set()

    def script(order):
        lines, vector_out = {"F": in_turn(spreads[0])}, []
        for mark in order:
            if mark in "FST":
                next(lines[mark], None)
            elif mark in "12":
                begin(int(mark))
                lines["ST"[int(mark) - 1]] = in_turn(spreads[int(mark)])
            elif mark == "t":
                next(token_steps, None)
            elif mark == "c":
                next(cot_steps, None)
            elif mark == "v":
                for copy in here[3:]:
                    copy.wait()
                for remote in vector_in:
                    remote.wait_recv()
                mine[...] = jnp.sum(slots[...], axis=0)
                width = mine.shape[1]
                lanes = pl.ds(pl.multiple_of(chip * width, width), width)
                for peer in plane_peers():
                    vector_out.append(wire.copy(mine, table.at[:, lanes], peer))
                table[:, lanes] = mine[...]
            elif mark == "V":
                for _ in token_steps:
                    pass
                for remote in vector_out:
                    remote.wait_recv()
                cross_turns.wait_recv()
            elif mark == "C":
                for _ in cot_steps:
                    pass
            elif mark in "fse":
                for _ in lines["FST"["fse".index(mark)]]:
                    pass
            done.add(mark)
            if mark not in "VCfse":
                yield

    steps = script(ORDER)

    def until(mark):
        while mark not in done:
            next(steps)

    until("V")
    save(turns_full, turns_save)
    weave(norm_pieces(tokens_full, hidden, table, 8), steps, 1.0)
    save(hidden, hidden_save)
    lse[...] = jnp.zeros_like(lse)
    until("f")
    project = project_pieces(
        hidden, in_full, table, turns_full.at[0], turns_full.at[1], qkv, middle, slope
    )
    for _ in range(3):
        next(project)
        next(steps, None)
    weave(attend_pieces(qkv, turns_full.at[2], middle, lse), steps, 0.75)
    until("s")
    save(in_full, in_save)
    for _ in range(wide_in // WIDE - 3):
        next(project)
        next(steps, None)
    until("C")
    save(cot_full, cot_save)
    for source, target in ((qkv, qkv_save), (lse, lse_save), (slope, slope_save)):
        save(source, target)
    weave(outer_pieces(cot_full, middle, slice(None), grad_out), steps, 0.75)
    save(middle, middle_save)
    save(grad_out, grad_save)
    for _ in steps:
        pass
    save(out_full, out_save)
    for remote in cross_moments:
        remote.wait_recv()
    wire.drain()
    for copy in saves:
        copy.wait()


def forward_all(weights, tokens, cotangent, turns, vector, moments):
    qkv, out, up, down = weights
    rows = qkv.shape[1]
    full = 2 * RING * RING * rows
    token_full, feature = 2 * RING * tokens.shape[0], tokens.shape[1]
    wide_in = (3 * qkv.shape[2] + up.shape[1]) // 2
    wide_out = (out.shape[1] + down.shape[1]) // 2
    hidden_units = wide_out - WIDE
    any_spec = pl.BlockSpec(memory_space=pl.ANY)
    vmem = pl.BlockSpec(memory_space=pltpu.VMEM)
    kept = [
        ((full, wide_in), bf16),
        ((full, wide_out), bf16),
        ((token_full, feature), bf16),
        ((token_full, feature), bf16),
        ((token_full, 3 * WIDE), bf16),
        ((token_full, LANES), f32),
        ((token_full, hidden_units), f32),
        ((token_full, wide_out), bf16),
        ((full, wide_out), bf16),
        ((3, 2 * GROUP_ROWS, LANES), f32),
    ]
    crossed = [(m.shape[:-1] + (m.shape[-1] // 2,), f32) for m in moments]
    scratch = [((2, rows, wide_in), bf16), ((2, rows, wide_out), bf16)]
    scratch += kept[:2] + [((token_full, feature), bf16)] + kept[2:]
    table = (vector.shape[0], RING * RING * vector.shape[1])
    return pl.pallas_call(
        forward_kernel,
        out_shape=tuple(jax.ShapeDtypeStruct(*entry) for entry in kept + crossed)
        + (jax.ShapeDtypeStruct(table, f32),),
        in_specs=[vmem] * 8 + [any_spec] * 4,
        out_specs=(any_spec,) * (len(kept) + len(crossed)) + (vmem,),
        scratch_shapes=[pltpu.VMEM(*entry) for entry in scratch]
        + [
            pltpu.VMEM((2 * RING,) + vector.shape, f32),
            pltpu.VMEM(vector.shape, f32),
            pltpu.SemaphoreType.DMA((WIRES,)),
            pltpu.SemaphoreType.DMA((WIRES,)),
            pltpu.SemaphoreType.DMA((7,)),
            pltpu.SemaphoreType.DMA((len(kept),)),
        ],
        compiler_params=pltpu.CompilerParams(
            collective_id=0, has_side_effects=True, vmem_limit_bytes=60 * 2**20
        ),
    )(*weights, tokens, cotangent, turns, vector, *moments)


REDUCES = 180
TOKEN_REDUCES = 10
RATES = (0.3, 0.7, 0.4, 1.0, 0.4, 1.25)


class Pump:
    def __init__(self):
        self.lines = []

    def add(self, *lines):
        for line in lines:
            next(line)
        self.lines += lines

    def step(self):
        if self.lines:
            line = self.lines.pop(0)
            if next(line, self) is not self:
                self.lines.append(line)

    def drive(self, work, per_piece):
        debt = 0.0
        for _ in work:
            debt += per_piece
            while debt >= 1.0:
                debt -= 1.0
                self.step()


class Stream:
    def __init__(self, tiles, slots, sems):
        self.tiles, self.slots, self.sems, self.copies = tiles, slots, sems, []
        for _ in range(2):
            self.fetch()

    def fetch(self):
        number = len(self.copies)
        if number < len(self.tiles):
            copy = pltpu.make_async_copy(
                self.tiles[number], self.slots[number % 2], self.sems.at[number % 2]
            )
            copy.start()
            self.copies.append(copy)

    def take(self, number):
        self.copies[number].wait()
        return self.slots[number % 2]


def middle_grad_pieces(cot, weights, slopes, grad_attended, lin_grad, count):
    for index in range(count):
        tile = weights.at[:, pl.ds(index * WIDE, WIDE)]
        if index == 0:
            grad_attended[...] = matmul(cot[...], tile[...]).astype(bf16)
        else:
            slope = slopes.take(index - 1)
            half = cot.shape[0] // 2

            def body(step, carry):
                down = pl.ds(pl.multiple_of(step * half, half), half)
                values = matmul(cot[down, :], tile[...]) * slope[down, :]
                lin_grad[down, pl.ds(3 * WIDE + (index - 1) * WIDE, WIDE)] = values.astype(bf16)
                return carry

            lax.fori_loop(0, 2, body, 0)
            slopes.fetch()
        yield


def back_pieces(left, weights, target, count):
    streamed = isinstance(weights, Stream)
    for index in range(count):
        at = pl.ds(index * WIDE, WIDE)
        tile = weights.take(index) if streamed else weights.at[at, :]
        target[:, at] = matmul(left[...], tile[...], ROWS_CROSS).astype(bf16)
        if streamed:
            weights.fetch()
        yield


def attend_back_pieces(qkv, turns, lse, grad_attended, lin_grad, key_sum, value_sum):
    cosine, sine, start = turns.at[0], turns.at[1], turns.at[2]

    def unturned(values, at):
        values = values * scale_value
        return (values * cosine[at, :] - swap_halves(values) * sine[at, :]).astype(bf16)

    for group in range(2):
        base = group * GROUP_ROWS
        for pair in range(2):
            lanes = pair * LANES
            for tile in (1, 0):
                low, count = tile * WIDE, (tile + 1) * WIDE
                down = pl.ds(base + low, WIDE)
                keys_at = pl.ds(base, count)
                queries = qkv[down, pl.ds(lanes, LANES)]
                keys = qkv[keys_at, pl.ds(WIDE + lanes, LANES)]
                values = qkv[keys_at, pl.ds(2 * WIDE + lanes, LANES)]
                grads = grad_attended[down, pl.ds(lanes, LANES)]
                visible = visible_block(start[down, 0:1], low, WIDE, count)
                query_grad = jnp.zeros((WIDE, LANES), f32)
                key_grad = jnp.zeros((count, LANES), f32)
                value_grad = jnp.zeros((count, LANES), f32)
                for side in range(2):
                    query, grad = head_lanes(queries, side), head_lanes(grads, side)
                    scores = matmul(query, keys, ROWS_CROSS) * scale_value
                    scores = jnp.where(visible, scores, masked_score)
                    head = pair * 2 + side
                    soft = jnp.exp(scores - lse[down, head : head + 1])
                    grad_soft = matmul(grad, values, ROWS_CROSS)
                    delta = jnp.sum(soft * grad_soft, -1, keepdims=True)
                    grad_scores = (soft * (grad_soft - delta)).astype(bf16)
                    query_grad += matmul(grad_scores, head_lanes(keys, side))
                    key_grad += matmul(grad_scores, query, COLUMNS_CROSS)
                    value_grad += matmul(soft.astype(bf16), grad, COLUMNS_CROSS)
                lin_grad[down, pl.ds(lanes, LANES)] = unturned(query_grad, down)
                if tile == 1:
                    key_sum[...] = key_grad
                    value_sum[...] = value_grad
                else:
                    key_sum[0:WIDE, :] += key_grad
                    value_sum[0:WIDE, :] += value_grad
                yield
            all_rows = pl.ds(base, GROUP_ROWS)
            lin_grad[all_rows, pl.ds(WIDE + lanes, LANES)] = unturned(key_sum[...], all_rows)
            lin_grad[all_rows, pl.ds(2 * WIDE + lanes, LANES)] = value_sum[...].astype(bf16)


def backward_kernel(
    in_save, out_save, cot_save, hidden_save, qkv_save, lse_save, slope_save, middle_save,
    grad_save, turns_save,
    in_result, out_result, first_sum, second_sum, bias_sum,
    token_matrix, out_full, rows_low, rows_high, slope_low, slope_high,
    qkv, lse, turns, middle, grad_out, grad_in, lin_grad, grad_attended, summand,
    key_sum, value_sum,
    out_up1, out_down1, out_up2, out_down2,
    up_up1, up_down1, up_up2, up_down2,
    qkv_up1, qkv_down1, qkv_up2, qkv_down2,
    pair, up1, down1, up2, down2,
    send_sem, recv_sem, token_send, token_recv, load_sem, stream_sem, credit,
):
    core = lax.axis_index("core")
    z = lax.axis_index("tensor")
    rows = in_result.shape[1]
    token_rows = first_sum.shape[0]
    hidden_units = slope_save.shape[1]
    qkv_width = qkv.shape[1]
    feature = token_matrix.shape[1]

    def load(number, source, target):
        copy = pltpu.make_async_copy(source, target, load_sem.at[number])
        copy.start()
        return copy

    grad_load = load(0, grad_save, grad_out)
    plane = [{axis: turn(lax.axis_index(axis), way)} for axis in ("x", "y") for way in (1, -1)]
    column = [{"tensor": turn(z, 1)}, {"tensor": turn(z, -1)}, {"core": 1 - core}]
    greet(plane + column)
    cot_load = load(1, cot_save, token_matrix)
    out_load = load(7, out_save, out_full)
    slopes = Stream(
        [slope_save.at[:, pl.ds(index * WIDE, WIDE)] for index in range(hidden_units // WIDE)],
        [slope_low, slope_high],
        stream_sem.at[0],
    )
    other_loads = [
        load(2, middle_save, middle),
        load(3, qkv_save, qkv),
        load(4, lse_save, lse),
        load(5, turns_save, turns),
    ]
    wire = Wire(send_sem, recv_sem)
    first_wire = Wire(token_send.at[0], token_recv.at[0])
    second_wires = [Wire(token_send.at[1], token_recv.at[1]), Wire(token_send.at[2], token_recv.at[2])]
    pump = Pump()

    def halves(grad, landing, result, origin=None):
        return [
            reduce_rows(
                wire, grad, half, rows, *axes, *[buffer.at[half] for buffer in landing],
                result.at[half], origin,
            )
            for half, axes in enumerate((("x", "y"), ("y", "x")))
        ]

    def sum_tokens(token_wire, result):
        return reduce_tokens(
            token_wire, summand, token_rows, pair, up1, down1, up2, down2, result
        )

    pump.add(
        *halves(grad_out, (out_up1, out_down1, out_up2, out_down2), out_result, grad_save)
    )
    grad_load.wait()
    def driven(work, per_piece, tokens=(), marks=()):
        debt = 0.0
        for number, _ in enumerate(work):
            debt += per_piece
            while debt >= 1.0:
                debt -= 1.0
                pump.step()
            for _ in range(marks.count(number)):
                next(tokens)

    out_load.wait()
    other_loads[0].wait()
    driven(back_pieces(middle, out_full, summand, feature // WIDE), RATES[0])
    first_tokens = sum_tokens(first_wire, first_sum)
    next(first_tokens)
    cot_load.wait()
    driven(
        middle_grad_pieces(
            token_matrix, out_full, slopes, grad_attended, lin_grad, 1 + hidden_units // WIDE
        ),
        RATES[1], first_tokens, (3, 4, 4),
    )
    hidden_load = load(6, hidden_save, token_matrix)
    for copy in other_loads[1:]:
        copy.wait()
    in_rows = Stream(
        [in_save.at[pl.ds(index * WIDE, WIDE), :] for index in range(feature // WIDE)],
        [rows_low, rows_high],
        stream_sem.at[1],
    )
    attend = attend_back_pieces(qkv, turns, lse, grad_attended, lin_grad, key_sum, value_sum)
    driven(itertools.islice(attend, 4), RATES[3])
    hidden_load.wait()
    up_at, qkv_at = pl.ds(qkv_width, hidden_units), pl.ds(0, qkv_width)
    driven(outer_pieces(token_matrix, lin_grad, up_at, grad_in.at[:, up_at]), RATES[2])
    pump.add(
        *halves(
            grad_in.at[:, up_at],
            (up_up1, up_down1, up_up2, up_down2),
            in_result.at[:, :, up_at],
        )
    )
    next(first_tokens)
    driven(attend, RATES[3])
    driven(outer_pieces(token_matrix, lin_grad, qkv_at, grad_in.at[:, qkv_at]), RATES[4])
    pump.add(
        *halves(
            grad_in.at[:, qkv_at],
            (qkv_up1, qkv_down1, qkv_up2, qkv_down2),
            in_result.at[:, :, qkv_at],
        )
    )
    span = feature // 2
    seconds = [
        reduce_tokens(
            token_wire, token_matrix.at[:, at], token_rows, pair.at[:, :, at],
            up1.at[:, at], down1.at[:, at], up2.at[:, at], down2.at[:, at], second_sum.at[:, at],
        )
        for token_wire, at in zip(second_wires, (pl.ds(0, span), pl.ds(span, span)))
    ]
    debt = 0.0
    for number, _ in enumerate(back_pieces(lin_grad, in_rows, token_matrix, feature // WIDE)):
        debt += RATES[5]
        while debt >= 1.0:
            debt -= 1.0
            pump.step()
        if number == 1:
            for _ in first_tokens:
                pass
            first_wire.drain()
            for peer in column:
                pl.semaphore_signal(credit, inc=1, device_id=peer, device_id_type=MESH)
        if number == feature // WIDE // 2 - 1:
            pl.semaphore_wait(credit, len(column))
            next(seconds[0])
        elif number > feature // WIDE // 2:
            next(seconds[0])
    next(seconds[1])
    ones = jnp.ones((8, lin_grad.shape[0]), bf16)
    bias_sum[...] = matmul(ones, lin_grad[...])
    pump.step()
    for _ in range(3):
        next(seconds[1])
        pump.step()
        pump.step()
    rest = in_turn(seconds)
    while pump.lines:
        pump.step()
        pump.step()
        next(rest, None)
    for _ in rest:
        pass
    for token_wire in second_wires:
        token_wire.drain()
    wire.drain()


def backward_all(saved, rows):
    in_save, out_save, cot_save, hidden_save, qkv_save, lse_save, slope_save, middle_save = saved[:8]
    token_full, feature = cot_save.shape
    wide_in, wide_out = in_save.shape[1], out_save.shape[1]
    hidden_units = slope_save.shape[1]
    token_rows = token_full // (2 * RING)
    any_spec = pl.BlockSpec(memory_space=pl.ANY)
    vmem = pl.BlockSpec(memory_space=pltpu.VMEM)

    def landing(width):
        return [
            pltpu.VMEM((2, 5, rows // 2, width), bf16),
            pltpu.VMEM((2, 5, rows // 2, width), bf16),
            pltpu.VMEM((2, 5, rows, width), bf16),
            pltpu.VMEM((2, 5, rows, width), bf16),
        ]

    return pl.pallas_call(
        backward_kernel,
        out_shape=(
            jax.ShapeDtypeStruct((2, rows, wide_in), f32),
            jax.ShapeDtypeStruct((2, rows, wide_out), f32),
            jax.ShapeDtypeStruct((token_rows, feature), f32),
            jax.ShapeDtypeStruct((token_rows, feature), f32),
            jax.ShapeDtypeStruct((8, wide_in), f32),
        ),
        in_specs=[any_spec] * 10,
        out_specs=(vmem,) * 5,
        scratch_shapes=[
            pltpu.VMEM((token_full, feature), bf16),
            pltpu.VMEM((feature, wide_out), bf16),
            pltpu.VMEM((WIDE, wide_in), bf16),
            pltpu.VMEM((WIDE, wide_in), bf16),
            pltpu.VMEM((token_full, WIDE), f32),
            pltpu.VMEM((token_full, WIDE), f32),
            pltpu.VMEM((token_full, 3 * WIDE), bf16),
            pltpu.VMEM((token_full, LANES), f32),
            pltpu.VMEM((3, token_full, LANES), f32),
            pltpu.VMEM((token_full, wide_out), bf16),
            pltpu.VMEM((feature, wide_out), bf16),
            pltpu.VMEM((feature, wide_in), bf16),
            pltpu.VMEM((token_full, wide_in), bf16),
            pltpu.VMEM((token_full, WIDE), bf16),
            pltpu.VMEM((token_full, feature), bf16),
            pltpu.VMEM((GROUP_ROWS, LANES), f32),
            pltpu.VMEM((GROUP_ROWS, LANES), f32),
            *landing(wide_out),
            *landing(hidden_units),
            *landing(3 * WIDE),
            pltpu.VMEM((4, token_rows, feature), bf16),
            pltpu.VMEM((token_rows // 2, feature), bf16),
            pltpu.VMEM((token_rows // 2, feature), bf16),
            pltpu.VMEM((token_rows, feature), bf16),
            pltpu.VMEM((token_rows, feature), bf16),
            pltpu.SemaphoreType.DMA((REDUCES,)),
            pltpu.SemaphoreType.DMA((REDUCES,)),
            pltpu.SemaphoreType.DMA((3, TOKEN_REDUCES)),
            pltpu.SemaphoreType.DMA((3, TOKEN_REDUCES)),
            pltpu.SemaphoreType.DMA((8,)),
            pltpu.SemaphoreType.DMA((2, 2)),
            pltpu.SemaphoreType.REGULAR,
        ],
        compiler_params=pltpu.CompilerParams(
            collective_id=1, has_side_effects=True, vmem_limit_bytes=62 * 2**20
        ),
    )(*saved)


BR = 256
SWEEPS = 5
ortho_epsilon = 1e-07
coef_linear = 3.4445
coef_square = -4.775
coef_cubic = 2.0315


def split(value):
    high = value.astype(bf16)
    return high, (value - high.astype(f32)).astype(bf16)


def triple(left, right, contract):
    dims = (contract, ((), ()))
    (left_high, left_low), (right_high, right_low) = left, right

    def dot(a, b):
        return lax.dot_general(a, b, dims, preferred_element_type=f32)

    return dot(left_high, right_high) + (dot(left_high, right_low) + dot(left_low, right_high))


def sweep_block(current, high, low):
    columns = current.shape[1]
    chunk = 512
    total = jnp.zeros((current.shape[0], chunk), f32)
    for index in range(columns // chunk):
        values = current[:, index * chunk : (index + 1) * chunk]
        total = total + values * values
    inverse = 1.0 / (jnp.sqrt(jnp.sum(total)) + ortho_epsilon)
    values = current[...] * inverse
    current[...] = values
    high[...], low[...] = split(values)

    def sweep(index, carry):
        rows, plain = ((1,), (1,)), ((1,), (0,))
        cross = matmul(high[...], low[...], rows)
        gram = matmul(high[...], high[...], rows) + (cross + cross.T)
        halves = split(gram)
        factor = split(coef_square * gram + coef_cubic * triple(halves, halves, plain))
        values = coef_linear * current[...] + triple(factor, (high[...], low[...]), plain)
        current[...] = values
        high[...], low[...] = split(values)
        return carry

    lax.fori_loop(0, SWEEPS, sweep, 0)


muon_decay = 0.95
decay_factor = 0.01
rate_qkv = 1.0
rate_out = 4.0
rate_up = 0.8
rate_down = 0.4


def finish_tokens(tokens, cotangent, first_sum, second_sum, table, layer_out, input_grad, sums):
    step_rows = 16
    sums[...] = jnp.zeros_like(sums)
    gain = table[0:1, :]
    bias = table[5:6, :] + table[6:7, :]

    def fold(values):
        return values[0:8] + values[8:16]

    def body(step, carry):
        at = pl.ds(pl.multiple_of(step * step_rows, step_rows), step_rows)
        residual = tokens[at, :].astype(f32)
        center = residual - jnp.mean(residual, -1, keepdims=True)
        variance = jnp.mean(center * center, -1, keepdims=True)
        scale_inv = lax.rsqrt(variance + norm_epsilon)
        normed = center * scale_inv
        layer_out[at, :] = (residual + first_sum[at, :] + bias).astype(bf16)
        grad_hidden = second_sum[at, :]
        cot = cotangent[at, :].astype(f32)
        grad_hat = grad_hidden * gain
        input_grad[at, :] = cot + scale_inv * (
            grad_hat
            - jnp.mean(grad_hat, -1, keepdims=True)
            - normed * jnp.mean(grad_hat * normed, -1, keepdims=True)
        )
        sums[0:8, :] += fold(grad_hidden * normed)
        sums[8:16, :] += fold(grad_hidden)
        sums[16:24, :] += fold(cot)
        return carry

    lax.fori_loop(0, tokens.shape[0] // step_rows, body, 0)


def finish_kernel(
    in_save, out_save, first_save, second_save,
    qkv_moment, out_moment, up_moment, down_moment, qkv_cross, out_cross, up_cross, down_cross,
    tokens, cotangent, bias_sum, table,
    in_sum, out_sum, update, layer_out, input_grad, vector_sum,
    in_result, out_result, first_sum, second_sum, nesterov, land, back, whole, current, high, low, sums, vector,
    plane_slots, mine, column_slots,
    out_send, out_recv, back_send, back_recv, plane_send, plane_recv, column_send, column_recv,
    cross_send, cross_recv, load_sem,
):
    loads = [
        pltpu.make_async_copy(source, target, load_sem.at[number])
        for number, (source, target) in enumerate(
            (
                (in_save, in_result),
                (out_save, out_result),
                (first_save, first_sum),
                (second_save, second_sum),
            )
        )
    ]
    for copy in loads:
        copy.start()
    core = lax.axis_index("core")
    z = lax.axis_index("tensor")
    chip = lax.axis_index("x") * RING + lax.axis_index("y")
    column = core * RING + z
    chips = RING * RING
    owners = nesterov.shape[1] // BR
    rows = nesterov.shape[0]
    half = rows // 2
    wide_in = in_result.shape[2]
    sibling = {"core": 1 - core}
    greet(plane_peers() + column_peers())

    def cross(number, source, target):
        remote = pltpu.make_async_remote_copy(
            src_ref=source,
            dst_ref=target,
            send_sem=cross_send.at[number],
            recv_sem=cross_recv.at[number],
            device_id=sibling,
            device_id_type=MESH,
        )
        remote.start()
        return remote

    def lanes(owner):
        return pl.ds(pl.multiple_of(owner * BR, BR), BR)

    def other(step):
        index = turn(chip, step, chips)
        return index, {"x": index // RING, "y": lax.rem(index, RING)}

    def outward(step):
        index, device = other(step)
        owner = jnp.minimum(index, owners - 1)
        return index, pltpu.make_async_remote_copy(
            src_ref=nesterov.at[:, lanes(owner)],
            dst_ref=land.at[chip],
            send_sem=out_send.at[step],
            recv_sem=out_recv.at[step],
            device_id=device,
            device_id_type=MESH,
        )

    def homeward(step):
        index, device = other(step)
        owner = jnp.minimum(chip, owners - 1)
        return index, pltpu.make_async_remote_copy(
            src_ref=back.at[index],
            dst_ref=whole.at[:, lanes(owner)],
            send_sem=back_send.at[step],
            recv_sem=back_recv.at[step],
            device_id=device,
            device_id_type=MESH,
        )

    def blend(at, moments):
        down = rows_at(at * half, half)
        column_at = 0
        for result, blocks in zip((in_result, out_result), moments):
            result_at = 0
            for own in blocks:
                width = own.shape[1]
                grad = result[at, :, result_at : result_at + width]
                values = grad + muon_decay * (muon_decay * own + grad)
                nesterov[down, column_at : column_at + width] = values.astype(bf16)
                column_at += width
                result_at += width

    loads[0].wait()
    loads[1].wait()
    blend(core, fold_rows(core, qkv_moment, out_moment, up_moment, down_moment))
    blend(
        1 - core,
        (
            [qkv_cross[0], qkv_cross[1], qkv_cross[2], up_cross[...]],
            [out_cross[...], down_cross[...]],
        ),
    )
    for step in range(1, chips):
        index, remote = outward(step)
        pl.when(index < owners)(remote.start)

    @pl.when(chip < owners)
    def own_piece():
        land[chip] = nesterov[:, lanes(chip)]

    crosses = [
        cross(0, out_result.at[1 - core], out_sum.at[core]),
        cross(1, in_result.at[1 - core], in_sum.at[core]),
    ]
    loads[2].wait()
    loads[3].wait()
    finish_tokens(
        tokens, cotangent, first_sum, second_sum, table, layer_out, input_grad, sums
    )
    vector[...] = jnp.zeros_like(vector)
    vector[0:1, :] = jnp.sum(sums[0:8, :], 0, keepdims=True)
    vector[1:2, :] = jnp.sum(sums[8:16, :], 0, keepdims=True)
    cot_sum = jnp.sum(sums[16:24, :], 0, keepdims=True)
    vector[5:6, :] = cot_sum
    vector[6:7, :] = cot_sum
    part = z * 2 + core
    for index in range(3):
        vector[2 + index : 3 + index, lanes(part)] = bias_sum[0:1, index * BR : (index + 1) * BR]
    hidden_units = wide_in - 3 * BR
    vector[pl.ds(7 + z, 1), pl.ds(pl.multiple_of(core * hidden_units, BR), hidden_units)] = (
        bias_sum[0:1, 3 * BR :]
    )
    width = mine.shape[1]

    def strip(place):
        return pl.ds(pl.multiple_of(place * width, width), width)

    plane_copies = []
    for step in range(1, chips):
        index, device = other(step)
        remote = pltpu.make_async_remote_copy(
            src_ref=vector.at[:, strip(index)],
            dst_ref=plane_slots.at[chip],
            send_sem=plane_send.at[step],
            recv_sem=plane_recv.at[step],
            device_id=device,
            device_id_type=MESH,
        )
        remote.start()
        plane_copies.append(remote)
    plane_slots[chip] = vector[:, strip(chip)]
    in_sum[core] = in_result[core]
    out_sum[core] = out_result[core]
    for remote in plane_copies:
        remote.wait_recv()
    mine[...] = jnp.sum(plane_slots[...], axis=0)
    column_slots[column] = mine[...]
    column_copies = []
    for step, peer in enumerate(column_peers()):
        remote = pltpu.make_async_remote_copy(
            src_ref=mine,
            dst_ref=column_slots.at[column],
            send_sem=column_send.at[step],
            recv_sem=column_recv.at[step],
            device_id=peer,
            device_id_type=MESH,
        )
        remote.start()
        column_copies.append(remote)

    @pl.when(chip < owners)
    def own_block():
        for step in range(1, chips):
            outward(step)[1].wait_recv()
        for place in range(chips):
            current[:, place * rows : (place + 1) * rows] = land[place].astype(f32).T
        sweep_block(current, high, low)
        for place in range(chips):
            back[place] = current[:, place * rows : (place + 1) * rows].T.astype(bf16)
        for step in range(1, chips):
            homeward(step)[1].start()
        whole[:, lanes(chip)] = back[chip]

    for remote in column_copies:
        remote.wait_recv()
    vector_sum[...] = jnp.sum(column_slots[...], axis=0)
    for step in range(1, chips):
        index, remote = homeward(step)
        sender = turn(chip, -step, chips)
        pl.when(sender < owners)(remote.wait_recv)
    crosses.append(cross(2, whole.at[rows_at((1 - core) * half, half)], update.at[core]))
    update[core] = whole[rows_at(core * half, half), :]
    for step in range(1, chips):
        index, remote = outward(step)
        pl.when(index < owners)(remote.wait_send)

    @pl.when(chip < owners)
    def sent_back():
        for step in range(1, chips):
            homeward(step)[1].wait_send()

    for remote in plane_copies + column_copies:
        remote.wait_send()
    for remote in crosses:
        remote.wait()


def finish_all(results, moments, crosses, tokens, cotangent, bias_sum, table):
    half = results[0].shape[1]
    columns = results[0].shape[2] + results[1].shape[2]
    rows = 2 * half
    token_rows, feature = tokens.shape
    chips = RING * RING
    small = (table.shape[0], feature // chips)
    vmem = pl.BlockSpec(memory_space=pltpu.VMEM)
    any_spec = pl.BlockSpec(memory_space=pl.ANY)
    return pl.pallas_call(
        finish_kernel,
        out_shape=(
            jax.ShapeDtypeStruct(results[0].shape, f32),
            jax.ShapeDtypeStruct(results[1].shape, f32),
            jax.ShapeDtypeStruct((2, half, columns), bf16),
            jax.ShapeDtypeStruct((token_rows, feature), bf16),
            jax.ShapeDtypeStruct((token_rows, feature), f32),
            jax.ShapeDtypeStruct(small, f32),
        ),
        in_specs=[any_spec] * 4 + [vmem] * 12,
        out_specs=(vmem,) * 6,
        scratch_shapes=[pltpu.VMEM(result.shape, f32) for result in results]
        + [
            pltpu.VMEM((rows, columns), bf16),
            pltpu.VMEM((chips, rows, BR), bf16),
            pltpu.VMEM((chips, rows, BR), bf16),
            pltpu.VMEM((rows, columns), bf16),
            pltpu.VMEM((BR, chips * rows), f32),
            pltpu.VMEM((BR, chips * rows), bf16),
            pltpu.VMEM((BR, chips * rows), bf16),
            pltpu.VMEM((24, feature), f32),
            pltpu.VMEM(table.shape, f32),
            pltpu.VMEM((chips,) + small, f32),
            pltpu.VMEM(small, f32),
            pltpu.VMEM((2 * RING,) + small, f32),
            *[pltpu.SemaphoreType.DMA((chips,)) for _ in range(6)],
            *[pltpu.SemaphoreType.DMA((2 * RING,)) for _ in range(2)],
            pltpu.SemaphoreType.DMA((3,)),
            pltpu.SemaphoreType.DMA((3,)),
            pltpu.SemaphoreType.DMA((4,)),
        ],
        compiler_params=pltpu.CompilerParams(
            collective_id=2, has_side_effects=True, vmem_limit_bytes=56 * 2**20
        ),
    )(*results, *moments, *crosses, tokens, cotangent, bias_sum, table)


def apply_kernel(
    in_save, out_save, update_save, layer_save, input_save,
    qkv_weight, out_weight, up_weight, down_weight,
    qkv_moment, out_moment, up_moment, down_moment,
    qkv_new, out_new, up_new, down_new,
    qkv_moment_new, out_moment_new, up_moment_new, down_moment_new, layer_out, input_grad,
    in_sum, out_sum, update, *rest,
):
    *held, load_sem = rest
    states = (
        qkv_weight, out_weight, up_weight, down_weight,
        qkv_moment, out_moment, up_moment, down_moment,
    )
    pairs = [(in_save, in_sum), (out_save, out_sum), (update_save, update)]
    pairs += [*zip(states, held), (layer_save, layer_out), (input_save, input_grad)]
    loads = [
        pltpu.make_async_copy(source, target, load_sem.at[number])
        for number, (source, target) in enumerate(pairs)
    ]
    for copy in loads:
        copy.start()
    for copy in loads:
        copy.wait()
    (
        qkv_weight, out_weight, up_weight, down_weight,
        qkv_moment, out_moment, up_moment, down_moment,
    ) = held
    heads, units = qkv_weight.shape[2] // 2, up_weight.shape[1] // 2
    outs, downs = out_weight.shape[1] // 2, down_weight.shape[1] // 2
    wide_in = in_sum.shape[2]

    def step(at, weight, moment, new, moment_new, grad, orthogonal, rate):
        moment_new[at] = muon_decay * moment[at] + grad
        new[at] = weight[at] * (1.0 - decay_factor * rate) - rate * orthogonal.astype(f32)

    for half in range(2):

        def lanes(size):
            return (slice(None), slice(half * size, (half + 1) * size))

        for index in range(3):
            from_at = slice(index * heads, (index + 1) * heads)
            step(
                (index,) + lanes(heads), qkv_weight, qkv_moment, qkv_new, qkv_moment_new,
                in_sum[half, :, from_at], update[half, :, from_at], rate_qkv,
            )
        step(
            lanes(units), up_weight, up_moment, up_new, up_moment_new,
            in_sum[half, :, 3 * heads :], update[half, :, 3 * heads : wide_in], rate_up,
        )
        step(
            lanes(outs), out_weight, out_moment, out_new, out_moment_new,
            out_sum[half, :, :outs], update[half, :, wide_in : wide_in + outs], rate_out,
        )
        step(
            lanes(downs), down_weight, down_moment, down_new, down_moment_new,
            out_sum[half, :, outs:], update[half, :, wide_in + outs :], rate_down,
        )


def apply_all(in_sum, out_sum, update, layer_out, input_grad, weights, moments):
    vmem = pl.BlockSpec(memory_space=pltpu.VMEM)
    hbm = pl.BlockSpec(memory_space=pltpu.HBM)
    return pl.pallas_call(
        apply_kernel,
        out_shape=tuple(
            jax.ShapeDtypeStruct(w.shape, w.dtype)
            for w in (*weights, *moments, layer_out, input_grad)
        ),
        in_specs=[hbm] * 13,
        out_specs=(vmem,) * 10,
        scratch_shapes=[
            pltpu.VMEM(in_sum.shape, f32),
            pltpu.VMEM(out_sum.shape, f32),
            pltpu.VMEM(update.shape, bf16),
            *[pltpu.VMEM(state.shape, f32) for state in (*weights, *moments)],
            pltpu.SemaphoreType.DMA((13,)),
        ],
        compiler_params=pltpu.CompilerParams(vmem_limit_bytes=62 * 2**20),
    )(in_sum, out_sum, update, layer_out, input_grad, *weights, *moments)


def turn_tables(positions):
    half = ROT // 2
    count = positions.shape[0]
    lane = jnp.arange(LANES)[None, None, :]
    kind = jnp.arange(3)[:, None, None]
    place = positions.astype(f32)[None, :, None]
    within = lane % HEAD
    angle = place * rotary_base ** (-2.0 * (lane % half).astype(f32) / ROT)
    sign = jnp.where(within < half, -1.0, 1.0)
    turns = within < ROT
    start = jnp.arange(count).astype(f32)[None, :, None] - place
    cosine = jnp.where(turns, jnp.cos(angle), 1.0)
    sine = jnp.where(turns, jnp.sin(angle) * sign, 0.0)
    return jnp.where(kind == 0, cosine, jnp.where(kind == 1, sine, start))


def local(
    inputs,
    cotangent,
    positions,
    qkv_weight,
    out_weight,
    up_weight,
    down_weight,
    qkv_moment,
    out_moment,
    up_moment,
    down_moment,
    vectors,
    vector_first,
    vector_second,
):
    vector_rows, vector_width = vectors.shape
    column = lax.axis_index("core") * RING + lax.axis_index("tensor")
    spread = jnp.tile(jnp.pad(vectors, ((0, 16 - vector_rows), (0, 0))), (1, 2 * RING))
    mine = jnp.arange(spread.shape[1])[None, :] // vector_width == column
    vector_mine = jnp.where(mine, spread, 0.0)
    rows = qkv_weight.shape[0]

    def turned_over(qkv, out, up, down):
        return (qkv.transpose(1, 0, 2), out.T, up, down.T)

    weights = turned_over(qkv_weight, out_weight, up_weight, down_weight)
    moments = turned_over(qkv_moment, out_moment, up_moment, down_moment)
    kept = forward_all(weights, inputs, cotangent, turn_tables(positions), vector_mine, moments)
    saved, crosses, table = kept[:10], kept[10:14], kept[14]
    *results, bias_sum = backward_all(saved, rows)
    in_sum, out_sum, update, layer_out, input_grad, vector_sum = finish_all(
        results, moments, crosses, inputs, cotangent, bias_sum, table
    )
    vector_grad = lax.dynamic_slice(
        vector_sum, (0, column * vector_width), (vector_rows, vector_width)
    )
    first_new = first_decay * vector_first + (1.0 - first_decay) * vector_grad
    second_new = second_decay * vector_second + (1.0 - second_decay) * vector_grad * vector_grad
    first_hat = first_new / (1.0 - first_decay**STEP)
    second_hat = second_new / (1.0 - second_decay**STEP)
    vectors_new = vectors - adam_rate * first_hat / (jnp.sqrt(second_hat) + adam_epsilon)

    applied = apply_all(in_sum, out_sum, update, layer_out, input_grad, weights, moments)
    qkv_new, out_new, up_new, down_new = turned_over(*applied[:4])
    qkv_moment_new, out_moment_new, up_moment_new, down_moment_new = turned_over(*applied[4:8])
    layer_out, input_grad = applied[8:]
    return (
        layer_out,
        input_grad,
        qkv_new,
        out_new,
        up_new,
        down_new,
        qkv_moment_new,
        out_moment_new,
        up_moment_new,
        down_moment_new,
        first_new,
        second_new,
        vectors_new,
    )


def solution(mesh):
    wide = Mesh(mesh.devices.reshape(4, 4, 2, 4), ALL)
    in_specs = (
        P(ALL, None),
        P(ALL, None),
        P(DP),
        P(DP, None, "tensor"),
        P("tensor", DP),
        P(DP, "tensor"),
        P("tensor", DP),
        P(DP, None, "tensor"),
        P("tensor", DP),
        P(DP, "tensor"),
        P("tensor", DP),
        P(None, ALL),
        P(None, ALL),
        P(None, ALL),
    )
    out_specs = (
        P(ALL, None),
        P(ALL, None),
        P(DP, None, "tensor"),
        P("tensor", DP),
        P(DP, "tensor"),
        P("tensor", DP),
        P(DP, None, "tensor"),
        P("tensor", DP),
        P(DP, "tensor"),
        P("tensor", DP),
        P(None, ALL),
        P(None, ALL),
        P(None, ALL),
    )
    return jax.shard_map(local, mesh=wide, in_specs=in_specs, out_specs=out_specs, check_vma=False)
```

```python
import itertools

import jax
import jax.numpy as jnp
from jax import lax
from jax.experimental import pallas as pl
from jax.experimental.pallas import tpu as pltpu
from jax.sharding import Mesh
from jax.sharding import PartitionSpec as P

STEP = 10

rotary_base = 10000.0
adam_rate = 0.2
first_decay = 0.9
second_decay = 0.95
adam_epsilon = 1e-08

f32 = jnp.float32
bf16 = jnp.bfloat16
DP = ("x", "y", "core")
ALL = ("x", "y", "core", "tensor")

MESH = pl.DeviceIdType.MESH
RING = 4
WIRES = 180


def turn(index, step, size=RING):
    return lax.rem(index + (step % size), size)


class Wire:
    def __init__(self, send_sem, recv_sem):
        self.send_sem, self.recv_sem, self.sent = send_sem, recv_sem, []

    def copy(self, src, dst, device):
        number = len(self.sent)
        remote = pltpu.make_async_remote_copy(
            src_ref=src,
            dst_ref=dst,
            send_sem=self.send_sem.at[number],
            recv_sem=self.recv_sem.at[number],
            device_id=device,
            device_id_type=MESH,
        )
        remote.start()
        self.sent.append(remote)
        return remote

    def drain(self):
        for remote in self.sent:
            remote.wait_send()


def rows_at(start, size):
    return pl.ds(pl.multiple_of(start, 16), size)


def greet(peers):
    barrier = pltpu.get_barrier_semaphore()
    for peer in peers:
        pl.semaphore_signal(barrier, inc=1, device_id=peer, device_id_type=MESH)
    pl.semaphore_wait(barrier, len(peers))


def plane_peers():
    place = lax.axis_index("x") * RING + lax.axis_index("y")
    peers = []
    for step in range(1, RING * RING):
        other = turn(place, step, RING * RING)
        peers.append({"x": other // RING, "y": lax.rem(other, RING)})
    return peers


def column_peers():
    place = lax.axis_index("core") * RING + lax.axis_index("tensor")
    peers = []
    for step in range(1, 2 * RING):
        other = turn(place, step, 2 * RING)
        peers.append({"core": other // RING, "tensor": lax.rem(other, RING)})
    return peers


def spread_rows(wire, table, half, rows, first, second, own=None):
    here_first, here_second = lax.axis_index(first), lax.axis_index(second)
    quarter = rows // 2

    def block(step_first, step_second, low, size):
        index = {first: turn(here_first, step_first), second: turn(here_second, step_second)}
        chip = index["x"] * RING + index["y"]
        return table.at[rows_at(chip * 2 * rows + half * rows + low, size)]

    def send(step_first, step_second, low, size, axis, direction):
        ref = src = block(step_first, step_second, low, size)
        if own is not None and step_first == 0 and step_second == 0:
            src = own
        here = here_first if axis == first else here_second
        return wire.copy(src, ref, {axis: turn(here, direction)})

    def both(step_first):
        return [send(step_first, 0, 0, rows, second, way) for way in (1, -1)]

    ahead = send(0, 0, 0, rows, first, 1)
    back = send(0, 0, 0, rows, first, -1)
    lines = {0: both(0)}
    yield
    ahead.wait_recv()
    tail_ahead = send(-1, 0, 0, quarter, first, 1)
    lines[-1] = both(-1)
    yield
    back.wait_recv()
    tail_back = send(1, 0, quarter, quarter, first, -1)
    lines[1] = both(1)
    tails = []

    def relay(step_first):
        from_back, from_ahead = lines[step_first]
        from_back.wait_recv()
        tails.append(send(step_first, -1, 0, quarter, second, 1))
        from_ahead.wait_recv()
        tails.append(send(step_first, 1, quarter, quarter, second, -1))

    yield
    relay(0)
    yield
    tail_ahead.wait_recv()
    tail_back.wait_recv()
    lines[2] = both(2)
    yield
    relay(-1)
    yield
    relay(1)
    yield
    relay(2)
    yield
    for tail in tails:
        tail.wait_recv()


def spread_tokens(wire, table, rows, own=None):
    here, core = lax.axis_index("tensor"), lax.axis_index("core")
    half = rows // 2

    def send(step, low, size, device):
        ref = table.at[rows_at((core * RING + turn(here, step)) * rows + low, size)]
        src = own if own is not None and step == 0 else ref
        return wire.copy(src, ref, device)

    sibling = {"core": 1 - core}
    ahead = send(0, 0, rows, {"tensor": turn(here, 1)})
    back = send(0, 0, rows, {"tensor": turn(here, -1)})
    across = [send(0, 0, rows, sibling)]
    yield
    ahead.wait_recv()
    tail_ahead = send(-1, 0, half, {"tensor": turn(here, 1)})
    across.append(send(-1, 0, rows, sibling))
    yield
    back.wait_recv()
    tail_back = send(1, half, half, {"tensor": turn(here, -1)})
    across.append(send(1, 0, rows, sibling))
    yield
    tail_ahead.wait_recv()
    tail_back.wait_recv()
    across.append(send(2, 0, rows, sibling))
    yield
    for remote in across:
        remote.wait_recv()


TILE = 16


def add_rows(target, sources):
    rows = target.shape[0]
    step_rows = min(rows, 2 * TILE)

    def body(step, carry):
        at = pl.ds(pl.multiple_of(step * step_rows, step_rows), step_rows)
        if len(sources) == 2 and target.dtype == bf16:
            target[at, :] = sources[0][at, :] + sources[1][at, :]
            return carry
        total = sources[0][at, :].astype(f32)
        for source in sources[1:]:
            total = total + source[at, :].astype(f32)
        target[at, :] = total.astype(target.dtype)
        return carry

    if rows == step_rows:
        body(0, 0)
    else:
        lax.fori_loop(0, rows // step_rows, body, 0)


def reduce_rows(
    wire, grad, half, rows, first, second, up1, down1, up2, down2, result, origin=None
):
    here_first, here_second = lax.axis_index(first), lax.axis_index(second)
    part = rows // 2
    top, bottom = pl.ds(0, part), pl.ds(part, part)

    def block(step_first, step_second, low, size, table=grad):
        index = {first: turn(here_first, step_first), second: turn(here_second, step_second)}
        chip = index["x"] * RING + index["y"]
        return table.at[rows_at(chip * 2 * rows + half * rows + low, size)]

    origin = grad if origin is None else origin
    ahead, back = {first: turn(here_first, 1)}, {first: turn(here_first, -1)}
    order = (2, 1, -1, 0)
    far, near = {}, {}
    for slot, ss in enumerate(order):
        far[ss] = (
            wire.copy(block(2, ss, 0, part, origin), up1.at[slot], ahead),
            wire.copy(block(2, ss, part, part, origin), down1.at[slot], back),
        )
        near[ss] = [
            wire.copy(block(1, ss, part, part, origin), up2.at[slot, bottom], ahead),
            wire.copy(block(-1, ss, 0, part, origin), down2.at[slot, top], back),
        ]
    yield
    for slot, ss in enumerate(order):
        far[ss][0].wait_recv()
        add_rows(up1.at[slot], [up1.at[slot], block(1, ss, 0, part)])
        near[ss].append(wire.copy(up1.at[slot], up2.at[slot, top], ahead))
        far[ss][1].wait_recv()
        add_rows(down1.at[slot], [down1.at[slot], block(-1, ss, part, part)])
        near[ss].append(wire.copy(down1.at[slot], down2.at[slot, bottom], back))
        yield
    ahead, back = {second: turn(here_second, 1)}, {second: turn(here_second, -1)}
    last = []
    for slot, ss in enumerate(order):
        for remote in near[ss]:
            remote.wait_recv()
        if ss == 0:
            break
        add_rows(up2.at[slot], [up2.at[slot], down2.at[slot], block(0, ss, 0, rows)])
        total = up2.at[slot]
        if ss == 2:
            across = (
                wire.copy(total.at[top], up1.at[4], ahead),
                wire.copy(total.at[bottom], down1.at[4], back),
            )
        elif ss == 1:
            last.append(wire.copy(total.at[bottom], up2.at[4, bottom], ahead))
            across[0].wait_recv()
            add_rows(up1.at[4], [up1.at[4], total.at[top]])
            last.append(wire.copy(up1.at[4], up2.at[4, top], ahead))
        else:
            last.append(wire.copy(total.at[top], down2.at[4, top], back))
            across[1].wait_recv()
            add_rows(down1.at[4], [down1.at[4], total.at[bottom]])
            last.append(wire.copy(down1.at[4], down2.at[4, bottom], back))
        yield
    for remote in last:
        remote.wait_recv()
    add_rows(result, [up2.at[3], down2.at[3], block(0, 0, 0, rows), up2.at[4], down2.at[4]])


def reduce_tokens(wire, partial, rows, pair, up1, down1, up2, down2, result):
    here, core = lax.axis_index("tensor"), lax.axis_index("core")
    part = rows // 2
    top, bottom = pl.ds(0, part), pl.ds(part, part)
    ahead, back = {"tensor": turn(here, 1)}, {"tensor": turn(here, -1)}

    def block(side, step):
        return partial.at[rows_at((side * RING + turn(here, step)) * rows, rows)]

    order = (2, 1, -1, 0)
    across = [
        wire.copy(block(1 - core, step), pair.at[slot], {"core": 1 - core})
        for slot, step in enumerate(order)
    ]
    yield
    near = []
    for slot, step in enumerate(order):
        across[slot].wait_recv()
        if step == 0:
            break
        add_rows(pair.at[slot], [pair.at[slot], block(core, step)])
        total = pair.at[slot]
        if step == 2:
            far = (
                wire.copy(total.at[top], up1, ahead),
                wire.copy(total.at[bottom], down1, back),
            )
        elif step == 1:
            near.append(wire.copy(total.at[bottom], up2.at[bottom], ahead))
        else:
            near.append(wire.copy(total.at[top], down2.at[top], back))
        yield
    far[0].wait_recv()
    add_rows(up1, [up1, pair.at[1, top]])
    near.append(wire.copy(up1, up2.at[top], ahead))
    far[1].wait_recv()
    add_rows(down1, [down1, pair.at[2, bottom]])
    near.append(wire.copy(down1, down2.at[bottom], back))
    yield
    for remote in near:
        remote.wait_recv()
    add_rows(result, [pair.at[3], block(core, 0), up2, down2])


HEAD = 64
ROT = 32
norm_epsilon = 1e-05
masked_score = -1e30
GROUP_ROWS = 512
ORDER = "".join(
    (
        "FFFF1vFFFFttcFFFFFSFSFSFSfttVS",
        "S2SSccSSSSSTSTSTSTsccCTTTTTTTTTTTTe",
    )
)
LANES = 128
WIDE = 256
gelu_scale = 0.7978845608028654
gelu_cubic = 0.044715
scale_value = HEAD ** (-0.5)
ROWS_CROSS = ((1,), (1,))
COLUMNS_CROSS = ((0,), (0,))


def matmul(left, right, contract=((1,), (0,))):
    return lax.dot_general(left, right, (contract, ((), ())), preferred_element_type=f32)


def lane_ids(rows, width):
    return lax.broadcasted_iota(jnp.int32, (rows, width), 1)


def swap_halves(values):
    width = values.shape[1]
    lane = lax.rem(lane_ids(*values.shape), HEAD)
    half = ROT // 2
    return jnp.where(
        lane < half, pltpu.roll(values, width - half, 1), pltpu.roll(values, half, 1)
    )


def turned(values, cosine, sine):
    return values * cosine + swap_halves(values) * sine


def head_lanes(values, side):
    keep = lane_ids(*values.shape) // HEAD == side
    return jnp.where(keep, values, jnp.zeros_like(values))


def visible_block(start, row_low, row_count, column_count):
    rows = lax.broadcasted_iota(jnp.int32, (row_count, column_count), 0) + row_low
    columns = lax.broadcasted_iota(jnp.int32, (row_count, column_count), 1)
    return (columns <= rows) & (columns.astype(f32) >= start)


def normalize(rows, gain, shift):
    residual = rows.astype(f32)
    center = residual - jnp.mean(residual, -1, keepdims=True)
    variance = jnp.mean(center * center, -1, keepdims=True)
    return center * lax.rsqrt(variance + norm_epsilon) * gain + shift


def norm_pieces(tokens, hidden, table, pieces):
    count = tokens.shape[0] // pieces
    step_rows = 32
    for piece in range(pieces):

        def body(step, carry):
            at = pl.ds(pl.multiple_of(piece * count + step * step_rows, step_rows), step_rows)
            hidden[at, :] = normalize(tokens[at, :], table[0:1, :], table[1:2, :]).astype(bf16)
            return carry

        lax.fori_loop(0, count // step_rows, body, 0)
        yield


def project_pieces(hidden, in_full, table, cosine, sine, qkv, middle, gelu_slope):
    part = lax.axis_index("tensor") * 2 + lax.axis_index("core")
    rows = hidden.shape[0]
    half = rows // 2
    for index in range(3):
        at = pl.ds(index * WIDE, WIDE)
        bias = table[2 + index : 3 + index, pl.ds(pl.multiple_of(part * WIDE, WIDE), WIDE)]

        def body(step, carry):
            down = pl.ds(pl.multiple_of(step * half, half), half)
            values = matmul(hidden[down, :], in_full[:, at]) + bias
            if index < 2:
                wide = [jnp.concatenate([t[down, :]] * 2, 1) for t in (cosine, sine)]
                values = turned(values, *wide)
            qkv[down, at] = values.astype(bf16)
            return carry

        lax.fori_loop(0, 2, body, 0)
        yield
    hidden_units = in_full.shape[1] - 3 * WIDE
    for index in range(hidden_units // WIDE):
        at = pl.ds(3 * WIDE + index * WIDE, WIDE)
        to = pl.ds(WIDE + index * WIDE, WIDE)
        slope_at = pl.ds(index * WIDE, WIDE)
        core, row = lax.axis_index("core"), 7 + lax.axis_index("tensor")
        low = pl.multiple_of(core * hidden_units + index * WIDE, WIDE)
        bias = table[pl.ds(row, 1), pl.ds(low, WIDE)]

        def body(step, carry):
            down = pl.ds(pl.multiple_of(step * half, half), half)
            unit = matmul(hidden[down, :], in_full[:, at]) + bias
            square = unit * unit
            curve = jnp.tanh(gelu_scale * (unit + gelu_cubic * unit * square))
            rise = 0.5 * (1.0 + curve)
            middle[down, to] = (unit * rise).astype(bf16)
            bend = 0.5 * gelu_scale * unit * (1.0 + 3.0 * gelu_cubic * square)
            gelu_slope[down, slope_at] = rise + bend * (1.0 - curve * curve)
            return carry

        lax.fori_loop(0, 2, body, 0)
        yield


def attend_pieces(qkv, start, middle, lse):
    for group in range(2):
        base = group * GROUP_ROWS
        for pair in range(2):
            for tile in range(2):
                low, count = tile * WIDE, (tile + 1) * WIDE
                down = pl.ds(base + low, WIDE)
                keys_at = pl.ds(base, count)
                queries = qkv[down, pl.ds(pair * LANES, LANES)]
                keys = qkv[keys_at, pl.ds(WIDE + pair * LANES, LANES)]
                values = qkv[keys_at, pl.ds(2 * WIDE + pair * LANES, LANES)]
                visible = visible_block(start[down, 0:1], low, WIDE, count)
                outs = []
                for side in range(2):
                    scores = matmul(head_lanes(queries, side), keys, ROWS_CROSS) * scale_value
                    scores = jnp.where(visible, scores, masked_score)
                    top = jnp.max(scores, -1, keepdims=True)
                    raised = jnp.exp(scores - top)
                    total = jnp.sum(raised, -1, keepdims=True)
                    soft = (raised / total).astype(bf16)
                    outs.append(matmul(soft, values))
                    head = pair * 2 + side
                    here = lane_ids(WIDE, LANES) == head
                    lse[down, :] = jnp.where(here, top + jnp.log(total), lse[down, :])
                first = lane_ids(WIDE, LANES) < HEAD
                middle[down, pl.ds(pair * LANES, LANES)] = jnp.where(
                    first, outs[0], outs[1]
                ).astype(bf16)
                yield


def outer_pieces(left, right, at, target):
    for step in range(left.shape[1] // WIDE):
        down = pl.ds(step * WIDE, WIDE)
        target[down, :] = matmul(left[:, down], right[:, at], COLUMNS_CROSS).astype(bf16)
        yield


def in_turn(processes):
    waiting = list(processes)
    while waiting:
        for process in list(waiting):
            if next(process, waiting) is waiting:
                waiting.remove(process)
            yield


def weave(work, wire_steps, per_piece):
    debt = 0.0
    for _ in work:
        debt += per_piece
        while debt >= 1.0:
            debt -= 1.0
            next(wire_steps, None)


def chained(*parts):
    for part in parts:
        for item in part:
            yield item


def fold_rows(at, qkv, out, up, down):
    def part(size):
        return pl.ds(pl.multiple_of(at * size, size), size)

    heads, units = part(qkv.shape[2] // 2), part(up.shape[1] // 2)
    inward = [qkv[index, :, heads] for index in range(3)] + [up[:, units]]
    return inward, [out[:, part(out.shape[1] // 2)], down[:, part(down.shape[1] // 2)]]


def forward_kernel(
    qkv_weight, out_weight, up_weight, down_weight, tokens, cotangent, turns, vector,
    qkv_moment, out_moment, up_moment, down_moment,
    in_save, out_save, cot_save, hidden_save, qkv_save, lse_save, slope_save, middle_save,
    grad_save, turns_save, qkv_cross, out_cross, up_cross, down_cross, table,
    in_low, out_low, in_full, out_full, tokens_full, cot_full, hidden, qkv, lse, slope, middle, grad_out,
    turns_full, slots, mine, send_sem, recv_sem, local_sem, save_sem,
):
    core = lax.axis_index("core")
    chip = lax.axis_index("x") * RING + lax.axis_index("y")
    column = core * RING + lax.axis_index("tensor")
    rows = in_low.shape[1]
    token_rows = tokens.shape[0]
    sibling = {"core": 1 - core}
    for half in range(2):
        inward, outward = fold_rows(half, qkv_weight, out_weight, up_weight, down_weight)
        for low, blocks in ((in_low, inward), (out_low, outward)):
            column_at = 0
            for block in blocks:
                low[half, :, column_at : column_at + block.shape[1]] = block.astype(bf16)
                column_at += block.shape[1]
    greet(plane_peers() + column_peers())
    wire = Wire(send_sem, recv_sem)
    saves = []

    def save(src, dst):
        copy = pltpu.make_async_copy(src, dst, save_sem.at[len(saves)])
        copy.start()
        saves.append(copy)

    own_rows = rows_at(chip * 2 * rows + core * rows, rows)
    own_tokens = rows_at(column * token_rows, token_rows)
    own_turns = rows_at(core * GROUP_ROWS, GROUP_ROWS)
    wide_in = in_low.shape[2]
    parts = [
        (in_low.at[:, :, pl.ds(0, 3 * WIDE)], in_full.at[:, pl.ds(0, 3 * WIDE)]),
        (
            in_low.at[:, :, pl.ds(3 * WIDE, wide_in - 3 * WIDE)],
            in_full.at[:, pl.ds(3 * WIDE, wide_in - 3 * WIDE)],
        ),
        (out_low, out_full),
    ]
    crosses = [wire.copy(low.at[1 - core], full.at[own_rows], sibling) for low, full in parts[:1]]
    pairs = [(low.at[core], full.at[own_rows]) for low, full in parts] + [
        (tokens, tokens_full.at[own_tokens]),
        (cotangent, cot_full.at[own_tokens]),
        (turns, turns_full.at[:, own_turns]),
        (vector, slots.at[column]),
    ]
    here = [
        pltpu.make_async_copy(src, dst, local_sem.at[number])
        for number, (src, dst) in enumerate(pairs)
    ]
    for copy in here:
        copy.start()
    token_steps = spread_tokens(wire, tokens_full, token_rows, tokens)
    next(token_steps)
    crosses += [wire.copy(low.at[1 - core], full.at[own_rows], sibling) for low, full in parts[1:]]
    vector_in = [wire.copy(vector, slots.at[column], peer) for peer in column_peers()]
    spreads = []

    def begin(number):
        here[number].wait()
        crosses[number].wait_recv()
        full = parts[number][1]
        spreads.append(
            [
                spread_rows(wire, full, 0, rows, "x", "y"),
                spread_rows(wire, full, 1, rows, "y", "x"),
            ]
        )
        for process in spreads[-1]:
            next(process)

    begin(0)
    cross_turns = wire.copy(turns, turns_full.at[:, own_turns], sibling)
    theirs = 1 - core

    def their_part(size):
        return pl.ds(pl.multiple_of(theirs * size, size), size)

    cross_moments = [
        wire.copy(qkv_moment.at[:, :, their_part(qkv_cross.shape[2])], qkv_cross, sibling)
    ] + [
        wire.copy(moment.at[:, their_part(target.shape[1])], target, sibling)
        for moment, target in (
            (out_moment, out_cross), (up_moment, up_cross), (down_moment, down_cross),
        )
    ]
    cot_steps = spread_tokens(wire, cot_full, token_rows, cotangent)
    done = set()

    def script(order):
        lines, vector_out = {"F": in_turn(spreads[0])}, []
        for mark in order:
            if mark in "FST":
                next(lines[mark], None)
            elif mark in "12":
                begin(int(mark))
                lines["ST"[int(mark) - 1]] = in_turn(spreads[int(mark)])
            elif mark == "t":
                next(token_steps, None)
            elif mark == "c":
                next(cot_steps, None)
            elif mark == "v":
                for copy in here[3:]:
                    copy.wait()
                for remote in vector_in:
                    remote.wait_recv()
                mine[...] = jnp.sum(slots[...], axis=0)
                width = mine.shape[1]
                lanes = pl.ds(pl.multiple_of(chip * width, width), width)
                for peer in plane_peers():
                    vector_out.append(wire.copy(mine, table.at[:, lanes], peer))
                table[:, lanes] = mine[...]
            elif mark == "V":
                for _ in token_steps:
                    pass
                for remote in vector_out:
                    remote.wait_recv()
                cross_turns.wait_recv()
            elif mark == "C":
                for _ in cot_steps:
                    pass
            elif mark in "fse":
                for _ in lines["FST"["fse".index(mark)]]:
                    pass
            done.add(mark)
            if mark not in "VCfse":
                yield

    steps = script(ORDER)

    def until(mark):
        while mark not in done:
            next(steps)

    until("V")
    save(turns_full, turns_save)
    weave(norm_pieces(tokens_full, hidden, table, 8), steps, 0.75)
    save(hidden, hidden_save)
    lse[...] = jnp.zeros_like(lse)
    until("f")
    project = project_pieces(
        hidden, in_full, table, turns_full.at[0], turns_full.at[1], qkv, middle, slope
    )
    for _ in range(3):
        next(project)
        next(steps, None)
    weave(attend_pieces(qkv, turns_full.at[2], middle, lse), steps, 0.5)
    until("s")
    save(in_full, in_save)
    for _ in range(wide_in // WIDE - 3):
        next(project)
        next(steps, None)
    until("C")
    save(cot_full, cot_save)
    for source, target in ((qkv, qkv_save), (lse, lse_save), (slope, slope_save)):
        save(source, target)
    weave(outer_pieces(cot_full, middle, slice(None), grad_out), steps, 0.5)
    save(middle, middle_save)
    save(grad_out, grad_save)
    for _ in steps:
        pass
    save(out_full, out_save)
    for remote in cross_moments:
        remote.wait_recv()
    wire.drain()
    for copy in saves:
        copy.wait()


def forward_all(weights, tokens, cotangent, turns, vector, moments):
    qkv, out, up, down = weights
    rows = qkv.shape[1]
    full = 2 * RING * RING * rows
    token_full, feature = 2 * RING * tokens.shape[0], tokens.shape[1]
    wide_in = (3 * qkv.shape[2] + up.shape[1]) // 2
    wide_out = (out.shape[1] + down.shape[1]) // 2
    hidden_units = wide_out - WIDE
    any_spec = pl.BlockSpec(memory_space=pl.ANY)
    vmem = pl.BlockSpec(memory_space=pltpu.VMEM)
    kept = [
        ((full, wide_in), bf16),
        ((full, wide_out), bf16),
        ((token_full, feature), bf16),
        ((token_full, feature), bf16),
        ((token_full, 3 * WIDE), bf16),
        ((token_full, LANES), f32),
        ((token_full, hidden_units), f32),
        ((token_full, wide_out), bf16),
        ((full, wide_out), bf16),
        ((3, 2 * GROUP_ROWS, LANES), f32),
    ]
    crossed = [(m.shape[:-1] + (m.shape[-1] // 2,), f32) for m in moments]
    scratch = [((2, rows, wide_in), bf16), ((2, rows, wide_out), bf16)]
    scratch += kept[:2] + [((token_full, feature), bf16)] + kept[2:]
    table = (vector.shape[0], RING * RING * vector.shape[1])
    return pl.pallas_call(
        forward_kernel,
        out_shape=tuple(jax.ShapeDtypeStruct(*entry) for entry in kept + crossed)
        + (jax.ShapeDtypeStruct(table, f32),),
        in_specs=[vmem] * 8 + [any_spec] * 4,
        out_specs=(any_spec,) * (len(kept) + len(crossed)) + (vmem,),
        scratch_shapes=[pltpu.VMEM(*entry) for entry in scratch]
        + [
            pltpu.VMEM((2 * RING,) + vector.shape, f32),
            pltpu.VMEM(vector.shape, f32),
            pltpu.SemaphoreType.DMA((WIRES,)),
            pltpu.SemaphoreType.DMA((WIRES,)),
            pltpu.SemaphoreType.DMA((7,)),
            pltpu.SemaphoreType.DMA((len(kept),)),
        ],
        compiler_params=pltpu.CompilerParams(
            collective_id=0, has_side_effects=True, vmem_limit_bytes=60 * 2**20
        ),
    )(*weights, tokens, cotangent, turns, vector, *moments)


REDUCES = 180
TOKEN_REDUCES = 10
RATES = (0.3, 0.7, 0.4, 0.75, 0.4, 0.75)


class Pump:
    def __init__(self):
        self.lines = []

    def add(self, *lines):
        for line in lines:
            next(line)
        self.lines += lines

    def step(self):
        if self.lines:
            line = self.lines.pop(0)
            if next(line, self) is not self:
                self.lines.append(line)

    def drive(self, work, per_piece):
        debt = 0.0
        for _ in work:
            debt += per_piece
            while debt >= 1.0:
                debt -= 1.0
                self.step()


class Stream:
    def __init__(self, tiles, slots, sems):
        self.tiles, self.slots, self.sems, self.copies = tiles, slots, sems, []
        for _ in range(2):
            self.fetch()

    def fetch(self):
        number = len(self.copies)
        if number < len(self.tiles):
            copy = pltpu.make_async_copy(
                self.tiles[number], self.slots[number % 2], self.sems.at[number % 2]
            )
            copy.start()
            self.copies.append(copy)

    def take(self, number):
        self.copies[number].wait()
        return self.slots[number % 2]


def middle_grad_pieces(cot, weights, slopes, grad_attended, lin_grad, count):
    for index in range(count):
        tile = weights.at[:, pl.ds(index * WIDE, WIDE)]
        if index == 0:
            grad_attended[...] = matmul(cot[...], tile[...]).astype(bf16)
        else:
            slope = slopes.take(index - 1)
            half = cot.shape[0] // 2

            def body(step, carry):
                down = pl.ds(pl.multiple_of(step * half, half), half)
                values = matmul(cot[down, :], tile[...]) * slope[down, :]
                lin_grad[down, pl.ds(3 * WIDE + (index - 1) * WIDE, WIDE)] = values.astype(bf16)
                return carry

            lax.fori_loop(0, 2, body, 0)
            slopes.fetch()
        yield


def back_pieces(left, weights, target, count):
    streamed = isinstance(weights, Stream)
    for index in range(count):
        at = pl.ds(index * WIDE, WIDE)
        tile = weights.take(index) if streamed else weights.at[at, :]
        target[:, at] = matmul(left[...], tile[...], ROWS_CROSS).astype(bf16)
        if streamed:
            weights.fetch()
        yield


def attend_back_pieces(qkv, turns, lse, grad_attended, lin_grad, key_sum, value_sum):
    cosine, sine, start = turns.at[0], turns.at[1], turns.at[2]

    def unturned(values, at):
        values = values * scale_value
        return (values * cosine[at, :] - swap_halves(values) * sine[at, :]).astype(bf16)

    for group in range(2):
        base = group * GROUP_ROWS
        for pair in range(2):
            lanes = pair * LANES
            for tile in (1, 0):
                low, count = tile * WIDE, (tile + 1) * WIDE
                down = pl.ds(base + low, WIDE)
                keys_at = pl.ds(base, count)
                queries = qkv[down, pl.ds(lanes, LANES)]
                keys = qkv[keys_at, pl.ds(WIDE + lanes, LANES)]
                values = qkv[keys_at, pl.ds(2 * WIDE + lanes, LANES)]
                grads = grad_attended[down, pl.ds(lanes, LANES)]
                visible = visible_block(start[down, 0:1], low, WIDE, count)
                query_grad = jnp.zeros((WIDE, LANES), f32)
                key_grad = jnp.zeros((count, LANES), f32)
                value_grad = jnp.zeros((count, LANES), f32)
                for side in range(2):
                    query, grad = head_lanes(queries, side), head_lanes(grads, side)
                    scores = matmul(query, keys, ROWS_CROSS) * scale_value
                    scores = jnp.where(visible, scores, masked_score)
                    head = pair * 2 + side
                    soft = jnp.exp(scores - lse[down, head : head + 1])
                    grad_soft = matmul(grad, values, ROWS_CROSS)
                    delta = jnp.sum(soft * grad_soft, -1, keepdims=True)
                    grad_scores = (soft * (grad_soft - delta)).astype(bf16)
                    query_grad += matmul(grad_scores, head_lanes(keys, side))
                    key_grad += matmul(grad_scores, query, COLUMNS_CROSS)
                    value_grad += matmul(soft.astype(bf16), grad, COLUMNS_CROSS)
                lin_grad[down, pl.ds(lanes, LANES)] = unturned(query_grad, down)
                if tile == 1:
                    key_sum[...] = key_grad
                    value_sum[...] = value_grad
                else:
                    key_sum[0:WIDE, :] += key_grad
                    value_sum[0:WIDE, :] += value_grad
                yield
            all_rows = pl.ds(base, GROUP_ROWS)
            lin_grad[all_rows, pl.ds(WIDE + lanes, LANES)] = unturned(key_sum[...], all_rows)
            lin_grad[all_rows, pl.ds(2 * WIDE + lanes, LANES)] = value_sum[...].astype(bf16)


def backward_kernel(
    in_save, out_save, cot_save, hidden_save, qkv_save, lse_save, slope_save, middle_save,
    grad_save, turns_save,
    in_result, out_result, first_sum, second_sum, bias_sum,
    token_matrix, out_full, rows_low, rows_high, slope_low, slope_high,
    qkv, lse, turns, middle, grad_out, grad_in, lin_grad, grad_attended, summand,
    key_sum, value_sum,
    out_up1, out_down1, out_up2, out_down2,
    up_up1, up_down1, up_up2, up_down2,
    qkv_up1, qkv_down1, qkv_up2, qkv_down2,
    pair, up1, down1, up2, down2,
    send_sem, recv_sem, token_send, token_recv, load_sem, stream_sem, credit,
):
    core = lax.axis_index("core")
    z = lax.axis_index("tensor")
    rows = in_result.shape[1]
    token_rows = first_sum.shape[0]
    hidden_units = slope_save.shape[1]
    qkv_width = qkv.shape[1]
    feature = token_matrix.shape[1]

    def load(number, source, target):
        copy = pltpu.make_async_copy(source, target, load_sem.at[number])
        copy.start()
        return copy

    grad_load = load(0, grad_save, grad_out)
    plane = [{axis: turn(lax.axis_index(axis), way)} for axis in ("x", "y") for way in (1, -1)]
    column = [{"tensor": turn(z, 1)}, {"tensor": turn(z, -1)}, {"core": 1 - core}]
    greet(plane + column)
    cot_load = load(1, cot_save, token_matrix)
    out_load = load(7, out_save, out_full)
    slopes = Stream(
        [slope_save.at[:, pl.ds(index * WIDE, WIDE)] for index in range(hidden_units // WIDE)],
        [slope_low, slope_high],
        stream_sem.at[0],
    )
    other_loads = [
        load(2, middle_save, middle),
        load(3, qkv_save, qkv),
        load(4, lse_save, lse),
        load(5, turns_save, turns),
    ]
    wire = Wire(send_sem, recv_sem)
    first_wire = Wire(token_send.at[0], token_recv.at[0])
    second_wires = [Wire(token_send.at[1], token_recv.at[1]), Wire(token_send.at[2], token_recv.at[2])]
    pump = Pump()

    def halves(grad, landing, result, origin=None):
        return [
            reduce_rows(
                wire, grad, half, rows, *axes, *[buffer.at[half] for buffer in landing],
                result.at[half], origin,
            )
            for half, axes in enumerate((("x", "y"), ("y", "x")))
        ]

    def sum_tokens(token_wire, result):
        return reduce_tokens(
            token_wire, summand, token_rows, pair, up1, down1, up2, down2, result
        )

    pump.add(
        *halves(grad_out, (out_up1, out_down1, out_up2, out_down2), out_result, grad_save)
    )
    grad_load.wait()
    def driven(work, per_piece, tokens=(), marks=()):
        debt = 0.0
        for number, _ in enumerate(work):
            debt += per_piece
            while debt >= 1.0:
                debt -= 1.0
                pump.step()
            for _ in range(marks.count(number)):
                next(tokens)

    out_load.wait()
    other_loads[0].wait()
    driven(back_pieces(middle, out_full, summand, feature // WIDE), RATES[0])
    first_tokens = sum_tokens(first_wire, first_sum)
    next(first_tokens)
    cot_load.wait()
    driven(
        middle_grad_pieces(
            token_matrix, out_full, slopes, grad_attended, lin_grad, 1 + hidden_units // WIDE
        ),
        RATES[1], first_tokens, (3, 4, 4),
    )
    hidden_load = load(6, hidden_save, token_matrix)
    for copy in other_loads[1:]:
        copy.wait()
    in_rows = Stream(
        [in_save.at[pl.ds(index * WIDE, WIDE), :] for index in range(feature // WIDE)],
        [rows_low, rows_high],
        stream_sem.at[1],
    )
    attend = attend_back_pieces(qkv, turns, lse, grad_attended, lin_grad, key_sum, value_sum)
    driven(itertools.islice(attend, 4), RATES[3])
    hidden_load.wait()
    up_at, qkv_at = pl.ds(qkv_width, hidden_units), pl.ds(0, qkv_width)
    driven(outer_pieces(token_matrix, lin_grad, up_at, grad_in.at[:, up_at]), RATES[2])
    pump.add(
        *halves(
            grad_in.at[:, up_at],
            (up_up1, up_down1, up_up2, up_down2),
            in_result.at[:, :, up_at],
        )
    )
    next(first_tokens)
    driven(attend, RATES[3])
    driven(outer_pieces(token_matrix, lin_grad, qkv_at, grad_in.at[:, qkv_at]), RATES[4])
    pump.add(
        *halves(
            grad_in.at[:, qkv_at],
            (qkv_up1, qkv_down1, qkv_up2, qkv_down2),
            in_result.at[:, :, qkv_at],
        )
    )
    span = feature // 2
    seconds = [
        reduce_tokens(
            token_wire, token_matrix.at[:, at], token_rows, pair.at[:, :, at],
            up1.at[:, at], down1.at[:, at], up2.at[:, at], down2.at[:, at], second_sum.at[:, at],
        )
        for token_wire, at in zip(second_wires, (pl.ds(0, span), pl.ds(span, span)))
    ]
    debt = 0.0
    for number, _ in enumerate(back_pieces(lin_grad, in_rows, token_matrix, feature // WIDE)):
        debt += RATES[5]
        while debt >= 1.0:
            debt -= 1.0
            pump.step()
        if number == 1:
            for _ in first_tokens:
                pass
            first_wire.drain()
            for peer in column:
                pl.semaphore_signal(credit, inc=1, device_id=peer, device_id_type=MESH)
        if number == feature // WIDE // 2 - 1:
            pl.semaphore_wait(credit, len(column))
            next(seconds[0])
        elif number > feature // WIDE // 2:
            next(seconds[0])
    next(seconds[1])
    ones = jnp.ones((8, lin_grad.shape[0]), bf16)
    bias_sum[...] = matmul(ones, lin_grad[...])
    pump.step()
    for _ in range(3):
        next(seconds[1])
        pump.step()
        pump.step()
    rest = in_turn(seconds)
    while pump.lines:
        pump.step()
        pump.step()
        next(rest, None)
    for _ in rest:
        pass
    for token_wire in second_wires:
        token_wire.drain()
    wire.drain()


def backward_all(saved, rows):
    in_save, out_save, cot_save, hidden_save, qkv_save, lse_save, slope_save, middle_save = saved[:8]
    token_full, feature = cot_save.shape
    wide_in, wide_out = in_save.shape[1], out_save.shape[1]
    hidden_units = slope_save.shape[1]
    token_rows = token_full // (2 * RING)
    any_spec = pl.BlockSpec(memory_space=pl.ANY)
    vmem = pl.BlockSpec(memory_space=pltpu.VMEM)

    def landing(width):
        return [
            pltpu.VMEM((2, 5, rows // 2, width), bf16),
            pltpu.VMEM((2, 5, rows // 2, width), bf16),
            pltpu.VMEM((2, 5, rows, width), bf16),
            pltpu.VMEM((2, 5, rows, width), bf16),
        ]

    return pl.pallas_call(
        backward_kernel,
        out_shape=(
            jax.ShapeDtypeStruct((2, rows, wide_in), f32),
            jax.ShapeDtypeStruct((2, rows, wide_out), f32),
            jax.ShapeDtypeStruct((token_rows, feature), f32),
            jax.ShapeDtypeStruct((token_rows, feature), f32),
            jax.ShapeDtypeStruct((8, wide_in), f32),
        ),
        in_specs=[any_spec] * 10,
        out_specs=(vmem,) * 5,
        scratch_shapes=[
            pltpu.VMEM((token_full, feature), bf16),
            pltpu.VMEM((feature, wide_out), bf16),
            pltpu.VMEM((WIDE, wide_in), bf16),
            pltpu.VMEM((WIDE, wide_in), bf16),
            pltpu.VMEM((token_full, WIDE), f32),
            pltpu.VMEM((token_full, WIDE), f32),
            pltpu.VMEM((token_full, 3 * WIDE), bf16),
            pltpu.VMEM((token_full, LANES), f32),
            pltpu.VMEM((3, token_full, LANES), f32),
            pltpu.VMEM((token_full, wide_out), bf16),
            pltpu.VMEM((feature, wide_out), bf16),
            pltpu.VMEM((feature, wide_in), bf16),
            pltpu.VMEM((token_full, wide_in), bf16),
            pltpu.VMEM((token_full, WIDE), bf16),
            pltpu.VMEM((token_full, feature), bf16),
            pltpu.VMEM((GROUP_ROWS, LANES), f32),
            pltpu.VMEM((GROUP_ROWS, LANES), f32),
            *landing(wide_out),
            *landing(hidden_units),
            *landing(3 * WIDE),
            pltpu.VMEM((4, token_rows, feature), bf16),
            pltpu.VMEM((token_rows // 2, feature), bf16),
            pltpu.VMEM((token_rows // 2, feature), bf16),
            pltpu.VMEM((token_rows, feature), bf16),
            pltpu.VMEM((token_rows, feature), bf16),
            pltpu.SemaphoreType.DMA((REDUCES,)),
            pltpu.SemaphoreType.DMA((REDUCES,)),
            pltpu.SemaphoreType.DMA((3, TOKEN_REDUCES)),
            pltpu.SemaphoreType.DMA((3, TOKEN_REDUCES)),
            pltpu.SemaphoreType.DMA((8,)),
            pltpu.SemaphoreType.DMA((2, 2)),
            pltpu.SemaphoreType.REGULAR,
        ],
        compiler_params=pltpu.CompilerParams(
            collective_id=1, has_side_effects=True, vmem_limit_bytes=62 * 2**20
        ),
    )(*saved)


BR = 256
SWEEPS = 5
ortho_epsilon = 1e-07
coef_linear = 3.4445
coef_square = -4.775
coef_cubic = 2.0315


def split(value):
    high = value.astype(bf16)
    return high, (value - high.astype(f32)).astype(bf16)


def triple(left, right, contract):
    dims = (contract, ((), ()))
    (left_high, left_low), (right_high, right_low) = left, right

    def dot(a, b):
        return lax.dot_general(a, b, dims, preferred_element_type=f32)

    return dot(left_high, right_high) + (dot(left_high, right_low) + dot(left_low, right_high))


def sweep_block(current, high, low):
    columns = current.shape[1]
    chunk = 512
    total = jnp.zeros((current.shape[0], chunk), f32)
    for index in range(columns // chunk):
        values = current[:, index * chunk : (index + 1) * chunk]
        total = total + values * values
    inverse = 1.0 / (jnp.sqrt(jnp.sum(total)) + ortho_epsilon)
    values = current[...] * inverse
    current[...] = values
    high[...], low[...] = split(values)

    def sweep(index, carry):
        rows, plain = ((1,), (1,)), ((1,), (0,))
        cross = matmul(high[...], low[...], rows)
        gram = matmul(high[...], high[...], rows) + (cross + cross.T)
        halves = split(gram)
        factor = split(coef_square * gram + coef_cubic * triple(halves, halves, plain))
        values = coef_linear * current[...] + triple(factor, (high[...], low[...]), plain)
        current[...] = values
        high[...], low[...] = split(values)
        return carry

    lax.fori_loop(0, SWEEPS, sweep, 0)


muon_decay = 0.95
decay_factor = 0.01
rate_qkv = 1.0
rate_out = 4.0
rate_up = 0.8
rate_down = 0.4


def finish_tokens(tokens, cotangent, first_sum, second_sum, table, layer_out, input_grad, sums):
    step_rows = 16
    sums[...] = jnp.zeros_like(sums)
    gain = table[0:1, :]
    bias = table[5:6, :] + table[6:7, :]

    def fold(values):
        return values[0:8] + values[8:16]

    def body(step, carry):
        at = pl.ds(pl.multiple_of(step * step_rows, step_rows), step_rows)
        residual = tokens[at, :].astype(f32)
        center = residual - jnp.mean(residual, -1, keepdims=True)
        variance = jnp.mean(center * center, -1, keepdims=True)
        scale_inv = lax.rsqrt(variance + norm_epsilon)
        normed = center * scale_inv
        layer_out[at, :] = (residual + first_sum[at, :] + bias).astype(bf16)
        grad_hidden = second_sum[at, :]
        cot = cotangent[at, :].astype(f32)
        grad_hat = grad_hidden * gain
        input_grad[at, :] = cot + scale_inv * (
            grad_hat
            - jnp.mean(grad_hat, -1, keepdims=True)
            - normed * jnp.mean(grad_hat * normed, -1, keepdims=True)
        )
        sums[0:8, :] += fold(grad_hidden * normed)
        sums[8:16, :] += fold(grad_hidden)
        sums[16:24, :] += fold(cot)
        return carry

    lax.fori_loop(0, tokens.shape[0] // step_rows, body, 0)


def finish_kernel(
    in_save, out_save, first_save, second_save,
    qkv_moment, out_moment, up_moment, down_moment, qkv_cross, out_cross, up_cross, down_cross,
    tokens, cotangent, bias_sum, table,
    in_sum, out_sum, update, layer_out, input_grad, vector_sum,
    in_result, out_result, first_sum, second_sum, nesterov, land, back, whole, current, high, low, sums, vector,
    plane_slots, mine, column_slots,
    out_send, out_recv, back_send, back_recv, plane_send, plane_recv, column_send, column_recv,
    cross_send, cross_recv, load_sem,
):
    loads = [
        pltpu.make_async_copy(source, target, load_sem.at[number])
        for number, (source, target) in enumerate(
            (
                (in_save, in_result),
                (out_save, out_result),
                (first_save, first_sum),
                (second_save, second_sum),
            )
        )
    ]
    for copy in loads:
        copy.start()
    core = lax.axis_index("core")
    z = lax.axis_index("tensor")
    chip = lax.axis_index("x") * RING + lax.axis_index("y")
    column = core * RING + z
    chips = RING * RING
    owners = nesterov.shape[1] // BR
    rows = nesterov.shape[0]
    half = rows // 2
    wide_in = in_result.shape[2]
    sibling = {"core": 1 - core}
    greet(plane_peers() + column_peers())

    def cross(number, source, target):
        remote = pltpu.make_async_remote_copy(
            src_ref=source,
            dst_ref=target,
            send_sem=cross_send.at[number],
            recv_sem=cross_recv.at[number],
            device_id=sibling,
            device_id_type=MESH,
        )
        remote.start()
        return remote

    def lanes(owner):
        return pl.ds(pl.multiple_of(owner * BR, BR), BR)

    def other(step):
        index = turn(chip, step, chips)
        return index, {"x": index // RING, "y": lax.rem(index, RING)}

    def outward(step):
        index, device = other(step)
        owner = jnp.minimum(index, owners - 1)
        return index, pltpu.make_async_remote_copy(
            src_ref=nesterov.at[:, lanes(owner)],
            dst_ref=land.at[chip],
            send_sem=out_send.at[step],
            recv_sem=out_recv.at[step],
            device_id=device,
            device_id_type=MESH,
        )

    def homeward(step):
        index, device = other(step)
        owner = jnp.minimum(chip, owners - 1)
        return index, pltpu.make_async_remote_copy(
            src_ref=back.at[index],
            dst_ref=whole.at[:, lanes(owner)],
            send_sem=back_send.at[step],
            recv_sem=back_recv.at[step],
            device_id=device,
            device_id_type=MESH,
        )

    def blend(at, moments):
        down = rows_at(at * half, half)
        column_at = 0
        for result, blocks in zip((in_result, out_result), moments):
            result_at = 0
            for own in blocks:
                width = own.shape[1]
                grad = result[at, :, result_at : result_at + width]
                values = grad + muon_decay * (muon_decay * own + grad)
                nesterov[down, column_at : column_at + width] = values.astype(bf16)
                column_at += width
                result_at += width

    loads[0].wait()
    loads[1].wait()
    blend(core, fold_rows(core, qkv_moment, out_moment, up_moment, down_moment))
    blend(
        1 - core,
        (
            [qkv_cross[0], qkv_cross[1], qkv_cross[2], up_cross[...]],
            [out_cross[...], down_cross[...]],
        ),
    )
    for step in range(1, chips):
        index, remote = outward(step)
        pl.when(index < owners)(remote.start)

    @pl.when(chip < owners)
    def own_piece():
        land[chip] = nesterov[:, lanes(chip)]

    crosses = [
        cross(0, out_result.at[1 - core], out_sum.at[core]),
        cross(1, in_result.at[1 - core], in_sum.at[core]),
    ]
    loads[2].wait()
    loads[3].wait()
    finish_tokens(
        tokens, cotangent, first_sum, second_sum, table, layer_out, input_grad, sums
    )
    vector[...] = jnp.zeros_like(vector)
    vector[0:1, :] = jnp.sum(sums[0:8, :], 0, keepdims=True)
    vector[1:2, :] = jnp.sum(sums[8:16, :], 0, keepdims=True)
    cot_sum = jnp.sum(sums[16:24, :], 0, keepdims=True)
    vector[5:6, :] = cot_sum
    vector[6:7, :] = cot_sum
    part = z * 2 + core
    for index in range(3):
        vector[2 + index : 3 + index, lanes(part)] = bias_sum[0:1, index * BR : (index + 1) * BR]
    hidden_units = wide_in - 3 * BR
    vector[pl.ds(7 + z, 1), pl.ds(pl.multiple_of(core * hidden_units, BR), hidden_units)] = (
        bias_sum[0:1, 3 * BR :]
    )
    width = mine.shape[1]

    def strip(place):
        return pl.ds(pl.multiple_of(place * width, width), width)

    plane_copies = []
    for step in range(1, chips):
        index, device = other(step)
        remote = pltpu.make_async_remote_copy(
            src_ref=vector.at[:, strip(index)],
            dst_ref=plane_slots.at[chip],
            send_sem=plane_send.at[step],
            recv_sem=plane_recv.at[step],
            device_id=device,
            device_id_type=MESH,
        )
        remote.start()
        plane_copies.append(remote)
    plane_slots[chip] = vector[:, strip(chip)]
    in_sum[core] = in_result[core]
    out_sum[core] = out_result[core]
    for remote in plane_copies:
        remote.wait_recv()
    mine[...] = jnp.sum(plane_slots[...], axis=0)
    column_slots[column] = mine[...]
    column_copies = []
    for step, peer in enumerate(column_peers()):
        remote = pltpu.make_async_remote_copy(
            src_ref=mine,
            dst_ref=column_slots.at[column],
            send_sem=column_send.at[step],
            recv_sem=column_recv.at[step],
            device_id=peer,
            device_id_type=MESH,
        )
        remote.start()
        column_copies.append(remote)

    @pl.when(chip < owners)
    def own_block():
        for step in range(1, chips):
            outward(step)[1].wait_recv()
        for place in range(chips):
            current[:, place * rows : (place + 1) * rows] = land[place].astype(f32).T
        sweep_block(current, high, low)
        for place in range(chips):
            back[place] = current[:, place * rows : (place + 1) * rows].T.astype(bf16)
        for step in range(1, chips):
            homeward(step)[1].start()
        whole[:, lanes(chip)] = back[chip]

    for remote in column_copies:
        remote.wait_recv()
    vector_sum[...] = jnp.sum(column_slots[...], axis=0)
    for step in range(1, chips):
        index, remote = homeward(step)
        sender = turn(chip, -step, chips)
        pl.when(sender < owners)(remote.wait_recv)
    crosses.append(cross(2, whole.at[rows_at((1 - core) * half, half)], update.at[core]))
    update[core] = whole[rows_at(core * half, half), :]
    for step in range(1, chips):
        index, remote = outward(step)
        pl.when(index < owners)(remote.wait_send)

    @pl.when(chip < owners)
    def sent_back():
        for step in range(1, chips):
            homeward(step)[1].wait_send()

    for remote in plane_copies + column_copies:
        remote.wait_send()
    for remote in crosses:
        remote.wait()


def finish_all(results, moments, crosses, tokens, cotangent, bias_sum, table):
    half = results[0].shape[1]
    columns = results[0].shape[2] + results[1].shape[2]
    rows = 2 * half
    token_rows, feature = tokens.shape
    chips = RING * RING
    small = (table.shape[0], feature // chips)
    vmem = pl.BlockSpec(memory_space=pltpu.VMEM)
    any_spec = pl.BlockSpec(memory_space=pl.ANY)
    return pl.pallas_call(
        finish_kernel,
        out_shape=(
            jax.ShapeDtypeStruct(results[0].shape, f32),
            jax.ShapeDtypeStruct(results[1].shape, f32),
            jax.ShapeDtypeStruct((2, half, columns), bf16),
            jax.ShapeDtypeStruct((token_rows, feature), bf16),
            jax.ShapeDtypeStruct((token_rows, feature), f32),
            jax.ShapeDtypeStruct(small, f32),
        ),
        in_specs=[any_spec] * 4 + [vmem] * 12,
        out_specs=(vmem,) * 6,
        scratch_shapes=[pltpu.VMEM(result.shape, f32) for result in results]
        + [
            pltpu.VMEM((rows, columns), bf16),
            pltpu.VMEM((chips, rows, BR), bf16),
            pltpu.VMEM((chips, rows, BR), bf16),
            pltpu.VMEM((rows, columns), bf16),
            pltpu.VMEM((BR, chips * rows), f32),
            pltpu.VMEM((BR, chips * rows), bf16),
            pltpu.VMEM((BR, chips * rows), bf16),
            pltpu.VMEM((24, feature), f32),
            pltpu.VMEM(table.shape, f32),
            pltpu.VMEM((chips,) + small, f32),
            pltpu.VMEM(small, f32),
            pltpu.VMEM((2 * RING,) + small, f32),
            *[pltpu.SemaphoreType.DMA((chips,)) for _ in range(6)],
            *[pltpu.SemaphoreType.DMA((2 * RING,)) for _ in range(2)],
            pltpu.SemaphoreType.DMA((3,)),
            pltpu.SemaphoreType.DMA((3,)),
            pltpu.SemaphoreType.DMA((4,)),
        ],
        compiler_params=pltpu.CompilerParams(
            collective_id=2, has_side_effects=True, vmem_limit_bytes=56 * 2**20
        ),
    )(*results, *moments, *crosses, tokens, cotangent, bias_sum, table)


def apply_kernel(
    in_save, out_save, update_save, layer_save, input_save,
    qkv_weight, out_weight, up_weight, down_weight,
    qkv_moment, out_moment, up_moment, down_moment,
    qkv_new, out_new, up_new, down_new,
    qkv_moment_new, out_moment_new, up_moment_new, down_moment_new, layer_out, input_grad,
    in_sum, out_sum, update, *rest,
):
    *held, load_sem = rest
    states = (
        qkv_weight, out_weight, up_weight, down_weight,
        qkv_moment, out_moment, up_moment, down_moment,
    )
    pairs = [(in_save, in_sum), (out_save, out_sum), (update_save, update)]
    pairs += [*zip(states, held), (layer_save, layer_out), (input_save, input_grad)]
    loads = [
        pltpu.make_async_copy(source, target, load_sem.at[number])
        for number, (source, target) in enumerate(pairs)
    ]
    for copy in loads:
        copy.start()
    for copy in loads:
        copy.wait()
    (
        qkv_weight, out_weight, up_weight, down_weight,
        qkv_moment, out_moment, up_moment, down_moment,
    ) = held
    heads, units = qkv_weight.shape[2] // 2, up_weight.shape[1] // 2
    outs, downs = out_weight.shape[1] // 2, down_weight.shape[1] // 2
    wide_in = in_sum.shape[2]

    def step(at, weight, moment, new, moment_new, grad, orthogonal, rate):
        moment_new[at] = muon_decay * moment[at] + grad
        new[at] = weight[at] * (1.0 - decay_factor * rate) - rate * orthogonal.astype(f32)

    for half in range(2):

        def lanes(size):
            return (slice(None), slice(half * size, (half + 1) * size))

        for index in range(3):
            from_at = slice(index * heads, (index + 1) * heads)
            step(
                (index,) + lanes(heads), qkv_weight, qkv_moment, qkv_new, qkv_moment_new,
                in_sum[half, :, from_at], update[half, :, from_at], rate_qkv,
            )
        step(
            lanes(units), up_weight, up_moment, up_new, up_moment_new,
            in_sum[half, :, 3 * heads :], update[half, :, 3 * heads : wide_in], rate_up,
        )
        step(
            lanes(outs), out_weight, out_moment, out_new, out_moment_new,
            out_sum[half, :, :outs], update[half, :, wide_in : wide_in + outs], rate_out,
        )
        step(
            lanes(downs), down_weight, down_moment, down_new, down_moment_new,
            out_sum[half, :, outs:], update[half, :, wide_in + outs :], rate_down,
        )


def apply_all(in_sum, out_sum, update, layer_out, input_grad, weights, moments):
    vmem = pl.BlockSpec(memory_space=pltpu.VMEM)
    hbm = pl.BlockSpec(memory_space=pltpu.HBM)
    return pl.pallas_call(
        apply_kernel,
        out_shape=tuple(
            jax.ShapeDtypeStruct(w.shape, w.dtype)
            for w in (*weights, *moments, layer_out, input_grad)
        ),
        in_specs=[hbm] * 13,
        out_specs=(vmem,) * 10,
        scratch_shapes=[
            pltpu.VMEM(in_sum.shape, f32),
            pltpu.VMEM(out_sum.shape, f32),
            pltpu.VMEM(update.shape, bf16),
            *[pltpu.VMEM(state.shape, f32) for state in (*weights, *moments)],
            pltpu.SemaphoreType.DMA((13,)),
        ],
        compiler_params=pltpu.CompilerParams(vmem_limit_bytes=62 * 2**20),
    )(in_sum, out_sum, update, layer_out, input_grad, *weights, *moments)


def turn_tables(positions):
    half = ROT // 2
    count = positions.shape[0]
    lane = jnp.arange(LANES)[None, None, :]
    kind = jnp.arange(3)[:, None, None]
    place = positions.astype(f32)[None, :, None]
    within = lane % HEAD
    angle = place * rotary_base ** (-2.0 * (lane % half).astype(f32) / ROT)
    sign = jnp.where(within < half, -1.0, 1.0)
    turns = within < ROT
    start = jnp.arange(count).astype(f32)[None, :, None] - place
    cosine = jnp.where(turns, jnp.cos(angle), 1.0)
    sine = jnp.where(turns, jnp.sin(angle) * sign, 0.0)
    return jnp.where(kind == 0, cosine, jnp.where(kind == 1, sine, start))


def local(
    inputs,
    cotangent,
    positions,
    qkv_weight,
    out_weight,
    up_weight,
    down_weight,
    qkv_moment,
    out_moment,
    up_moment,
    down_moment,
    vectors,
    vector_first,
    vector_second,
):
    vector_rows, vector_width = vectors.shape
    column = lax.axis_index("core") * RING + lax.axis_index("tensor")
    spread = jnp.tile(jnp.pad(vectors, ((0, 16 - vector_rows), (0, 0))), (1, 2 * RING))
    mine = jnp.arange(spread.shape[1])[None, :] // vector_width == column
    vector_mine = jnp.where(mine, spread, 0.0)
    rows = qkv_weight.shape[0]

    def turned_over(qkv, out, up, down):
        return (qkv.transpose(1, 0, 2), out.T, up, down.T)

    weights = turned_over(qkv_weight, out_weight, up_weight, down_weight)
    moments = turned_over(qkv_moment, out_moment, up_moment, down_moment)
    kept = forward_all(weights, inputs, cotangent, turn_tables(positions), vector_mine, moments)
    saved, crosses, table = kept[:10], kept[10:14], kept[14]
    *results, bias_sum = backward_all(saved, rows)
    in_sum, out_sum, update, layer_out, input_grad, vector_sum = finish_all(
        results, moments, crosses, inputs, cotangent, bias_sum, table
    )
    vector_grad = lax.dynamic_slice(
        vector_sum, (0, column * vector_width), (vector_rows, vector_width)
    )
    first_new = first_decay * vector_first + (1.0 - first_decay) * vector_grad
    second_new = second_decay * vector_second + (1.0 - second_decay) * vector_grad * vector_grad
    first_hat = first_new / (1.0 - first_decay**STEP)
    second_hat = second_new / (1.0 - second_decay**STEP)
    vectors_new = vectors - adam_rate * first_hat / (jnp.sqrt(second_hat) + adam_epsilon)

    applied = apply_all(in_sum, out_sum, update, layer_out, input_grad, weights, moments)
    qkv_new, out_new, up_new, down_new = turned_over(*applied[:4])
    qkv_moment_new, out_moment_new, up_moment_new, down_moment_new = turned_over(*applied[4:8])
    layer_out, input_grad = applied[8:]
    return (
        layer_out,
        input_grad,
        qkv_new,
        out_new,
        up_new,
        down_new,
        qkv_moment_new,
        out_moment_new,
        up_moment_new,
        down_moment_new,
        first_new,
        second_new,
        vectors_new,
    )


def solution(mesh):
    wide = Mesh(mesh.devices.reshape(4, 4, 2, 4), ALL)
    in_specs = (
        P(ALL, None),
        P(ALL, None),
        P(DP),
        P(DP, None, "tensor"),
        P("tensor", DP),
        P(DP, "tensor"),
        P("tensor", DP),
        P(DP, None, "tensor"),
        P("tensor", DP),
        P(DP, "tensor"),
        P("tensor", DP),
        P(None, ALL),
        P(None, ALL),
        P(None, ALL),
    )
    out_specs = (
        P(ALL, None),
        P(ALL, None),
        P(DP, None, "tensor"),
        P("tensor", DP),
        P(DP, "tensor"),
        P("tensor", DP),
        P(DP, None, "tensor"),
        P("tensor", DP),
        P(DP, "tensor"),
        P("tensor", DP),
        P(None, ALL),
        P(None, ALL),
        P(None, ALL),
    )
    return jax.shard_map(local, mesh=wide, in_specs=in_specs, out_specs=out_specs, check_vma=False)
```
